32 devices in a mesh: dom: 8 (over y, x, core), head: 4 (over z).
Axes of the slice: x: 2, y: 2, z: 4, core: 2. Of those that a mesh axis runs over, the one named last changes fastest.
Arguments:
- queries: bfloat16 [4608, 2048], P(('dom', 'head')), may hold values from -8 to 8
- keys_in: bfloat16 [4608, 2048], P(('dom', 'head')), may hold values from -8 to 8
- values_in: bfloat16 [4608, 2048], P(('dom', 'head')), may hold values from -6 to 6
- grad_out: bfloat16 [4608, 2048], P(('dom', 'head')), may hold values from -6 to 6
- pos_bias: float32 [32, 64, 576], P('head'), may hold values from -4 to 4
- neighbours: int32 [72, 9], P('dom'), may hold values from 0 to 32, as said below
- send_block: int32 [8, 8, 3], P('dom'), may hold values from 0 to 8, as said below
- orient: int32 [8, 8], P('dom'), may hold values from 0 to 7
Outputs:
- grad_q: bfloat16 [4608, 2048], P(('dom', 'head'))
- grad_k: bfloat16 [4608, 2048], P(('dom', 'head'))
- grad_v: bfloat16 [4608, 2048], P(('dom', 'head'))
The draws below stay inside these ranges and needn't reach their ends.
Inputs may be any that keep to these rules, and one draw needn't show every extreme that they name: `neighbours`: entry [d * 9 + b, j] names the j-th key block of query block b of domain d: e below 9 is the domain's own block e, and 9 + k * 3 + c is slot c of what domain d borrows from direction k. The 9 entries of a query block are distinct and name only live slots of send_block. `send_block`: entry [p, k, c] is the block that domain p lends in slot c to the domain d with nb(d, k) = p. The live slots of one entry [p, k] name distinct blocks; there are 3 of them for the four edge directions and one for the four corner directions, none where no such d exists; slots that are not live hold 0 and no neighbours entry names them.
All inputs are finite; a program needn't handle non-finite values.
Results may differ from the reference program's by a relative error of at most 0.025.
Values may be sent and summed in bfloat16 or wider, within the bound.
No kernel may reach another device: no remote copies, remote signals or barrier semaphores. Data moves between devices by JAX's collectives and lax.ppermute only.
A program may use at most 128 MiB of HBM per device.

```python
import jax
import jax.numpy as jnp
import numpy as np
from jax import lax

HEADS = 32
HD = 64
D = 2048
PATCH = 8
BT = 64
TILE = 3
GRID_ROWS = 4
DIRS = 8
WIN = 9
WINK = 576
QB_DOM = 9
DOMAINS = 8
TOKENS = 4608
CAP = 3


def grid_layout(key):
    grid_cols = DOMAINS // GRID_ROWS
    domain_ids = jnp.arange(DOMAINS, dtype=jnp.int32)
    cell_row = domain_ids // grid_cols
    cell_col = domain_ids % grid_cols
    block_ids = jnp.arange(QB_DOM, dtype=jnp.int32)
    glob_row = cell_row[:, None] * TILE + block_ids[None, :] // TILE
    glob_col = cell_col[:, None] * TILE + block_ids[None, :] % TILE
    centre_row = jnp.clip(glob_row, 1, GRID_ROWS * TILE - 2)
    centre_col = jnp.clip(glob_col, 1, grid_cols * TILE - 2)
    step_row = jnp.array([-1, -1, -1, 0, 0, 0, 1, 1, 1], jnp.int32)
    step_col = jnp.array([-1, 0, 1, -1, 0, 1, -1, 0, 1], jnp.int32)
    key_row = centre_row[:, :, None] + step_row
    key_col = centre_col[:, :, None] + step_col
    tile_row = key_row // TILE
    tile_col = key_col // TILE
    owner_dom = tile_row * grid_cols + tile_col
    local_row = key_row % TILE
    local_col = key_col % TILE
    shift_row = tile_row - cell_row[:, None, None]
    shift_col = tile_col - cell_col[:, None, None]
    slot_pos = jnp.where(shift_row == 0, local_row, jnp.where(shift_col == 0, local_col, 0))
    flat_dir = (shift_row + 1) * 3 + (shift_col + 1)
    direction = jnp.clip(jnp.where(flat_dir > 4, flat_dir - 1, flat_dir), 0, DIRS - 1)
    slot_keys = jax.random.split(jax.random.fold_in(key, 101), DOMAINS * DIRS)
    slot_perm = jax.vmap(lambda one_key: jax.random.permutation(one_key, CAP))(slot_keys)
    slot_perm = slot_perm.reshape(DOMAINS, DIRS, CAP).astype(jnp.int32)
    dom_index = jnp.broadcast_to(domain_ids[:, None, None], direction.shape)
    slot_num = slot_perm[dom_index, direction, slot_pos]
    is_mine = owner_dom == domain_ids[:, None, None]
    near = jnp.where(is_mine, local_row * TILE + local_col, QB_DOM + direction * CAP + slot_num)
    near = near.reshape(DOMAINS * QB_DOM, WIN).astype(jnp.int32)
    order_keys = jax.random.split(jax.random.fold_in(key, 102), DOMAINS * QB_DOM)
    orders = jax.vmap(lambda one_key: jax.random.permutation(one_key, WIN))(order_keys).astype(jnp.int32)
    near = jnp.take_along_axis(near, orders, axis=1).astype(jnp.int32)
    off_row = jnp.array([-1, -1, -1, 0, 0, 1, 1, 1], jnp.int32)
    off_col = jnp.array([-1, 0, 1, -1, 1, -1, 0, 1], jnp.int32)
    recv_row = cell_row[:, None] - off_row[None, :]
    recv_col = cell_col[:, None] - off_col[None, :]
    valid = (recv_row >= 0) & (recv_row < GRID_ROWS) & (recv_col >= 0) & (recv_col < grid_cols)
    recv_dom = jnp.clip(recv_row, 0, GRID_ROWS - 1) * grid_cols + jnp.clip(recv_col, 0, grid_cols - 1)
    corner = (off_row != 0) & (off_col != 0)
    send_count = jnp.where(valid, jnp.where(corner[None, :], 1, TILE), 0)
    position = jnp.arange(CAP, dtype=jnp.int32)[None, None, :]
    row_dir = off_row[None, :, None]
    col_dir = off_col[None, :, None]
    pick_row = jnp.where(row_dir == 1, 0, jnp.where(row_dir == -1, TILE - 1, position))
    pick_col = jnp.where(col_dir == 1, 0, jnp.where(col_dir == -1, TILE - 1, position))
    values = jnp.where(position < send_count[:, :, None], pick_row * TILE + pick_col, 0).astype(jnp.int32)
    shape3 = (DOMAINS, DIRS, CAP)
    dir_index = jnp.broadcast_to(jnp.arange(DIRS, dtype=jnp.int32)[None, :, None], shape3)
    pos_index = jnp.broadcast_to(position, shape3)
    recv_index = jnp.broadcast_to(recv_dom[:, :, None], shape3)
    target = slot_perm[recv_index, dir_index, pos_index]
    sender_index = jnp.broadcast_to(domain_ids[:, None, None], shape3)
    sends = jnp.zeros(shape3, jnp.int32).at[sender_index, dir_index, target].set(values)
    return (near, sends.astype(jnp.int32))


def draw_queries(key, part):
    return jnp.clip(jax.random.normal(jax.random.fold_in(key, 301), (TOKENS, D), jnp.float32), -6.0, 6.0).astype(jnp.bfloat16)


def draw_keys_in(key, part):
    return jnp.clip(jax.random.normal(jax.random.fold_in(key, 302), (TOKENS, D), jnp.float32), -6.0, 6.0).astype(jnp.bfloat16)


def draw_neighbours(key, part):
    return grid_layout(key)[0]


def draw_send_block(key, part):
    return grid_layout(key)[1]


def set_ends(entries, rng, smallest, high):
    extent = entries.shape
    spot = [jax.random.randint(jax.random.fold_in(rng, axis), (), 0, extent[axis]) for axis in range(len(extent))]
    entries = entries.at[tuple(spot)].set(smallest)
    longest = extent.index(max(extent))
    spot[longest] = (spot[longest] + 1) % extent[longest]
    return entries.at[tuple(spot)].set(high)


def block_scale(own_key, shape, cuts, smallest, top_value):
    loudness, own = 1.0, jax.random.fold_in(own_key, 6)
    for dim, blocks in cuts:
        heights = jnp.exp(jax.random.uniform(jax.random.fold_in(own, dim), (blocks,), jnp.float32, smallest / len(cuts), top_value / len(cuts)))
        loudness = loudness * jnp.repeat(heights, shape[dim] // blocks).reshape([-1 if axis == dim else 1 for axis in range(len(shape))])
    return loudness


def normal_values(own_key, shape, scale, bound, cuts=(), kind=jnp.bfloat16):
    loudness = block_scale(own_key, shape, cuts, -0.22, 0.18) if cuts else 1.0
    values = jax.random.normal(own_key, shape, jnp.float32) * scale * loudness
    return jnp.minimum(jnp.maximum(values, -bound), bound).astype(kind)


def setup_inputs(seed: int = 0) -> dict:
    streams_of = jax.random.split(jax.random.key(seed), 9)
    queries = draw_queries(jax.random.fold_in(streams_of[8], 71), 0)
    keys_in = draw_keys_in(jax.random.fold_in(streams_of[8], 71), 0)
    values_in = normal_values(streams_of[2], (TOKENS, D), 1.0, 6.0, ((0, 32),))
    grad_out = normal_values(streams_of[3], (TOKENS, D), 1.0, 6.0, ((0, 32),))
    pos_bias = normal_values(streams_of[4], (HEADS, BT, WINK), 0.8, 4.0, ((0, 4),), jnp.float32)
    neighbours = draw_neighbours(jax.random.fold_in(streams_of[8], 71), 0)
    send_block = draw_send_block(jax.random.fold_in(streams_of[8], 71), 0)
    orient = set_ends(jax.random.randint(streams_of[7], (DOMAINS, DIRS), 0, 8), jax.random.fold_in(streams_of[7], 1), 0, 7).astype(jnp.int32)
    return dict(queries=queries, keys_in=keys_in, values_in=values_in, grad_out=grad_out, pos_bias=pos_bias, neighbours=neighbours, send_block=send_block, orient=orient)


def patch_tables(patch_side):
    flat_index = np.arange(patch_side * patch_side)
    row_of = flat_index // patch_side
    col_of = flat_index % patch_side
    table_list = []
    for orient_id in range(8):
        row_new = patch_side - 1 - row_of if orient_id % 2 == 1 else row_of
        col_new = patch_side - 1 - col_of if (orient_id // 2) % 2 == 1 else col_of
        mapped = patch_side * col_new + row_new if orient_id >= 4 else patch_side * row_new + col_new
        table_list.append(mapped)
    forward = np.stack(table_list).astype(np.int32)
    inverse = np.argsort(forward, axis=1).astype(np.int32)
    return forward, inverse


def reference(queries, keys_in, values_in, grad_out, pos_bias, neighbours, send_block, orient):
    forward, inverse = patch_tables(PATCH)
    turn_table = jnp.asarray(forward)
    back_table = jnp.asarray(inverse)
    score_scale = HD ** -0.5
    grid_cols = DOMAINS // GRID_ROWS
    step_rows = jnp.array([-1, -1, -1, 0, 0, 1, 1, 1], jnp.int32)
    step_cols = jnp.array([-1, 0, 1, -1, 1, -1, 0, 1], jnp.int32)
    pairs_all = jnp.concatenate([keys_in.reshape(DOMAINS * QB_DOM, BT, HEADS, HD),
                                 values_in.reshape(DOMAINS * QB_DOM, BT, HEADS, HD)], axis=-1)
    query_all = queries.reshape(DOMAINS, QB_DOM, BT, HEADS, HD)
    grad_all = grad_out.reshape(DOMAINS, QB_DOM, BT, HEADS, HD)
    near_all = neighbours.reshape(DOMAINS, QB_DOM * WIN)
    dir_ids = jnp.arange(DIRS, dtype=jnp.int32)

    def one_domain(totals, domain):
        cell_row = domain // grid_cols
        cell_col = domain % grid_cols
        lender_row = jnp.clip(cell_row + step_rows, 0, GRID_ROWS - 1)
        lender_col = jnp.clip(cell_col + step_cols, 0, grid_cols - 1)
        lender = (lender_row * grid_cols + lender_col).astype(jnp.int32)
        lent = send_block[lender, dir_ids]
        global_ids = (lender[:, None] * QB_DOM + lent).reshape(-1).astype(jnp.int32)
        arrived = pairs_all[global_ids]
        turn_index = jnp.repeat(turn_table[orient[domain]], CAP, axis=0)
        oriented = jnp.take_along_axis(arrived, turn_index[:, :, None, None], axis=1)
        own_ids = (domain * QB_DOM + jnp.arange(QB_DOM, dtype=jnp.int32)).astype(jnp.int32)
        extended = jnp.concatenate([pairs_all[own_ids], oriented], axis=0)
        near_ids = near_all[domain]
        window = extended[near_ids].reshape(QB_DOM, WINK, HEADS, 2 * HD).astype(jnp.float32)
        win_k = window[..., :HD]
        win_v = window[..., HD:]
        query_blk = query_all[domain].astype(jnp.float32)
        grad_blk = grad_all[domain].astype(jnp.float32)
        scores = jnp.einsum('bthd,bkhd->bhtk', query_blk, win_k) * score_scale + pos_bias[None]
        row_top = jnp.max(scores, axis=-1, keepdims=True)
        exp_scores = jnp.exp(scores - row_top)
        probs = exp_scores / jnp.sum(exp_scores, axis=-1, keepdims=True)
        probs_half = probs.astype(jnp.bfloat16)
        probs_wide = lax.optimization_barrier(probs_half).astype(jnp.float32)
        attended = jnp.einsum('bhtk,bkhd->bthd', probs_wide, win_v)
        row_delta = jnp.sum(grad_blk * attended, axis=-1)
        dprobs = jnp.einsum('bthd,bkhd->bhtk', grad_blk, win_v)
        dscores = (probs * (dprobs - jnp.transpose(row_delta, (0, 2, 1))[..., None])).astype(jnp.bfloat16)
        dscores_wide = lax.optimization_barrier(dscores).astype(jnp.float32)
        grad_q_blk = (jnp.einsum('bhtk,bkhd->bthd', dscores_wide, win_k) * score_scale).astype(jnp.bfloat16)
        grad_kw = jnp.einsum('bhtk,bthd->bkhd', dscores_wide, query_blk) * score_scale
        grad_vw = jnp.einsum('bhtk,bthd->bkhd', probs_wide, grad_blk)
        window_grad = jnp.concatenate([grad_kw, grad_vw], axis=-1).reshape(QB_DOM * WIN, BT, HEADS, 2 * HD)
        slot_grad = jax.ops.segment_sum(window_grad, near_ids, num_segments=QB_DOM + DIRS * CAP)
        back_order = jnp.repeat(back_table[orient[domain]], CAP, axis=0)
        returned = jnp.take_along_axis(slot_grad[QB_DOM:], back_order[:, :, None, None], axis=1).astype(jnp.bfloat16)
        returned_wide = lax.optimization_barrier(returned).astype(jnp.float32)
        totals = totals.at[own_ids].add(slot_grad[:QB_DOM])
        totals = totals.at[global_ids].add(returned_wide)
        return totals, grad_q_blk

    start = jnp.zeros((DOMAINS * QB_DOM, BT, HEADS, 2 * HD), jnp.float32)
    totals, grad_q = lax.scan(one_domain, start, jnp.arange(DOMAINS, dtype=jnp.int32))
    grad_q = grad_q.reshape(TOKENS, D)
    grad_k = totals[..., :HD].astype(jnp.bfloat16).reshape(TOKENS, D)
    grad_v = totals[..., HD:].astype(jnp.bfloat16).reshape(TOKENS, D)
    return (grad_q, grad_k, grad_v)
```

```python
import functools

import jax
import jax.numpy as jnp
import numpy as np
from jax import lax
from jax.experimental import pallas as pl
from jax.experimental.pallas import tpu as pltpu
from jax.sharding import PartitionSpec as P

HD = 64
PATCH = 8
BT = 64
GRID_ROWS = 4
DIRS = 8
WIN = 9
WINK = 576
QB_DOM = 9
CAP = 3
GROUP_HEADS = 4
VMEM_LIMIT = 48 * 1024 * 1024

OFFSET_LIST = [(-1, -1), (-1, 0), (-1, 1), (0, -1), (0, 1), (1, -1), (1, 0), (1, 1)]


class Plan:
    def __init__(self, domains):
        grid_cols = domains // GRID_ROWS
        groups = []
        for k, (row_step, col_step) in enumerate(OFFSET_LIST):
            pairs = []
            for d in range(domains):
                row, col = d // grid_cols + row_step, d % grid_cols + col_step
                if 0 <= row < GRID_ROWS and 0 <= col < grid_cols:
                    pairs.append((row * grid_cols + col, d))
            count = 1 if row_step and col_step else CAP
            if not pairs:
                continue
            lenders, borrowers = {p for p, _ in pairs}, {d for _, d in pairs}
            for group in groups:
                taken_l = {p for p, _ in group["pairs"]}
                taken_b = {d for _, d in group["pairs"]}
                if group["count"] == count and not (taken_l & lenders) and not (taken_b & borrowers):
                    break
            else:
                group = dict(count=count, pairs=[], send=[0] * domains, recv=[0] * domains)
                groups.append(group)
            group["pairs"] += pairs
            for p, d in pairs:
                group["send"][p] = k
                group["recv"][d] = k
        groups.sort(key=lambda group: -group["count"])
        self.groups = groups
        self.counts = [group["count"] for group in groups]
        self.offsets = [sum(self.counts[:i]) for i in range(len(groups))]
        self.borrowed = sum(self.counts)
        self.slots = QB_DOM + self.borrowed
        slot_total = QB_DOM + DIRS * CAP
        table = np.zeros((domains, slot_total + 2 * len(groups)), np.int32)
        for d in range(domains):
            table[d, :QB_DOM] = np.arange(QB_DOM)
            for i, group in enumerate(groups):
                k = group["recv"][d]
                for c in range(CAP if any(d == to for _, to in group["pairs"]) else 0):
                    place = QB_DOM + self.offsets[i] + (c if group["count"] > 1 else 0)
                    table[d, QB_DOM + k * CAP + c] = place
                table[d, slot_total + i] = group["send"][d]
                table[d, slot_total + len(groups) + i] = k
        self.table = table
        self.send_at = slot_total
        self.recv_at = slot_total + len(groups)

    def lent_block(self, i, c, table_ref, send_ref):
        k = table_ref[self.send_at + i]
        if self.counts[i] > 1:
            return send_ref[k * CAP + c]
        found = send_ref[k * CAP]
        for other in range(1, CAP):
            found = jnp.maximum(found, send_ref[k * CAP + other])
        return found


def block_rows(index):
    return pl.ds(pl.multiple_of(index * BT, BT), BT)


def turn_matrix(orient, back):
    token = lax.broadcasted_iota(jnp.int32, (BT, BT), 1 if back else 0)
    place = lax.broadcasted_iota(jnp.int32, (BT, BT), 0 if back else 1)
    row, col = token >> 3, token & (PATCH - 1)
    row = jnp.where((orient & 1) == 1, PATCH - 1 - row, row)
    col = jnp.where(((orient >> 1) & 1) == 1, PATCH - 1 - col, col)
    mapped = jnp.where(orient >= 4, PATCH * col + row, PATCH * row + col)
    return (mapped == place).astype(jnp.float32).astype(jnp.bfloat16)


def lend_kernel(plan, table_ref, send_ref, kv_ref, *out_refs):
    for i, count in enumerate(plan.counts):
        for c in range(count):
            block = plan.lent_block(i, c, table_ref, send_ref)
            out_refs[i][c * BT:(c + 1) * BT, :] = kv_ref[block_rows(block), :]


def settle_kernel(plan, table_ref, send_ref, own_ref, *refs):
    out_ref, total = refs[-2:]
    total[...] = own_ref[...]
    for i, count in enumerate(plan.counts):
        for c in range(count):
            block = plan.lent_block(i, c, table_ref, send_ref)
            total[block_rows(block), :] += refs[i][c * BT:(c + 1) * BT, :].astype(jnp.float32)
    out_ref[...] = total[...].astype(jnp.bfloat16)


def dot(a, b, contract):
    return lax.dot_general(a, b, ((contract[:1], contract[1:]), ((), ())),
                           preferred_element_type=jnp.float32)


def attend_kernel(plan, heads, table_ref, near_ref, orient_ref, qg_ref, kv_ref, bias_ref, *refs):
    groups = len(plan.groups)
    arrived = refs[:groups]
    dq_ref, own_ref = refs[groups:groups + 2]
    leaving = refs[groups + 2:2 * groups + 2]
    ext, acc, win = refs[2 * groups + 2:]
    width = heads * HD
    some = min(heads, GROUP_HEADS)
    lanes = some * HD
    scale = HD ** -0.5

    ext[:QB_DOM * BT, :] = kv_ref[...]
    for i, count in enumerate(plan.counts):
        turn = turn_matrix(orient_ref[table_ref[plan.recv_at + i]], False)
        for c in range(count):
            at = (QB_DOM + plan.offsets[i] + c) * BT
            ext[at:at + BT, :] = dot(turn, arrived[i][c * BT:(c + 1) * BT, :], (1, 0)).astype(jnp.bfloat16)
    acc[...] = jnp.zeros_like(acc)

    same_head = (lax.broadcasted_iota(jnp.int32, (lanes, lanes), 0) // HD
                 == lax.broadcasted_iota(jnp.int32, (lanes, lanes), 1) // HD)

    def spread(block):
        wide = jnp.concatenate([block] * some, axis=0)
        return jnp.where(same_head, wide, jnp.zeros_like(wide))

    def one_block(b, carry):
        rows = block_rows(b)
        places = [table_ref[near_ref[b * WIN + j]] for j in range(WIN)]
        for j in range(WIN):
            win[j * BT:(j + 1) * BT, :] = ext[block_rows(places[j]), :]
        for part in range(heads // some):
            here = slice(part * lanes, (part + 1) * lanes)
            there = slice(width + part * lanes, width + (part + 1) * lanes)
            win_k, win_v = win[:, here], win[:, there]
            query = spread(qg_ref[rows, here] * jnp.bfloat16(scale))
            grad = spread(qg_ref[rows, there])
            scores = dot(win_k, query, (1, 1)) + bias_ref[:, here]
            weight = jnp.exp(scores - jnp.max(scores, axis=0, keepdims=True))
            probs = weight * (1.0 / jnp.sum(weight, axis=0, keepdims=True))
            probs_half = probs.astype(jnp.bfloat16)
            dprobs = dot(win_v, grad, (1, 1))
            delta = jnp.sum(probs_half.astype(jnp.float32) * dprobs, axis=0, keepdims=True)
            dscores = (probs * (dprobs - delta)).astype(jnp.bfloat16)
            grad_q = dot(dscores, win_k, (0, 0))
            grad_q = jnp.where(same_head, grad_q, 0.0)
            total_q = grad_q[:BT]
            for h in range(1, some):
                total_q = total_q + grad_q[h * BT:(h + 1) * BT]
            dq_ref[rows, here] = (total_q * scale).astype(jnp.bfloat16)
            grad_k = dot(dscores, query, (1, 0))
            grad_v = dot(probs_half, grad, (1, 0))
            for j in range(WIN):
                acc[block_rows(places[j]), here] += grad_k[j * BT:(j + 1) * BT]
                acc[block_rows(places[j]), there] += grad_v[j * BT:(j + 1) * BT]
        return carry

    lax.fori_loop(0, QB_DOM, one_block, 0)
    own_ref[...] = acc[:QB_DOM * BT, :]
    for i, count in enumerate(plan.counts):
        turn = turn_matrix(orient_ref[table_ref[plan.recv_at + i]], True)
        for c in range(count):
            at = (QB_DOM + plan.offsets[i] + c) * BT
            slot = acc[at:at + BT, :].astype(jnp.bfloat16)
            leaving[i][c * BT:(c + 1) * BT, :] = dot(turn, slot, (1, 0)).astype(jnp.bfloat16)


def smem_specs(count):
    return [pl.BlockSpec(memory_space=pltpu.SMEM)] * count


def vmem_specs(count):
    return [pl.BlockSpec(memory_space=pltpu.VMEM)] * count


def params():
    return pltpu.CompilerParams(vmem_limit_bytes=VMEM_LIMIT)


def bf16(*shape):
    return jax.ShapeDtypeStruct(shape, jnp.bfloat16)


def per_device(plan, queries, keys_in, values_in, grad_out, pos_bias, neighbours, send_block, orient):
    heads = pos_bias.shape[0]
    width = heads * HD
    tokens = queries.shape[0]
    holders = lax.axis_size("head")
    tokens_dom = tokens * holders
    groups = len(plan.groups)
    table = lax.dynamic_index_in_dim(jnp.asarray(plan.table), lax.axis_index("dom"), 0, False)
    near, sends, turns = neighbours.reshape(-1), send_block.reshape(-1), orient.reshape(-1)

    def gather_heads(left, right):
        pair = jnp.concatenate([left.reshape(tokens, holders, width), right.reshape(tokens, holders, width)], axis=-1)
        pair = jnp.transpose(pair, (1, 0, 2))
        pair = lax.all_to_all(pair, "head", split_axis=0, concat_axis=0, tiled=True)
        return pair.reshape(tokens_dom, 2 * width)

    def scatter_heads(matrix):
        matrix = matrix.reshape(holders, tokens, matrix.shape[1])
        return lax.all_to_all(matrix, "head", split_axis=0, concat_axis=0, tiled=True)

    def by_token(matrix):
        return jnp.transpose(matrix, (1, 0, 2)).reshape(tokens, holders * width)

    kv = gather_heads(keys_in, values_in)
    qg = gather_heads(queries, grad_out)
    bias = jnp.transpose(pos_bias, (2, 0, 1)).reshape(WINK, heads * BT)

    block_shapes = [bf16(count * BT, 2 * width) for count in plan.counts]
    lent = pl.pallas_call(
        functools.partial(lend_kernel, plan),
        out_shape=block_shapes,
        in_specs=smem_specs(2) + vmem_specs(1),
        out_specs=vmem_specs(groups),
        compiler_params=params(),
        name="lend",
    )(table, sends, kv)
    arrived = [lax.ppermute(lent[i], "dom", group["pairs"]) for i, group in enumerate(plan.groups)]

    outs = pl.pallas_call(
        functools.partial(attend_kernel, plan, heads),
        out_shape=[bf16(tokens_dom, width), jax.ShapeDtypeStruct((tokens_dom, 2 * width), jnp.float32)] + block_shapes,
        in_specs=smem_specs(3) + vmem_specs(3 + groups),
        out_specs=vmem_specs(2 + groups),
        scratch_shapes=[
            pltpu.VMEM((plan.slots * BT, 2 * width), jnp.bfloat16),
            pltpu.VMEM((plan.slots * BT, 2 * width), jnp.float32),
            pltpu.VMEM((WINK, 2 * width), jnp.bfloat16),
        ],
        compiler_params=params(),
        cost_estimate=pl.CostEstimate(flops=5 * 2 * tokens_dom * WINK * width, bytes_accessed=8 * tokens_dom * width,
                                      transcendentals=tokens_dom * WINK * heads),
        name="attend",
    )(table, near, turns, qg, kv, bias, *arrived)
    grad_q, own, leaving = outs[0], outs[1], outs[2:]

    returned = [lax.ppermute(leaving[i], "dom", [(d, p) for p, d in group["pairs"]])
                for i, group in enumerate(plan.groups)]
    grad_q = scatter_heads(grad_q)
    grad_kv = pl.pallas_call(
        functools.partial(settle_kernel, plan),
        out_shape=bf16(tokens_dom, 2 * width),
        in_specs=smem_specs(2) + vmem_specs(1 + groups),
        out_specs=vmem_specs(1)[0],
        scratch_shapes=[pltpu.VMEM((tokens_dom, 2 * width), jnp.float32)],
        compiler_params=params(),
        name="settle",
    )(table, sends, own, *returned)
    grad_kv = scatter_heads(grad_kv)
    return by_token(grad_q), by_token(grad_kv[..., :width]), by_token(grad_kv[..., width:])


def solution(mesh):
    plan = Plan(mesh.shape["dom"])
    tokens = P(("dom", "head"), None)
    return jax.shard_map(
        functools.partial(per_device, plan),
        mesh=mesh,
        in_specs=(
            tokens,
            tokens,
            tokens,
            tokens,
            P("head", None, None),
            P("dom", None),
            P("dom", None, None),
            P("dom", None),
        ),
        out_specs=(tokens, tokens, tokens),
        check_vma=False,
    )
```

```python
import functools

import jax
import jax.numpy as jnp
import numpy as np
from jax import lax
from jax.experimental import pallas as pl
from jax.experimental.pallas import tpu as pltpu
from jax.sharding import PartitionSpec as P

HD = 64
PATCH = 8
BT = 64
GRID_ROWS = 4
DIRS = 8
WIN = 9
WINK = 576
QB_DOM = 9
CAP = 3
GROUP_HEADS = 4
VMEM_LIMIT = 48 * 1024 * 1024

OFFSET_LIST = [(-1, -1), (-1, 0), (-1, 1), (0, -1), (0, 1), (1, -1), (1, 0), (1, 1)]


class Plan:
    def __init__(self, domains):
        grid_cols = domains // GRID_ROWS
        groups = []
        for k, (row_step, col_step) in enumerate(OFFSET_LIST):
            pairs = []
            for d in range(domains):
                row, col = d // grid_cols + row_step, d % grid_cols + col_step
                if 0 <= row < GRID_ROWS and 0 <= col < grid_cols:
                    pairs.append((row * grid_cols + col, d))
            count = 1 if row_step and col_step else CAP
            if not pairs:
                continue
            lenders, borrowers = {p for p, _ in pairs}, {d for _, d in pairs}
            for group in groups:
                taken_l = {p for p, _ in group["pairs"]}
                taken_b = {d for _, d in group["pairs"]}
                if group["count"] == count and not (taken_l & lenders) and not (taken_b & borrowers):
                    break
            else:
                group = dict(count=count, pairs=[], send=[0] * domains, recv=[0] * domains)
                groups.append(group)
            group["pairs"] += pairs
            for p, d in pairs:
                group["send"][p] = k
                group["recv"][d] = k
        groups.sort(key=lambda group: -group["count"])
        self.groups = groups
        self.counts = [group["count"] for group in groups]
        self.offsets = [sum(self.counts[:i]) for i in range(len(groups))]
        self.borrowed = sum(self.counts)
        self.slots = QB_DOM + self.borrowed
        slot_total = QB_DOM + DIRS * CAP
        table = np.zeros((domains, slot_total + 2 * len(groups)), np.int32)
        for d in range(domains):
            table[d, :QB_DOM] = np.arange(QB_DOM)
            for i, group in enumerate(groups):
                k = group["recv"][d]
                for c in range(CAP if any(d == to for _, to in group["pairs"]) else 0):
                    place = QB_DOM + self.offsets[i] + (c if group["count"] > 1 else 0)
                    table[d, QB_DOM + k * CAP + c] = place
                table[d, slot_total + i] = group["send"][d]
                table[d, slot_total + len(groups) + i] = k
        self.table = table
        self.send_at = slot_total
        self.recv_at = slot_total + len(groups)

    def lent_block(self, i, c, table_ref, send_ref):
        k = table_ref[self.send_at + i]
        if self.counts[i] > 1:
            return send_ref[k * CAP + c]
        found = send_ref[k * CAP]
        for other in range(1, CAP):
            found = jnp.maximum(found, send_ref[k * CAP + other])
        return found


def block_rows(index):
    return pl.ds(pl.multiple_of(index * BT, BT), BT)


def turn_matrix(orient, back):
    token = lax.broadcasted_iota(jnp.int32, (BT, BT), 1 if back else 0)
    place = lax.broadcasted_iota(jnp.int32, (BT, BT), 0 if back else 1)
    row, col = token >> 3, token & (PATCH - 1)
    row = jnp.where((orient & 1) == 1, PATCH - 1 - row, row)
    col = jnp.where(((orient >> 1) & 1) == 1, PATCH - 1 - col, col)
    mapped = jnp.where(orient >= 4, PATCH * col + row, PATCH * row + col)
    return (mapped == place).astype(jnp.float32).astype(jnp.bfloat16)


def pack_kernel(chunks, left_ref, right_ref, *out_refs):
    holders, _, pair_width = out_refs[0].shape
    width = pair_width // 2
    for chunk in range(chunks):
        for s in range(holders):
            at = (s * chunks + chunk) * width
            out_refs[chunk][s, :, :width] = left_ref[:, at:at + width]
            out_refs[chunk][s, :, width:] = right_ref[:, at:at + width]


def unpack_kernel(chunks, *refs):
    outs = refs[chunks:]
    holders, _, all_width = refs[0].shape
    width = all_width // len(outs)
    for chunk in range(chunks):
        for s in range(holders):
            at = (s * chunks + chunk) * width
            for which, out_ref in enumerate(outs):
                out_ref[:, at:at + width] = refs[chunk][s, :, which * width:(which + 1) * width]


def lend_kernel(plan, table_ref, send_ref, kv_ref, *out_refs):
    for i, count in enumerate(plan.counts):
        for c in range(count):
            block = plan.lent_block(i, c, table_ref, send_ref)
            out_refs[i][c * BT:(c + 1) * BT, :] = kv_ref[block_rows(block), :]


def settle_kernel(plan, table_ref, send_ref, grad_q_ref, own_ref, *refs):
    out_ref, total = refs[-2:]
    width = grad_q_ref.shape[1]
    out_ref[:, :width] = grad_q_ref[...]
    total[...] = own_ref[...]
    for i, count in enumerate(plan.counts):
        for c in range(count):
            block = plan.lent_block(i, c, table_ref, send_ref)
            total[block_rows(block), :] += refs[i][c * BT:(c + 1) * BT, :].astype(jnp.float32)
    out_ref[:, width:] = total[...].astype(jnp.bfloat16)


def dot(a, b, contract):
    return lax.dot_general(a, b, ((contract[:1], contract[1:]), ((), ())),
                           preferred_element_type=jnp.float32)


def attend_kernel(plan, heads, table_ref, near_ref, orient_ref, qg_ref, kv_ref, bias_ref, *refs):
    groups = len(plan.groups)
    arrived = refs[:groups]
    dq_ref, own_ref = refs[groups:groups + 2]
    leaving = refs[groups + 2:2 * groups + 2]
    ext, acc, win = refs[2 * groups + 2:]
    width = heads * HD
    some = min(heads, GROUP_HEADS)
    lanes = some * HD
    scale = HD ** -0.5

    ext[:QB_DOM * BT, :] = kv_ref[...]
    for i, count in enumerate(plan.counts):
        turn = turn_matrix(orient_ref[table_ref[plan.recv_at + i]], False)
        for c in range(count):
            at = (QB_DOM + plan.offsets[i] + c) * BT
            ext[at:at + BT, :] = dot(turn, arrived[i][c * BT:(c + 1) * BT, :], (1, 0)).astype(jnp.bfloat16)
    acc[...] = jnp.zeros_like(acc)

    same_head = (lax.broadcasted_iota(jnp.int32, (lanes, lanes), 0) // HD
                 == lax.broadcasted_iota(jnp.int32, (lanes, lanes), 1) // HD)

    def spread(block):
        wide = jnp.concatenate([block] * some, axis=0)
        return jnp.where(same_head, wide, jnp.zeros_like(wide))

    def one_block(b, carry):
        rows = block_rows(b)
        places = [table_ref[near_ref[b * WIN + j]] for j in range(WIN)]
        for j in range(WIN):
            win[j * BT:(j + 1) * BT, :] = ext[block_rows(places[j]), :]
        for part in range(heads // some):
            here = slice(part * lanes, (part + 1) * lanes)
            there = slice(width + part * lanes, width + (part + 1) * lanes)
            win_k, win_v = win[:, here], win[:, there]
            query = spread(qg_ref[rows, here] * jnp.bfloat16(scale))
            grad = spread(qg_ref[rows, there])
            scores = dot(win_k, query, (1, 1)) + bias_ref[:, here]
            weight = jnp.exp(scores - jnp.max(scores, axis=0, keepdims=True))
            probs = weight * (1.0 / jnp.sum(weight, axis=0, keepdims=True))
            probs_half = probs.astype(jnp.bfloat16)
            dprobs = dot(win_v, grad, (1, 1))
            delta = jnp.sum(probs_half.astype(jnp.float32) * dprobs, axis=0, keepdims=True)
            dscores = (probs * (dprobs - delta)).astype(jnp.bfloat16)
            grad_q = dot(dscores, win_k, (0, 0))
            grad_q = jnp.where(same_head, grad_q, 0.0)
            total_q = grad_q[:BT]
            for h in range(1, some):
                total_q = total_q + grad_q[h * BT:(h + 1) * BT]
            dq_ref[rows, here] = (total_q * scale).astype(jnp.bfloat16)
            grad_k = dot(dscores, query, (1, 0))
            grad_v = dot(probs_half, grad, (1, 0))
            for j in range(WIN):
                acc[block_rows(places[j]), here] += grad_k[j * BT:(j + 1) * BT]
                acc[block_rows(places[j]), there] += grad_v[j * BT:(j + 1) * BT]
        return carry

    lax.fori_loop(0, QB_DOM, one_block, 0)
    own_ref[...] = acc[:QB_DOM * BT, :]
    for i, count in enumerate(plan.counts):
        turn = turn_matrix(orient_ref[table_ref[plan.recv_at + i]], True)
        for c in range(count):
            at = (QB_DOM + plan.offsets[i] + c) * BT
            slot = acc[at:at + BT, :].astype(jnp.bfloat16)
            leaving[i][c * BT:(c + 1) * BT, :] = dot(turn, slot, (1, 0)).astype(jnp.bfloat16)


def smem_specs(count):
    return [pl.BlockSpec(memory_space=pltpu.SMEM)] * count


def vmem_specs(count):
    return [pl.BlockSpec(memory_space=pltpu.VMEM)] * count


def params():
    return pltpu.CompilerParams(vmem_limit_bytes=VMEM_LIMIT)


def bf16(*shape):
    return jax.ShapeDtypeStruct(shape, jnp.bfloat16)


def per_device(plan, queries, keys_in, values_in, grad_out, pos_bias, neighbours, send_block, orient):
    chunks = 2 if pos_bias.shape[0] % 2 == 0 else 1
    heads = pos_bias.shape[0] // chunks
    width = heads * HD
    tokens = queries.shape[0]
    holders = lax.axis_size("head")
    tokens_dom = tokens * holders
    groups = len(plan.groups)
    table = lax.dynamic_index_in_dim(jnp.asarray(plan.table), lax.axis_index("dom"), 0, False)
    near, sends, turns = neighbours.reshape(-1), send_block.reshape(-1), orient.reshape(-1)
    block_shapes = [bf16(count * BT, 2 * width) for count in plan.counts]

    def gather_heads(left, right):
        pairs = pl.pallas_call(
            functools.partial(pack_kernel, chunks),
            out_shape=[bf16(holders, tokens, 2 * width)] * chunks,
            in_specs=vmem_specs(2),
            out_specs=vmem_specs(chunks),
            compiler_params=params(),
            name="pack",
        )(left, right)
        return [lax.all_to_all(pair, "head", split_axis=0, concat_axis=0, tiled=True)
                .reshape(tokens_dom, 2 * width) for pair in pairs]

    def lend(kv):
        lent = pl.pallas_call(
            functools.partial(lend_kernel, plan),
            out_shape=block_shapes,
            in_specs=smem_specs(2) + vmem_specs(1),
            out_specs=vmem_specs(groups),
            compiler_params=params(),
            name="lend",
        )(table, sends, kv)
        return [lax.ppermute(lent[i], "dom", group["pairs"]) for i, group in enumerate(plan.groups)]

    def attend(kv, qg, arrived, chunk):
        bias = jnp.transpose(pos_bias[chunk * heads:(chunk + 1) * heads], (2, 0, 1)).reshape(WINK, heads * BT)
        outs = pl.pallas_call(
            functools.partial(attend_kernel, plan, heads),
            out_shape=[bf16(tokens_dom, width),
                       jax.ShapeDtypeStruct((tokens_dom, 2 * width), jnp.float32)] + block_shapes,
            in_specs=smem_specs(3) + vmem_specs(3 + groups),
            out_specs=vmem_specs(2 + groups),
            scratch_shapes=[
                pltpu.VMEM((plan.slots * BT, 2 * width), jnp.bfloat16),
                pltpu.VMEM((plan.slots * BT, 2 * width), jnp.float32),
                pltpu.VMEM((WINK, 2 * width), jnp.bfloat16),
            ],
            compiler_params=params(),
            cost_estimate=pl.CostEstimate(flops=5 * 2 * tokens_dom * WINK * width,
                                          bytes_accessed=8 * tokens_dom * width,
                                          transcendentals=tokens_dom * WINK * heads),
            name="attend",
        )(table, near, turns, qg, kv, bias, *arrived)
        returned = [lax.ppermute(outs[2 + i], "dom", [(d, p) for p, d in group["pairs"]])
                    for i, group in enumerate(plan.groups)]
        return outs[0], outs[1], returned

    def settle(grad_q, own, returned):
        grads = pl.pallas_call(
            functools.partial(settle_kernel, plan),
            out_shape=bf16(tokens_dom, 3 * width),
            in_specs=smem_specs(2) + vmem_specs(2 + groups),
            out_specs=vmem_specs(1)[0],
            scratch_shapes=[pltpu.VMEM((tokens_dom, 2 * width), jnp.float32)],
            compiler_params=params(),
            name="settle",
        )(table, sends, grad_q, own, *returned)
        grads = grads.reshape(holders, tokens, 3 * width)
        return lax.all_to_all(grads, "head", split_axis=0, concat_axis=0, tiled=True)

    kv = gather_heads(keys_in, values_in)
    qg = gather_heads(queries, grad_out)
    grads = []
    for chunk in range(chunks):
        grads.append(settle(*attend(kv[chunk], qg[chunk], lend(kv[chunk]), chunk)))
    return pl.pallas_call(
        functools.partial(unpack_kernel, chunks),
        out_shape=[bf16(tokens, holders * chunks * width)] * 3,
        in_specs=vmem_specs(chunks),
        out_specs=vmem_specs(3),
        compiler_params=params(),
        name="unpack",
    )(*grads)


def solution(mesh):
    plan = Plan(mesh.shape["dom"])
    tokens = P(("dom", "head"), None)
    return jax.shard_map(
        functools.partial(per_device, plan),
        mesh=mesh,
        in_specs=(
            tokens,
            tokens,
            tokens,
            tokens,
            P("head", None, None),
            P("dom", None),
            P("dom", None, None),
            P("dom", None),
        ),
        out_specs=(tokens, tokens, tokens),
        check_vma=False,
    )
```

```python
import functools

import jax
import jax.numpy as jnp
import numpy as np
from jax import lax
from jax.experimental import pallas as pl
from jax.experimental.pallas import tpu as pltpu
from jax.sharding import PartitionSpec as P

HD = 64
PATCH = 8
BT = 64
GRID_ROWS = 4
DIRS = 8
WIN = 9
WINK = 576
QB_DOM = 9
CAP = 3
GROUP_HEADS = 4
VMEM_LIMIT = 48 * 1024 * 1024

OFFSET_LIST = [(-1, -1), (-1, 0), (-1, 1), (0, -1), (0, 1), (1, -1), (1, 0), (1, 1)]


class Plan:
    def __init__(self, domains):
        cols = domains // GRID_ROWS
        cells = [divmod(d, cols) for d in range(domains)]
        steps = [(-1, 1)] if cols == 2 else [(-1,), (1,)] if cols > 2 else []
        self.side_pairs = [[(d + step, d) for step in side for d, (_, col) in enumerate(cells)
                            if 0 <= col + step < cols] for side in steps]
        self.rise_pairs = [[(d + step * cols, d) for d, (row, _) in enumerate(cells)
                            if 0 <= row + step < GRID_ROWS] for step in (-1, 1)]
        sides = len(steps)
        self.sides = sides
        self.rise_blocks = CAP + sides
        self.borrowed = sides * CAP + 2 * self.rise_blocks
        self.slots = QB_DOM + self.borrowed
        self.shapes = [CAP] * sides + [self.rise_blocks] * 2
        self.starts = [QB_DOM + sum(self.shapes[:i]) for i in range(len(self.shapes))]
        slot_total = QB_DOM + DIRS * CAP
        self.dir_at = slot_total
        self.lend_at = slot_total + self.borrowed
        table = np.zeros((domains, self.lend_at + 3 * sides), np.int32)
        for d, (_, col) in enumerate(cells):
            table[d, :QB_DOM] = np.arange(QB_DOM)

            def borrow(k, place, count):
                for c in range(CAP):
                    table[d, QB_DOM + k * CAP + c] = place + c % count
                table[d, self.dir_at + place - QB_DOM:self.dir_at + place - QB_DOM + count] = k

            for v, row_step in enumerate((-1, 1)):
                borrow(OFFSET_LIST.index((row_step, 0)), self.starts[sides + v], CAP)
            for i, side in enumerate(steps):
                for step in side:
                    if 0 <= col + step < cols:
                        borrow(OFFSET_LIST.index((0, step)), self.starts[i], CAP)
                        for v, row_step in enumerate((-1, 1)):
                            borrow(OFFSET_LIST.index((row_step, step)), self.starts[sides + v] + CAP + i, 1)
                    if 0 <= col - step < cols:
                        for n, row_step in enumerate((0, -1, 1)):
                            table[d, self.lend_at + 3 * i + n] = OFFSET_LIST.index((row_step, step))
        self.table = table

    def side_edge(self, i, c, table_ref, send_ref):
        return send_ref[table_ref[self.lend_at + 3 * i] * CAP + c]

    def side_corner(self, i, v, table_ref, send_ref):
        k = table_ref[self.lend_at + 3 * i + 1 + v]
        found = send_ref[k * CAP]
        for other in range(1, CAP):
            found = jnp.maximum(found, send_ref[k * CAP + other])
        return found

    def rise_edge(self, v, c, send_ref):
        return send_ref[OFFSET_LIST.index((2 * v - 1, 0)) * CAP + c]


def rows_of(c):
    return slice(c * BT, (c + 1) * BT)


def block_rows(index):
    return pl.ds(pl.multiple_of(index * BT, BT), BT)


def turn_matrix(orient, back):
    token = lax.broadcasted_iota(jnp.int32, (BT, BT), 1 if back else 0)
    place = lax.broadcasted_iota(jnp.int32, (BT, BT), 0 if back else 1)
    row, col = token >> 3, token & (PATCH - 1)
    row = jnp.where((orient & 1) == 1, PATCH - 1 - row, row)
    col = jnp.where(((orient >> 1) & 1) == 1, PATCH - 1 - col, col)
    mapped = jnp.where(orient >= 4, PATCH * col + row, PATCH * row + col)
    return (mapped == place).astype(jnp.float32).astype(jnp.bfloat16)


def pack_kernel(chunks, picked, left_ref, right_ref, *refs):
    out_ref = refs[-1]
    holders = out_ref.shape[0]
    width = left_ref.shape[1] // (holders * chunks)
    for s in range(holders):
        for n, chunk in enumerate(picked):
            at, to = (s * chunks + chunk) * width, 2 * n * width
            out_ref[s, :, to:to + width] = left_ref[:, at:at + width]
            out_ref[s, :, to + width:to + 2 * width] = right_ref[:, at:at + width]


def unpack_kernel(chunks, *refs):
    outs = refs[chunks:]
    holders, _, all_width = refs[0].shape
    width = all_width // len(outs)
    for chunk in range(chunks):
        for s in range(holders):
            at = (s * chunks + chunk) * width
            for which, out_ref in enumerate(outs):
                out_ref[:, at:at + width] = refs[chunk][s, :, which * width:(which + 1) * width]


def lend_corners_kernel(plan, table_ref, send_ref, kv_ref, *out_refs):
    for i in range(plan.sides):
        for v in range(2):
            block = plan.side_corner(i, v, table_ref, send_ref)
            out_refs[i][rows_of(v), :] = kv_ref[block_rows(block), :]


def lend_edges_kernel(plan, table_ref, send_ref, kv_ref, *refs):
    corners, out_refs = refs[:plan.sides], refs[plan.sides:]
    for v in range(2):
        out_ref = out_refs[plan.sides + v]
        for c in range(CAP):
            out_ref[rows_of(c), :] = kv_ref[block_rows(plan.rise_edge(v, c, send_ref)), :]
        for i in range(plan.sides):
            out_ref[rows_of(CAP + i), :] = corners[i][rows_of(v), :]
    for i in range(plan.sides):
        for c in range(CAP):
            out_refs[i][rows_of(c), :] = kv_ref[block_rows(plan.side_edge(i, c, table_ref, send_ref)), :]


def forward_kernel(plan, *refs):
    for i in range(plan.sides):
        for v in range(2):
            refs[2 + i][rows_of(v), :] = refs[v][rows_of(CAP + i), :]


def settle_kernel(plan, table_ref, send_ref, grad_q_ref, own_ref, *refs):
    out_ref, total = refs[-2:]
    sides, rises, corners = refs[:plan.sides], refs[plan.sides:plan.sides + 2], refs[plan.sides + 2:-2]
    width = grad_q_ref.shape[1]
    out_ref[:, :width] = grad_q_ref[...]
    total[...] = own_ref[...]

    def add(block, ref, c):
        total[block_rows(block), :] += ref[rows_of(c), :].astype(jnp.float32)

    for i in range(plan.sides):
        for c in range(CAP):
            add(plan.side_edge(i, c, table_ref, send_ref), sides[i], c)
        for v in range(2):
            add(plan.side_corner(i, v, table_ref, send_ref), corners[i], v)
    for v in range(2):
        for c in range(CAP):
            add(plan.rise_edge(v, c, send_ref), rises[v], c)
    out_ref[:, width:] = total[...].astype(jnp.bfloat16)


def dot(a, b, contract):
    return lax.dot_general(a, b, ((contract[:1], contract[1:]), ((), ())),
                           preferred_element_type=jnp.float32)


def attend_kernel(plan, heads, chunk, table_ref, near_ref, orient_ref, qg_ref, kv_ref, bias_ref, *refs):
    groups = len(plan.shapes)
    arrived = refs[:groups]
    dq_ref, own_ref, *leaving = refs[-5 - groups:-3]
    ext, acc, win = refs[-3:]
    width = heads * HD
    some = min(heads, GROUP_HEADS)
    lanes = some * HD
    scale = HD ** -0.5
    mine = slice(chunk * 2 * width, (chunk + 1) * 2 * width)

    def turned(i, c, back):
        return turn_matrix(orient_ref[table_ref[plan.dir_at + plan.starts[i] - QB_DOM + c]], back)

    ext[:QB_DOM * BT, :] = kv_ref[:, mine]
    for i, count in enumerate(plan.shapes):
        for c in range(count):
            if c == 0 or c >= CAP:
                turn = turned(i, c, False)
            ext[rows_of(plan.starts[i] + c), :] = dot(turn, arrived[i][rows_of(c), mine], (1, 0)).astype(jnp.bfloat16)
    acc[...] = jnp.zeros_like(acc)

    same_head = (lax.broadcasted_iota(jnp.int32, (lanes, lanes), 0) // HD
                 == lax.broadcasted_iota(jnp.int32, (lanes, lanes), 1) // HD)

    def spread(block):
        wide = jnp.concatenate([block] * some, axis=0)
        return jnp.where(same_head, wide, jnp.zeros_like(wide))

    def one_block(b, carry):
        rows = block_rows(b)
        places = [table_ref[near_ref[b * WIN + j]] for j in range(WIN)]
        for j in range(WIN):
            win[j * BT:(j + 1) * BT, :] = ext[block_rows(places[j]), :]
        for part in range(heads // some):
            here = slice(part * lanes, (part + 1) * lanes)
            there = slice(width + part * lanes, width + (part + 1) * lanes)
            win_k, win_v = win[:, here], win[:, there]
            query = spread(qg_ref[rows, here] * jnp.bfloat16(scale))
            grad = spread(qg_ref[rows, there])
            scores = dot(win_k, query, (1, 1)) + bias_ref[:, here]
            weight = jnp.exp(scores - jnp.max(scores, axis=0, keepdims=True))
            probs = weight * (1.0 / jnp.sum(weight, axis=0, keepdims=True))
            probs_half = probs.astype(jnp.bfloat16)
            dprobs = dot(win_v, grad, (1, 1))
            delta = jnp.sum(probs_half.astype(jnp.float32) * dprobs, axis=0, keepdims=True)
            dscores = (probs * (dprobs - delta)).astype(jnp.bfloat16)
            grad_q = dot(dscores, win_k, (0, 0))
            grad_q = jnp.where(same_head, grad_q, 0.0)
            total_q = grad_q[:BT]
            for h in range(1, some):
                total_q = total_q + grad_q[h * BT:(h + 1) * BT]
            dq_ref[rows, here] = (total_q * scale).astype(jnp.bfloat16)
            grad_k = dot(dscores, query, (1, 0))
            grad_v = dot(probs_half, grad, (1, 0))
            for j in range(WIN):
                acc[block_rows(places[j]), here] += grad_k[j * BT:(j + 1) * BT]
                acc[block_rows(places[j]), there] += grad_v[j * BT:(j + 1) * BT]
        return carry

    lax.fori_loop(0, QB_DOM, one_block, 0)
    own_ref[...] = acc[:QB_DOM * BT, :]
    for i, count in enumerate(plan.shapes):
        for c in range(count):
            if c == 0 or c >= CAP:
                turn = turned(i, c, True)
            slot = acc[rows_of(plan.starts[i] + c), :].astype(jnp.bfloat16)
            leaving[i][rows_of(c), :] = dot(turn, slot, (1, 0)).astype(jnp.bfloat16)


def smem_specs(count):
    return [pl.BlockSpec(memory_space=pltpu.SMEM)] * count


def vmem_specs(count):
    return [pl.BlockSpec(memory_space=pltpu.VMEM)] * count


def params():
    return pltpu.CompilerParams(vmem_limit_bytes=VMEM_LIMIT)


def bf16(*shape):
    return jax.ShapeDtypeStruct(shape, jnp.bfloat16)


def any_specs(count):
    return [pl.BlockSpec(memory_space=pl.ANY)] * count


def call(kernel, name, scalars, arrays, outs, after=(), **more):
    return pl.pallas_call(
        kernel,
        out_shape=outs,
        in_specs=smem_specs(len(scalars)) + vmem_specs(len(arrays)) + any_specs(len(after)),
        out_specs=vmem_specs(len(outs)),
        compiler_params=params(),
        name=name,
        **more,
    )(*scalars, *arrays, *after)


def per_device(plan, queries, keys_in, values_in, grad_out, pos_bias, neighbours, send_block, orient):
    chunks = 2 if pos_bias.shape[0] % 2 == 0 else 1
    heads = pos_bias.shape[0] // chunks
    width = heads * HD
    tokens = queries.shape[0]
    holders = lax.axis_size("head")
    tokens_dom = tokens * holders
    sides = plan.sides
    table = lax.dynamic_index_in_dim(jnp.asarray(plan.table), lax.axis_index("dom"), 0, False)
    near, sends, turns = neighbours.reshape(-1), send_block.reshape(-1), orient.reshape(-1)

    def swap(matrix):
        return lax.all_to_all(matrix, "head", split_axis=0, concat_axis=0, tiled=True)

    def pack(left, right, picked, after):
        return call(functools.partial(pack_kernel, chunks, picked), "pack", [], [left, right],
                    [bf16(holders, tokens, 2 * len(picked) * width)], after)[0]

    def permute(value, pairs):
        return lax.ppermute(value, "dom", pairs)

    def permute_back(value, pairs):
        return lax.ppermute(value, "dom", [(d, p) for p, d in pairs])

    def lend(kv):
        columns = kv.shape[1]
        corners = call(functools.partial(lend_corners_kernel, plan), "lend_corners", [table, sends], [kv],
                       [bf16(2 * BT, columns)] * sides)
        corners = [permute(x, pairs) for x, pairs in zip(corners, plan.side_pairs)]
        lent = call(functools.partial(lend_edges_kernel, plan), "lend_edges", [table, sends], [kv, *corners],
                    [bf16(count * BT, columns) for count in plan.shapes])
        return [permute(x, pairs) for x, pairs in zip(lent, plan.side_pairs + plan.rise_pairs)]

    def attend(kv, qg, arrived, chunk, after):
        bias = jnp.transpose(pos_bias[chunk * heads:(chunk + 1) * heads], (2, 0, 1)).reshape(WINK, heads * BT)
        grad_q, own, *leaving = call(
            functools.partial(attend_kernel, plan, heads, chunk), "attend", [table, near, turns],
            [qg, kv, bias, *arrived],
            [bf16(tokens_dom, width), jax.ShapeDtypeStruct((tokens_dom, 2 * width), jnp.float32)]
            + [bf16(count * BT, 2 * width) for count in plan.shapes], after,
            scratch_shapes=[
                pltpu.VMEM((plan.slots * BT, 2 * width), jnp.bfloat16),
                pltpu.VMEM((plan.slots * BT, 2 * width), jnp.float32),
                pltpu.VMEM((WINK, 2 * width), jnp.bfloat16),
            ],
            cost_estimate=pl.CostEstimate(flops=5 * 2 * tokens_dom * WINK * width,
                                          bytes_accessed=8 * tokens_dom * width,
                                          transcendentals=tokens_dom * WINK * heads),
        )
        rises = [permute_back(x, pairs) for x, pairs in zip(leaving[sides:], plan.rise_pairs)]
        edges = [permute_back(x, pairs) for x, pairs in zip(leaving[:sides], plan.side_pairs)]
        corners = call(functools.partial(forward_kernel, plan), "forward", [], rises, [bf16(2 * BT, 2 * width)] * sides)
        corners = [permute_back(x, pairs) for x, pairs in zip(corners, plan.side_pairs)]
        return call(functools.partial(settle_kernel, plan), "settle", [table, sends],
                    [grad_q, own, *edges, *rises, *corners], [bf16(tokens_dom, 3 * width)],
                    scratch_shapes=[pltpu.VMEM((tokens_dom, 2 * width), jnp.float32)])[0]

    kv = swap(pack(keys_in, values_in, range(chunks), ())).reshape(tokens_dom, 2 * chunks * width)
    arrived = lend(kv)
    packed, qg = [], []
    for chunk in range(chunks):
        packed.append(pack(queries, grad_out, [chunk], [kv] if chunk == 0 else [qg[-1], arrived[-1]]))
        qg.append(swap(packed[-1]).reshape(tokens_dom, 2 * width))
    settled, grads = [], []
    for chunk in range(chunks):
        after = packed[chunk + 1:chunk + 2] + settled[-1:]
        settled.append(attend(kv, qg[chunk], arrived, chunk, after))
        grads.append(swap(settled[-1].reshape(holders, tokens, 3 * width)))
    return call(functools.partial(unpack_kernel, chunks), "unpack", [], grads,
                [bf16(tokens, holders * chunks * width)] * 3)


def solution(mesh):
    plan = Plan(mesh.shape["dom"])
    tokens = P(("dom", "head"), None)
    return jax.shard_map(
        functools.partial(per_device, plan),
        mesh=mesh,
        in_specs=(
            tokens,
            tokens,
            tokens,
            tokens,
            P("head", None, None),
            P("dom", None),
            P("dom", None, None),
            P("dom", None),
        ),
        out_specs=(tokens, tokens, tokens),
        check_vma=False,
    )
```

```python
import functools

import jax
import jax.numpy as jnp
import numpy as np
from jax import lax
from jax.experimental import pallas as pl
from jax.experimental.pallas import tpu as pltpu
from jax.sharding import PartitionSpec as P

HD = 64
PATCH = 8
BT = 64
GRID_ROWS = 4
DIRS = 8
WIN = 9
WINK = 576
QB_DOM = 9
CAP = 3
SLAB = 32
VMEM_LIMIT = 48 * 1024 * 1024

OFFSET_LIST = [(-1, -1), (-1, 0), (-1, 1), (0, -1), (0, 1), (1, -1), (1, 0), (1, 1)]


class Plan:
    def __init__(self, domains):
        cols = domains // GRID_ROWS
        cells = [divmod(d, cols) for d in range(domains)]
        steps = [(-1, 1)] if cols == 2 else [(-1,), (1,)] if cols > 2 else []
        self.side_pairs = [[(d + step, d) for step in side for d, (_, col) in enumerate(cells)
                            if 0 <= col + step < cols] for side in steps]
        self.rise_pairs = [[(d + step * cols, d) for d, (row, _) in enumerate(cells)
                            if 0 <= row + step < GRID_ROWS] for step in (-1, 1)]
        sides = len(steps)
        self.sides = sides
        self.rise_blocks = CAP + sides
        self.borrowed = sides * CAP + 2 * self.rise_blocks
        self.slots = QB_DOM + self.borrowed
        self.shapes = [CAP] * sides + [self.rise_blocks] * 2
        self.starts = [QB_DOM + sum(self.shapes[:i]) for i in range(len(self.shapes))]
        slot_total = QB_DOM + DIRS * CAP
        self.dir_at = slot_total
        self.lend_at = slot_total + self.borrowed
        table = np.zeros((domains, self.lend_at + 3 * sides), np.int32)
        for d, (_, col) in enumerate(cells):
            table[d, :QB_DOM] = np.arange(QB_DOM)

            def borrow(k, place, count):
                for c in range(CAP):
                    table[d, QB_DOM + k * CAP + c] = place + c % count
                table[d, self.dir_at + place - QB_DOM:self.dir_at + place - QB_DOM + count] = k

            for v, row_step in enumerate((-1, 1)):
                borrow(OFFSET_LIST.index((row_step, 0)), self.starts[sides + v], CAP)
            for i, side in enumerate(steps):
                for step in side:
                    if 0 <= col + step < cols:
                        borrow(OFFSET_LIST.index((0, step)), self.starts[i], CAP)
                        for v, row_step in enumerate((-1, 1)):
                            borrow(OFFSET_LIST.index((row_step, step)), self.starts[sides + v] + CAP + i, 1)
                    if 0 <= col - step < cols:
                        for n, row_step in enumerate((0, -1, 1)):
                            table[d, self.lend_at + 3 * i + n] = OFFSET_LIST.index((row_step, step))
        self.table = table

    def side_edge(self, i, c, table_ref, send_ref):
        return send_ref[table_ref[self.lend_at + 3 * i] * CAP + c]

    def side_corner(self, i, v, table_ref, send_ref):
        k = table_ref[self.lend_at + 3 * i + 1 + v]
        found = send_ref[k * CAP]
        for other in range(1, CAP):
            found = jnp.maximum(found, send_ref[k * CAP + other])
        return found

    def rise_edge(self, v, c, send_ref):
        return send_ref[OFFSET_LIST.index((2 * v - 1, 0)) * CAP + c]


def rows_of(c):
    return slice(c * BT, (c + 1) * BT)


def block_rows(index):
    return pl.ds(pl.multiple_of(index * BT, BT), BT)


def turn_matrix(orient, back):
    token = lax.broadcasted_iota(jnp.int32, (BT, BT), 1 if back else 0)
    place = lax.broadcasted_iota(jnp.int32, (BT, BT), 0 if back else 1)
    row, col = token >> 3, token & (PATCH - 1)
    row = jnp.where((orient & 1) == 1, PATCH - 1 - row, row)
    col = jnp.where(((orient >> 1) & 1) == 1, PATCH - 1 - col, col)
    mapped = jnp.where(orient >= 4, PATCH * col + row, PATCH * row + col)
    return (mapped == place).astype(jnp.float32).astype(jnp.bfloat16)


def pack_kernel(chunks, picked, left_ref, right_ref, *refs):
    out_ref = refs[-1]
    holders = out_ref.shape[0]
    width = left_ref.shape[1] // (holders * chunks)
    for s in range(holders):
        for n, chunk in enumerate(picked):
            at, to = (s * chunks + chunk) * width, 2 * n * width
            out_ref[s, :, to:to + width] = left_ref[:, at:at + width]
            out_ref[s, :, to + width:to + 2 * width] = right_ref[:, at:at + width]


def unpack_kernel(chunks, *refs):
    outs = refs[chunks:]
    holders, _, all_width = refs[0].shape
    width = all_width // len(outs)
    for chunk in range(chunks):
        for s in range(holders):
            at = (s * chunks + chunk) * width
            for which, out_ref in enumerate(outs):
                out_ref[:, at:at + width] = refs[chunk][s, :, which * width:(which + 1) * width]


def lend_corners_kernel(plan, table_ref, send_ref, kv_ref, *out_refs):
    for i in range(plan.sides):
        for v in range(2):
            block = plan.side_corner(i, v, table_ref, send_ref)
            out_refs[i][rows_of(v), :] = kv_ref[block_rows(block), :]


def lend_edges_kernel(plan, table_ref, send_ref, kv_ref, *refs):
    corners, out_refs = refs[:plan.sides], refs[plan.sides:]
    for v in range(2):
        out_ref = out_refs[plan.sides + v]
        for c in range(CAP):
            out_ref[rows_of(c), :] = kv_ref[block_rows(plan.rise_edge(v, c, send_ref)), :]
        for i in range(plan.sides):
            out_ref[rows_of(CAP + i), :] = corners[i][rows_of(v), :]
    for i in range(plan.sides):
        for c in range(CAP):
            out_refs[i][rows_of(c), :] = kv_ref[block_rows(plan.side_edge(i, c, table_ref, send_ref)), :]


def forward_kernel(plan, *refs):
    for i in range(plan.sides):
        for v in range(2):
            refs[2 + i][rows_of(v), :] = refs[v][rows_of(CAP + i), :]


def settle_kernel(plan, table_ref, send_ref, grad_q_ref, own_ref, *refs):
    out_ref, total = refs[-2:]
    sides, rises, corners = refs[:plan.sides], refs[plan.sides:plan.sides + 2], refs[plan.sides + 2:-2]
    width = grad_q_ref.shape[1]
    out_ref[:, :width] = grad_q_ref[...]
    total[...] = own_ref[...]

    def add(block, ref, c):
        total[block_rows(block), :] += ref[rows_of(c), :].astype(jnp.float32)

    for i in range(plan.sides):
        for c in range(CAP):
            add(plan.side_edge(i, c, table_ref, send_ref), sides[i], c)
        for v in range(2):
            add(plan.side_corner(i, v, table_ref, send_ref), corners[i], v)
    for v in range(2):
        for c in range(CAP):
            add(plan.rise_edge(v, c, send_ref), rises[v], c)
    out_ref[:, width:] = total[...].astype(jnp.bfloat16)


def dot(a, b, contract):
    return lax.dot_general(a, b, ((contract[:1], contract[1:]), ((), ())),
                           preferred_element_type=jnp.float32)


def attend_kernel(plan, heads, table_ref, near_ref, orient_ref, qg_ref, kv_ref, bias_ref, *refs):
    groups = len(plan.shapes)
    arrived = refs[:groups]
    dq_ref, own_ref, *leaving = refs[-8 - groups:-6]
    ext, acc, win, work, probs_ref, dscores_ref = refs[-6:]
    width = heads * HD
    scale = HD ** -0.5
    keys, values = slice(0, width), slice(width, 2 * width)
    slabs = [slice(at, at + SLAB) for at in range(0, WINK, SLAB)]

    def turned(i, c, back):
        return turn_matrix(orient_ref[table_ref[plan.dir_at + plan.starts[i] - QB_DOM + c]], back)

    ext[:QB_DOM * BT, :] = kv_ref[...]
    for i, count in enumerate(plan.shapes):
        for c in range(count):
            if c == 0 or c >= CAP:
                turn = turned(i, c, False)
            ext[rows_of(plan.starts[i] + c), :] = dot(turn, arrived[i][rows_of(c), :], (1, 0)).astype(jnp.bfloat16)
    acc[...] = jnp.zeros_like(acc)

    same_head = (lax.broadcasted_iota(jnp.int32, (width, width), 0) // HD
                 == lax.broadcasted_iota(jnp.int32, (width, width), 1) // HD)

    def spread(block):
        wide = jnp.concatenate([block] * heads, axis=0)
        return jnp.where(same_head, wide, jnp.zeros_like(wide))

    def products(b):
        even = b % 2
        places = [table_ref[near_ref[b * WIN + j]] for j in range(WIN)]
        for j in range(WIN):
            win[even, rows_of(j), :] = ext[block_rows(places[j]), :]
        query = spread(qg_ref[rows_of(b), keys] * jnp.bfloat16(scale))
        grad = spread(qg_ref[rows_of(b), values])
        work[even, 0] = dot(win[even, :, keys], query, (1, 1)) + bias_ref[...]
        work[even, 1] = dot(win[even, :, values], grad, (1, 1))
        return places, query, grad

    def softmax(b):
        even = b % 2
        top = work[even, 0, slabs[0], :]
        for slab in slabs[1:]:
            top = jnp.maximum(top, work[even, 0, slab, :])
        top = jnp.max(top, axis=0, keepdims=True)
        total = jnp.zeros((SLAB, width), jnp.float32)
        delta = jnp.zeros((SLAB, width), jnp.float32)
        for slab in slabs:
            weight = jnp.exp(work[even, 0, slab, :] - top)
            work[even, 0, slab, :] = weight
            total = total + weight
            delta = delta + weight * work[even, 1, slab, :]
        inverse = 1.0 / jnp.sum(total, axis=0, keepdims=True)
        delta = jnp.sum(delta, axis=0, keepdims=True) * inverse
        for slab in slabs:
            probs = work[even, 0, slab, :] * inverse
            probs_ref[even, slab, :] = probs.astype(jnp.bfloat16)
            dscores_ref[even, slab, :] = (probs * (work[even, 1, slab, :] - delta)).astype(jnp.bfloat16)

    def gradients(b, places, query, grad):
        even = b % 2
        dscores = dscores_ref[even]
        grad_q = dot(dscores, win[even, :, keys], (0, 0))
        grad_q = jnp.where(same_head, grad_q, 0.0)
        total_q = grad_q[:BT]
        for h in range(1, heads):
            total_q = total_q + grad_q[rows_of(h)]
        dq_ref[rows_of(b), :] = (total_q * scale).astype(jnp.bfloat16)
        grad_k = dot(dscores, query, (1, 0))
        grad_v = dot(probs_ref[even], grad, (1, 0))
        for j in range(WIN):
            acc[block_rows(places[j]), keys] += grad_k[rows_of(j)]
            acc[block_rows(places[j]), values] += grad_v[rows_of(j)]

    here = products(0)
    for b in range(QB_DOM):
        following = products(b + 1) if b + 1 < QB_DOM else None
        softmax(b)
        gradients(b, *here)
        here = following

    own_ref[...] = acc[:QB_DOM * BT, :]
    for i, count in enumerate(plan.shapes):
        for c in range(count):
            if c == 0 or c >= CAP:
                turn = turned(i, c, True)
            slot = acc[rows_of(plan.starts[i] + c), :].astype(jnp.bfloat16)
            leaving[i][rows_of(c), :] = dot(turn, slot, (1, 0)).astype(jnp.bfloat16)


def smem_specs(count):
    return [pl.BlockSpec(memory_space=pltpu.SMEM)] * count


def vmem_specs(count):
    return [pl.BlockSpec(memory_space=pltpu.VMEM)] * count


def params():
    return pltpu.CompilerParams(vmem_limit_bytes=VMEM_LIMIT)


def bf16(*shape):
    return jax.ShapeDtypeStruct(shape, jnp.bfloat16)


def any_specs(count):
    return [pl.BlockSpec(memory_space=pl.ANY)] * count


def call(kernel, name, scalars, arrays, outs, after=(), **more):
    return pl.pallas_call(
        kernel,
        out_shape=outs,
        in_specs=smem_specs(len(scalars)) + vmem_specs(len(arrays)) + any_specs(len(after)),
        out_specs=vmem_specs(len(outs)),
        compiler_params=params(),
        name=name,
        **more,
    )(*scalars, *arrays, *after)


def per_device(plan, queries, keys_in, values_in, grad_out, pos_bias, neighbours, send_block, orient):
    chunks = 2 if pos_bias.shape[0] % 2 == 0 else 1
    heads = pos_bias.shape[0] // chunks
    width = heads * HD
    tokens = queries.shape[0]
    holders = lax.axis_size("head")
    tokens_dom = tokens * holders
    sides = plan.sides
    table = lax.dynamic_index_in_dim(jnp.asarray(plan.table), lax.axis_index("dom"), 0, False)
    near, sends, turns = neighbours.reshape(-1), send_block.reshape(-1), orient.reshape(-1)

    def swap(matrix):
        return lax.all_to_all(matrix, "head", split_axis=0, concat_axis=0, tiled=True)

    def pack(left, right, picked, after):
        return call(functools.partial(pack_kernel, chunks, picked), "pack", [], [left, right],
                    [bf16(holders, tokens, 2 * len(picked) * width)], after)[0]

    def permute(value, pairs):
        return lax.ppermute(value, "dom", pairs)

    def permute_back(value, pairs):
        return lax.ppermute(value, "dom", [(d, p) for p, d in pairs])

    def lend(kv):
        columns = kv.shape[1]
        corners = call(functools.partial(lend_corners_kernel, plan), "lend_corners", [table, sends], [kv],
                       [bf16(2 * BT, columns)] * sides)
        corners = [permute(x, pairs) for x, pairs in zip(corners, plan.side_pairs)]
        lent = call(functools.partial(lend_edges_kernel, plan), "lend_edges", [table, sends], [kv, *corners],
                    [bf16(count * BT, columns) for count in plan.shapes])
        return [permute(x, pairs) for x, pairs in zip(lent, plan.side_pairs + plan.rise_pairs)]

    def attend(kv, qg, arrived, bias, after, settle_after):
        grad_q, own, *leaving = call(
            functools.partial(attend_kernel, plan, heads), "attend", [table, near, turns],
            [qg, kv, bias, *arrived],
            [bf16(tokens_dom, width), jax.ShapeDtypeStruct((tokens_dom, 2 * width), jnp.float32)]
            + [bf16(count * BT, 2 * width) for count in plan.shapes], after,
            scratch_shapes=[
                pltpu.VMEM((plan.slots * BT, 2 * width), jnp.bfloat16),
                pltpu.VMEM((plan.slots * BT, 2 * width), jnp.float32),
                pltpu.VMEM((2, WINK, 2 * width), jnp.bfloat16),
                pltpu.VMEM((2, 2, WINK, width), jnp.float32),
                pltpu.VMEM((2, WINK, width), jnp.bfloat16),
                pltpu.VMEM((2, WINK, width), jnp.bfloat16),
            ],
            cost_estimate=pl.CostEstimate(flops=5 * 2 * tokens_dom * WINK * width,
                                          bytes_accessed=8 * tokens_dom * width,
                                          transcendentals=tokens_dom * WINK * heads),
        )
        rises = [permute_back(x, pairs) for x, pairs in zip(leaving[sides:], plan.rise_pairs)]
        edges = [permute_back(x, pairs) for x, pairs in zip(leaving[:sides], plan.side_pairs)]
        corners = call(functools.partial(forward_kernel, plan), "forward", [], rises, [bf16(2 * BT, 2 * width)] * sides)
        corners = [permute_back(x, pairs) for x, pairs in zip(corners, plan.side_pairs)]
        return call(functools.partial(settle_kernel, plan), "settle", [table, sends],
                    [grad_q, own, *edges, *rises, *corners], [bf16(tokens_dom, 3 * width)],
                    settle_after, scratch_shapes=[pltpu.VMEM((tokens_dom, 2 * width), jnp.float32)])[0]

    bias = [jnp.transpose(x, (2, 0, 1)).reshape(WINK, heads * BT)
            for x in jnp.split(pos_bias, chunks, axis=0)]
    packed, kv, qg, arrived, settled, grads = [], [], [], [], [], []
    for chunk in range(chunks):
        packed.append(pack(keys_in, values_in, [chunk], qg[-1:]))
        kv.append(swap(packed[-1]).reshape(tokens_dom, 2 * width))
        qg.append(pack(queries, grad_out, [chunk], [kv[-1]] + (bias if chunk == 0 else [])))
        qg[-1] = swap(qg[-1]).reshape(tokens_dom, 2 * width)
        arrived.append(lend(kv[-1]))
    for chunk in range(chunks):
        settled.append(attend(kv[chunk], qg[chunk], arrived[chunk], bias[chunk],
                              packed[chunk + 1:chunk + 2] + settled[-1:], qg[chunk + 1:chunk + 2]))
        grads.append(swap(settled[-1].reshape(holders, tokens, 3 * width)))
    return call(functools.partial(unpack_kernel, chunks), "unpack", [], grads,
                [bf16(tokens, holders * chunks * width)] * 3)


def solution(mesh):
    plan = Plan(mesh.shape["dom"])
    tokens = P(("dom", "head"), None)
    return jax.shard_map(
        functools.partial(per_device, plan),
        mesh=mesh,
        in_specs=(
            tokens,
            tokens,
            tokens,
            tokens,
            P("head", None, None),
            P("dom", None),
            P("dom", None, None),
            P("dom", None),
        ),
        out_specs=(tokens, tokens, tokens),
        check_vma=False,
    )
```

```python
import functools

import jax
import jax.numpy as jnp
import numpy as np
from jax import lax
from jax.experimental import pallas as pl
from jax.experimental.pallas import tpu as pltpu
from jax.sharding import PartitionSpec as P

HD = 64
PATCH = 8
BT = 64
GRID_ROWS = 4
DIRS = 8
WIN = 9
WINK = 576
QB_DOM = 9
CAP = 3
SLAB = 32
VMEM_LIMIT = 48 * 1024 * 1024

OFFSET_LIST = [(-1, -1), (-1, 0), (-1, 1), (0, -1), (0, 1), (1, -1), (1, 0), (1, 1)]


class Plan:
    def __init__(self, domains):
        cols = domains // GRID_ROWS
        cells = [divmod(d, cols) for d in range(domains)]
        steps = [(-1, 1)] if cols == 2 else [(-1,), (1,)] if cols > 2 else []
        self.side_pairs = [[(d + step, d) for step in side for d, (_, col) in enumerate(cells)
                            if 0 <= col + step < cols] for side in steps]
        self.rise_pairs = [[(d + step * cols, d) for d, (row, _) in enumerate(cells)
                            if 0 <= row + step < GRID_ROWS] for step in (-1, 1)]
        sides = len(steps)
        self.sides = sides
        self.rise_blocks = CAP + sides
        self.borrowed = sides * CAP + 2 * self.rise_blocks
        self.slots = QB_DOM + self.borrowed
        self.shapes = [CAP] * sides + [self.rise_blocks] * 2
        self.starts = [QB_DOM + sum(self.shapes[:i]) for i in range(len(self.shapes))]
        slot_total = QB_DOM + DIRS * CAP
        self.dir_at = slot_total
        self.lend_at = slot_total + self.borrowed
        table = np.zeros((domains, self.lend_at + 3 * sides), np.int32)
        for d, (_, col) in enumerate(cells):
            table[d, :QB_DOM] = np.arange(QB_DOM)

            def borrow(k, place, count):
                for c in range(CAP):
                    table[d, QB_DOM + k * CAP + c] = place + c % count
                table[d, self.dir_at + place - QB_DOM:self.dir_at + place - QB_DOM + count] = k

            for v, row_step in enumerate((-1, 1)):
                borrow(OFFSET_LIST.index((row_step, 0)), self.starts[sides + v], CAP)
            for i, side in enumerate(steps):
                for step in side:
                    if 0 <= col + step < cols:
                        borrow(OFFSET_LIST.index((0, step)), self.starts[i], CAP)
                        for v, row_step in enumerate((-1, 1)):
                            borrow(OFFSET_LIST.index((row_step, step)), self.starts[sides + v] + CAP + i, 1)
                    if 0 <= col - step < cols:
                        for n, row_step in enumerate((0, -1, 1)):
                            table[d, self.lend_at + 3 * i + n] = OFFSET_LIST.index((row_step, step))
        self.table = table

    def side_edge(self, i, c, table_ref, send_ref):
        return send_ref[table_ref[self.lend_at + 3 * i] * CAP + c]

    def side_corner(self, i, v, table_ref, send_ref):
        k = table_ref[self.lend_at + 3 * i + 1 + v]
        found = send_ref[k * CAP]
        for other in range(1, CAP):
            found = jnp.maximum(found, send_ref[k * CAP + other])
        return found

    def rise_edge(self, v, c, send_ref):
        return send_ref[OFFSET_LIST.index((2 * v - 1, 0)) * CAP + c]


def rows_of(c):
    return slice(c * BT, (c + 1) * BT)


def block_rows(index):
    return pl.ds(pl.multiple_of(index * BT, BT), BT)


def turn_matrix(orient, back):
    token = lax.broadcasted_iota(jnp.int32, (BT, BT), 1 if back else 0)
    place = lax.broadcasted_iota(jnp.int32, (BT, BT), 0 if back else 1)
    row, col = token >> 3, token & (PATCH - 1)
    row = jnp.where((orient & 1) == 1, PATCH - 1 - row, row)
    col = jnp.where(((orient >> 1) & 1) == 1, PATCH - 1 - col, col)
    mapped = jnp.where(orient >= 4, PATCH * col + row, PATCH * row + col)
    return (mapped == place).astype(jnp.float32).astype(jnp.bfloat16)


def pack_kernel(chunks, picked, left_ref, right_ref, *refs):
    out_ref = refs[-1]
    holders = out_ref.shape[0]
    width = left_ref.shape[1] // (holders * chunks)
    for s in range(holders):
        for n, chunk in enumerate(picked):
            at, to = (s * chunks + chunk) * width, 2 * n * width
            out_ref[s, :, to:to + width] = left_ref[:, at:at + width]
            out_ref[s, :, to + width:to + 2 * width] = right_ref[:, at:at + width]


def unpack_kernel(chunks, *refs):
    outs = refs[chunks:]
    holders, _, all_width = refs[0].shape
    width = all_width // len(outs)
    for chunk in range(chunks):
        for s in range(holders):
            at = (s * chunks + chunk) * width
            for which, out_ref in enumerate(outs):
                out_ref[:, at:at + width] = refs[chunk][s, :, which * width:(which + 1) * width]


def lend_corners_kernel(plan, table_ref, send_ref, kv_ref, *out_refs):
    for i in range(plan.sides):
        for v in range(2):
            block = plan.side_corner(i, v, table_ref, send_ref)
            out_refs[i][rows_of(v), :] = kv_ref[block_rows(block), :]


def lend_edges_kernel(plan, table_ref, send_ref, kv_ref, *refs):
    corners, out_refs = refs[:plan.sides], refs[plan.sides:]
    for v in range(2):
        out_ref = out_refs[plan.sides + v]
        for c in range(CAP):
            out_ref[rows_of(c), :] = kv_ref[block_rows(plan.rise_edge(v, c, send_ref)), :]
        for i in range(plan.sides):
            out_ref[rows_of(CAP + i), :] = corners[i][rows_of(v), :]
    for i in range(plan.sides):
        for c in range(CAP):
            out_refs[i][rows_of(c), :] = kv_ref[block_rows(plan.side_edge(i, c, table_ref, send_ref)), :]


def forward_kernel(plan, *refs):
    for i in range(plan.sides):
        for v in range(2):
            refs[2 + i][rows_of(v), :] = refs[v][rows_of(CAP + i), :]


def settle_kernel(plan, table_ref, send_ref, grad_q_ref, own_ref, *refs):
    out_ref, total = refs[-2:]
    sides, rises, corners = refs[:plan.sides], refs[plan.sides:plan.sides + 2], refs[plan.sides + 2:-2]
    width = grad_q_ref.shape[1]
    out_ref[:, :width] = grad_q_ref[...]
    total[...] = own_ref[...]

    def add(block, ref, c):
        total[block_rows(block), :] += ref[rows_of(c), :].astype(jnp.float32)

    for i in range(plan.sides):
        for c in range(CAP):
            add(plan.side_edge(i, c, table_ref, send_ref), sides[i], c)
        for v in range(2):
            add(plan.side_corner(i, v, table_ref, send_ref), corners[i], v)
    for v in range(2):
        for c in range(CAP):
            add(plan.rise_edge(v, c, send_ref), rises[v], c)
    out_ref[:, width:] = total[...].astype(jnp.bfloat16)


def dot(a, b, contract):
    return lax.dot_general(a, b, ((contract[:1], contract[1:]), ((), ())),
                           preferred_element_type=jnp.float32)


def attend_kernel(plan, heads, table_ref, near_ref, orient_ref, qg_ref, kv_ref, bias_ref, *refs):
    groups = len(plan.shapes)
    arrived = refs[:groups]
    dq_ref, own_ref, *leaving = refs[-8 - groups:-6]
    ext, acc, win, work, probs_ref, dscores_ref = refs[-6:]
    width = heads * HD
    scale = HD ** -0.5
    keys, values = slice(0, width), slice(width, 2 * width)
    slabs = [slice(at, at + SLAB) for at in range(0, WINK, SLAB)]

    def turned(i, c, back):
        return turn_matrix(orient_ref[table_ref[plan.dir_at + plan.starts[i] - QB_DOM + c]], back)

    ext[:QB_DOM * BT, :] = kv_ref[...]
    for i, count in enumerate(plan.shapes):
        for c in range(count):
            if c == 0 or c >= CAP:
                turn = turned(i, c, False)
            ext[rows_of(plan.starts[i] + c), :] = dot(turn, arrived[i][rows_of(c), :], (1, 0)).astype(jnp.bfloat16)
    acc[...] = jnp.zeros_like(acc)

    same_head = (lax.broadcasted_iota(jnp.int32, (width, width), 0) // HD
                 == lax.broadcasted_iota(jnp.int32, (width, width), 1) // HD)

    def spread(block):
        wide = jnp.concatenate([block] * heads, axis=0)
        return jnp.where(same_head, wide, jnp.zeros_like(wide))

    def products(b):
        even = b % 2
        places = [table_ref[near_ref[b * WIN + j]] for j in range(WIN)]
        for j in range(WIN):
            win[even, rows_of(j), :] = ext[block_rows(places[j]), :]
        query = spread(qg_ref[rows_of(b), keys] * jnp.bfloat16(scale))
        grad = spread(qg_ref[rows_of(b), values])
        work[even, 0] = dot(win[even, :, keys], query, (1, 1)) + bias_ref[...]
        work[even, 1] = dot(win[even, :, values], grad, (1, 1))
        return places, query, grad

    def softmax(b):
        even = b % 2
        top = work[even, 0, slabs[0], :]
        for slab in slabs[1:]:
            top = jnp.maximum(top, work[even, 0, slab, :])
        top = jnp.max(top, axis=0, keepdims=True)
        total = jnp.zeros((SLAB, width), jnp.float32)
        delta = jnp.zeros((SLAB, width), jnp.float32)
        for slab in slabs:
            weight = jnp.exp(work[even, 0, slab, :] - top)
            work[even, 0, slab, :] = weight
            total = total + weight
            delta = delta + weight * work[even, 1, slab, :]
        inverse = 1.0 / jnp.sum(total, axis=0, keepdims=True)
        delta = jnp.sum(delta, axis=0, keepdims=True) * inverse
        for slab in slabs:
            probs = work[even, 0, slab, :] * inverse
            probs_ref[even, slab, :] = probs.astype(jnp.bfloat16)
            dscores_ref[even, slab, :] = (probs * (work[even, 1, slab, :] - delta)).astype(jnp.bfloat16)

    def gradients(b, places, query, grad):
        even = b % 2
        dscores = dscores_ref[even]
        grad_q = dot(dscores, win[even, :, keys], (0, 0))
        grad_q = jnp.where(same_head, grad_q, 0.0)
        total_q = grad_q[:BT]
        for h in range(1, heads):
            total_q = total_q + grad_q[rows_of(h)]
        dq_ref[rows_of(b), :] = (total_q * scale).astype(jnp.bfloat16)
        grad_k = dot(dscores, query, (1, 0))
        grad_v = dot(probs_ref[even], grad, (1, 0))
        for j in range(WIN):
            acc[block_rows(places[j]), keys] += grad_k[rows_of(j)]
            acc[block_rows(places[j]), values] += grad_v[rows_of(j)]

    here = products(0)
    for b in range(QB_DOM):
        following = products(b + 1) if b + 1 < QB_DOM else None
        softmax(b)
        gradients(b, *here)
        here = following

    own_ref[...] = acc[:QB_DOM * BT, :]
    for i, count in enumerate(plan.shapes):
        for c in range(count):
            if c == 0 or c >= CAP:
                turn = turned(i, c, True)
            slot = acc[rows_of(plan.starts[i] + c), :].astype(jnp.bfloat16)
            leaving[i][rows_of(c), :] = dot(turn, slot, (1, 0)).astype(jnp.bfloat16)


def smem_specs(count):
    return [pl.BlockSpec(memory_space=pltpu.SMEM)] * count


def vmem_specs(count):
    return [pl.BlockSpec(memory_space=pltpu.VMEM)] * count


def params():
    return pltpu.CompilerParams(vmem_limit_bytes=VMEM_LIMIT)


def bf16(*shape):
    return jax.ShapeDtypeStruct(shape, jnp.bfloat16)


def any_specs(count):
    return [pl.BlockSpec(memory_space=pl.ANY)] * count


def call(kernel, name, scalars, arrays, outs, after=(), **more):
    taken = len(scalars) + len(arrays)

    def body(*refs):
        kernel(*refs[:taken], *refs[taken + len(after):])

    return pl.pallas_call(
        body,
        out_shape=outs,
        in_specs=smem_specs(len(scalars)) + vmem_specs(len(arrays)) + any_specs(len(after)),
        out_specs=vmem_specs(len(outs)),
        compiler_params=params(),
        name=name,
        **more,
    )(*scalars, *arrays, *after)


def per_device(plan, queries, keys_in, values_in, grad_out, pos_bias, neighbours, send_block, orient):
    chunks = 2 if pos_bias.shape[0] % 2 == 0 else 1
    heads = pos_bias.shape[0] // chunks
    width = heads * HD
    tokens = queries.shape[0]
    holders = lax.axis_size("head")
    tokens_dom = tokens * holders
    sides = plan.sides
    table = lax.dynamic_index_in_dim(jnp.asarray(plan.table), lax.axis_index("dom"), 0, False)
    near, sends, turns = neighbours.reshape(-1), send_block.reshape(-1), orient.reshape(-1)

    def swap(matrix):
        return lax.all_to_all(matrix, "head", split_axis=0, concat_axis=0, tiled=True)

    def pack(left, right, picked, after):
        return call(functools.partial(pack_kernel, chunks, picked), "pack", [], [left, right],
                    [bf16(holders, tokens, 2 * len(picked) * width)], after)[0]

    def permute(value, pairs):
        return lax.ppermute(value, "dom", pairs)

    def permute_back(value, pairs):
        return lax.ppermute(value, "dom", [(d, p) for p, d in pairs])

    def lend(kv, after):
        columns = kv.shape[1]
        corners = call(functools.partial(lend_corners_kernel, plan), "lend_corners", [table, sends], [kv],
                       [bf16(2 * BT, columns)] * sides, after)
        corners = [permute(x, pairs) for x, pairs in zip(corners, plan.side_pairs)]
        lent = call(functools.partial(lend_edges_kernel, plan), "lend_edges", [table, sends], [kv, *corners],
                    [bf16(count * BT, columns) for count in plan.shapes])
        return [permute(x, pairs) for x, pairs in zip(lent, plan.side_pairs + plan.rise_pairs)]

    def attend(kv, qg, arrived, bias, after):
        return call(
            functools.partial(attend_kernel, plan, heads), "attend", [table, near, turns],
            [qg, kv, bias, *arrived],
            [bf16(tokens_dom, width), jax.ShapeDtypeStruct((tokens_dom, 2 * width), jnp.float32)]
            + [bf16(count * BT, 2 * width) for count in plan.shapes], after,
            scratch_shapes=[
                pltpu.VMEM((plan.slots * BT, 2 * width), jnp.bfloat16),
                pltpu.VMEM((plan.slots * BT, 2 * width), jnp.float32),
                pltpu.VMEM((2, WINK, 2 * width), jnp.bfloat16),
                pltpu.VMEM((2, 2, WINK, width), jnp.float32),
                pltpu.VMEM((2, WINK, width), jnp.bfloat16),
                pltpu.VMEM((2, WINK, width), jnp.bfloat16),
            ],
            cost_estimate=pl.CostEstimate(flops=5 * 2 * tokens_dom * WINK * width,
                                          bytes_accessed=8 * tokens_dom * width,
                                          transcendentals=tokens_dom * WINK * heads),
        )

    def settle(grad_q, own, *rest):
        leaving, after = rest[:-1], rest[-1]
        rises = [permute_back(x, pairs) for x, pairs in zip(leaving[sides:], plan.rise_pairs)]
        edges = [permute_back(x, pairs) for x, pairs in zip(leaving[:sides], plan.side_pairs)]
        corners = call(functools.partial(forward_kernel, plan), "forward", [], rises, [bf16(2 * BT, 2 * width)] * sides)
        corners = [permute_back(x, pairs) for x, pairs in zip(corners, plan.side_pairs)]
        return call(functools.partial(settle_kernel, plan), "settle", [table, sends],
                    [grad_q, own, *edges, *rises, *corners], [bf16(tokens_dom, 3 * width)],
                    after, scratch_shapes=[pltpu.VMEM((tokens_dom, 2 * width), jnp.float32)])[0]

    bias = [jnp.transpose(x, (2, 0, 1)).reshape(WINK, heads * BT)
            for x in jnp.split(pos_bias, chunks, axis=0)]
    kv, qg, arrived, settled, grads = [], [], [], [], []
    chain = []
    for chunk in range(chunks):
        packed_kv = pack(keys_in, values_in, [chunk], chain)
        kv.append(swap(packed_kv).reshape(tokens_dom, 2 * width))
        chain = [kv[-1]] + (bias if chunk == 0 else [])
        if chunk > 0:
            attended = attend(kv[-2], qg[-1], arrived[-1], bias[chunk - 1], [packed_kv] + settled[-1:])
            chain = [*chain, attended[0]]
        packed_qg = pack(queries, grad_out, [chunk], chain)
        qg.append(swap(packed_qg).reshape(tokens_dom, 2 * width))
        arrived.append(lend(kv[-1], [packed_qg]))
        if chunk > 0:
            settled.append(settle(*attended, qg[-1:]))
            grads.append(swap(settled[-1].reshape(holders, tokens, 3 * width)))
        chain = qg[-1:] + arrived[-1]
    attended = attend(kv[-1], qg[-1], arrived[-1], bias[-1], settled[-1:])
    settled.append(settle(*attended, ()))
    grads.append(swap(settled[-1].reshape(holders, tokens, 3 * width)))
    return call(functools.partial(unpack_kernel, chunks), "unpack", [], grads,
                [bf16(tokens, holders * chunks * width)] * 3)


def solution(mesh):
    plan = Plan(mesh.shape["dom"])
    tokens = P(("dom", "head"), None)
    return jax.shard_map(
        functools.partial(per_device, plan),
        mesh=mesh,
        in_specs=(
            tokens,
            tokens,
            tokens,
            tokens,
            P("head", None, None),
            P("dom", None),
            P("dom", None, None),
            P("dom", None),
        ),
        out_specs=(tokens, tokens, tokens),
        check_vma=False,
    )
```

```python
import functools

import jax
import jax.numpy as jnp
import numpy as np
from jax import lax
from jax.experimental import pallas as pl
from jax.experimental.pallas import tpu as pltpu
from jax.sharding import PartitionSpec as P

HD = 64
PATCH = 8
BT = 64
GRID_ROWS = 4
DIRS = 8
WIN = 9
WINK = 576
QB_DOM = 9
CAP = 3
SLAB = 32
VMEM_LIMIT = 48 * 1024 * 1024

OFFSET_LIST = [(-1, -1), (-1, 0), (-1, 1), (0, -1), (0, 1), (1, -1), (1, 0), (1, 1)]


class Plan:
    def __init__(self, domains):
        cols = domains // GRID_ROWS
        cells = [divmod(d, cols) for d in range(domains)]
        steps = [(-1, 1)] if cols == 2 else [(-1,), (1,)] if cols > 2 else []
        self.side_pairs = [[(d + step, d) for step in side for d, (_, col) in enumerate(cells)
                            if 0 <= col + step < cols] for side in steps]
        self.rise_pairs = [[(d + step * cols, d) for d, (row, _) in enumerate(cells)
                            if 0 <= row + step < GRID_ROWS] for step in (-1, 1)]
        sides = len(steps)
        self.sides = sides
        self.rise_blocks = CAP + sides
        self.borrowed = sides * CAP + 2 * self.rise_blocks
        self.slots = QB_DOM + self.borrowed
        self.shapes = [CAP] * sides + [self.rise_blocks] * 2
        self.starts = [QB_DOM + sum(self.shapes[:i]) for i in range(len(self.shapes))]
        slot_total = QB_DOM + DIRS * CAP
        self.dir_at = slot_total
        self.lend_at = slot_total + self.borrowed
        table = np.zeros((domains, self.lend_at + 3 * sides), np.int32)
        for d, (_, col) in enumerate(cells):
            table[d, :QB_DOM] = np.arange(QB_DOM)

            def borrow(k, place, count):
                for c in range(CAP):
                    table[d, QB_DOM + k * CAP + c] = place + c % count
                table[d, self.dir_at + place - QB_DOM:self.dir_at + place - QB_DOM + count] = k

            for v, row_step in enumerate((-1, 1)):
                borrow(OFFSET_LIST.index((row_step, 0)), self.starts[sides + v], CAP)
            for i, side in enumerate(steps):
                for step in side:
                    if 0 <= col + step < cols:
                        borrow(OFFSET_LIST.index((0, step)), self.starts[i], CAP)
                        for v, row_step in enumerate((-1, 1)):
                            borrow(OFFSET_LIST.index((row_step, step)), self.starts[sides + v] + CAP + i, 1)
                    if 0 <= col - step < cols:
                        for n, row_step in enumerate((0, -1, 1)):
                            table[d, self.lend_at + 3 * i + n] = OFFSET_LIST.index((row_step, step))
        self.table = table

    def side_edge(self, i, c, table_ref, send_ref):
        return send_ref[table_ref[self.lend_at + 3 * i] * CAP + c]

    def side_corner(self, i, v, table_ref, send_ref):
        k = table_ref[self.lend_at + 3 * i + 1 + v]
        found = send_ref[k * CAP]
        for other in range(1, CAP):
            found = jnp.maximum(found, send_ref[k * CAP + other])
        return found

    def rise_edge(self, v, c, send_ref):
        return send_ref[OFFSET_LIST.index((2 * v - 1, 0)) * CAP + c]


def rows_of(c):
    return slice(c * BT, (c + 1) * BT)


def block_rows(index):
    return pl.ds(pl.multiple_of(index * BT, BT), BT)


def turn_matrix(orient, back):
    token = lax.broadcasted_iota(jnp.int32, (BT, BT), 1 if back else 0)
    place = lax.broadcasted_iota(jnp.int32, (BT, BT), 0 if back else 1)
    row, col = token >> 3, token & (PATCH - 1)
    row = jnp.where((orient & 1) == 1, PATCH - 1 - row, row)
    col = jnp.where(((orient >> 1) & 1) == 1, PATCH - 1 - col, col)
    mapped = jnp.where(orient >= 4, PATCH * col + row, PATCH * row + col)
    return (mapped == place).astype(jnp.float32).astype(jnp.bfloat16)


def pack_kernel(chunks, picked, left_ref, right_ref, out_ref, *sems):
    holders = out_ref.shape[0]
    width = left_ref.shape[1] // (holders * chunks)
    copies = []
    for s in range(holders):
        for n, chunk in enumerate(picked):
            at, to = (s * chunks + chunk) * width, 2 * n * width
            for ref, to in ((left_ref, 2 * n * width), (right_ref, (2 * n + 1) * width)):
                if sems:
                    copies.append(pltpu.make_async_copy(ref.at[:, at:at + width], out_ref.at[s, :, to:to + width],
                                                        sems[0].at[len(copies)]))
                    copies[-1].start()
                else:
                    out_ref[s, :, to:to + width] = ref[:, at:at + width]
    for copy in copies:
        copy.wait()


def unpack_kernel(chunks, *refs):
    outs = refs[chunks:]
    holders, _, all_width = refs[0].shape
    width = all_width // len(outs)
    for chunk in range(chunks):
        for s in range(holders):
            at = (s * chunks + chunk) * width
            for which, out_ref in enumerate(outs):
                out_ref[:, at:at + width] = refs[chunk][s, :, which * width:(which + 1) * width]


def lend_corners_kernel(plan, table_ref, send_ref, kv_ref, *out_refs):
    for i in range(plan.sides):
        for v in range(2):
            block = plan.side_corner(i, v, table_ref, send_ref)
            out_refs[i][rows_of(v), :] = kv_ref[block_rows(block), :]


def lend_edges_kernel(plan, table_ref, send_ref, kv_ref, *refs):
    corners, out_refs = refs[:plan.sides], refs[plan.sides:]
    for v in range(2):
        out_ref = out_refs[plan.sides + v]
        for c in range(CAP):
            out_ref[rows_of(c), :] = kv_ref[block_rows(plan.rise_edge(v, c, send_ref)), :]
        for i in range(plan.sides):
            out_ref[rows_of(CAP + i), :] = corners[i][rows_of(v), :]
    for i in range(plan.sides):
        for c in range(CAP):
            out_refs[i][rows_of(c), :] = kv_ref[block_rows(plan.side_edge(i, c, table_ref, send_ref)), :]


def forward_kernel(plan, *refs):
    for i in range(plan.sides):
        for v in range(2):
            refs[2 + i][rows_of(v), :] = refs[v][rows_of(CAP + i), :]


def settle_kernel(plan, table_ref, send_ref, grad_q_ref, own_ref, *refs):
    out_ref, total = refs[-2:]
    sides, rises, corners = refs[:plan.sides], refs[plan.sides:plan.sides + 2], refs[plan.sides + 2:-2]
    width = grad_q_ref.shape[1]
    out_ref[:, :width] = grad_q_ref[...]
    total[...] = own_ref[...]

    def add(block, ref, c):
        total[block_rows(block), :] += ref[rows_of(c), :].astype(jnp.float32)

    for i in range(plan.sides):
        for c in range(CAP):
            add(plan.side_edge(i, c, table_ref, send_ref), sides[i], c)
        for v in range(2):
            add(plan.side_corner(i, v, table_ref, send_ref), corners[i], v)
    for v in range(2):
        for c in range(CAP):
            add(plan.rise_edge(v, c, send_ref), rises[v], c)
    out_ref[:, width:] = total[...].astype(jnp.bfloat16)


def dot(a, b, contract):
    return lax.dot_general(a, b, ((contract[:1], contract[1:]), ((), ())),
                           preferred_element_type=jnp.float32)


def attend_kernel(plan, heads, table_ref, near_ref, orient_ref, qg_ref, kv_ref, bias_ref, *refs):
    groups = len(plan.shapes)
    arrived = refs[:groups]
    dq_ref, own_ref, *leaving = refs[-9 - groups:-7]
    ext, acc, win, wide, work, probs_ref, dscores_ref = refs[-7:]
    width = heads * HD
    scale = HD ** -0.5
    keys, values = slice(0, width), slice(width, 2 * width)
    slabs = [slice(at, at + SLAB) for at in range(0, WINK, SLAB)]

    def turned(i, c, back):
        return turn_matrix(orient_ref[table_ref[plan.dir_at + plan.starts[i] - QB_DOM + c]], back)

    ext[:QB_DOM * BT, :] = kv_ref[...]
    for i, count in enumerate(plan.shapes):
        for c in range(count):
            if c == 0 or c >= CAP:
                turn = turned(i, c, False)
            ext[rows_of(plan.starts[i] + c), :] = dot(turn, arrived[i][rows_of(c), :], (1, 0)).astype(jnp.bfloat16)
    acc[...] = jnp.zeros_like(acc)

    same_head = (lax.broadcasted_iota(jnp.int32, (width, width), 0) // HD
                 == lax.broadcasted_iota(jnp.int32, (width, width), 1) // HD)

    def spread(block):
        copies = jnp.concatenate([block] * heads, axis=0)
        return jnp.where(same_head, copies, jnp.zeros_like(copies))

    def products(b, even):
        places = [table_ref[near_ref[b * WIN + j]] for j in range(WIN)]
        for j in range(WIN):
            win[even, rows_of(j), :] = ext[block_rows(places[j]), :]
        block = qg_ref[block_rows(b), :]
        wide[even, 0] = spread(block[:, keys] * jnp.bfloat16(scale))
        wide[even, 1] = spread(block[:, values])
        work[even, 0] = dot(win[even, :, keys], wide[even, 0], (1, 1)) + bias_ref[...]
        work[even, 1] = dot(win[even, :, values], wide[even, 1], (1, 1))

    def softmax(even):
        top = work[even, 0, slabs[0], :]
        for slab in slabs[1:]:
            top = jnp.maximum(top, work[even, 0, slab, :])
        top = jnp.max(top, axis=0, keepdims=True)
        total = jnp.zeros((SLAB, width), jnp.float32)
        delta = jnp.zeros((SLAB, width), jnp.float32)
        for slab in slabs:
            weight = jnp.exp(work[even, 0, slab, :] - top)
            work[even, 0, slab, :] = weight
            total = total + weight
            delta = delta + weight * work[even, 1, slab, :]
        inverse = 1.0 / jnp.sum(total, axis=0, keepdims=True)
        delta = jnp.sum(delta, axis=0, keepdims=True) * inverse
        for slab in slabs:
            probs = work[even, 0, slab, :] * inverse
            probs_ref[even, slab, :] = probs.astype(jnp.bfloat16)
            dscores_ref[even, slab, :] = (probs * (work[even, 1, slab, :] - delta)).astype(jnp.bfloat16)

    def gradients(b, even):
        places = [table_ref[near_ref[b * WIN + j]] for j in range(WIN)]
        dscores = dscores_ref[even]
        grad_q = dot(dscores, win[even, :, keys], (0, 0))
        grad_q = jnp.where(same_head, grad_q, 0.0)
        total_q = grad_q[:BT]
        for h in range(1, heads):
            total_q = total_q + grad_q[rows_of(h)]
        dq_ref[block_rows(b), :] = (total_q * scale).astype(jnp.bfloat16)
        grad_k = dot(dscores, wide[even, 0], (1, 0))
        grad_v = dot(probs_ref[even], wide[even, 1], (1, 0))
        for j in range(WIN):
            acc[block_rows(places[j]), keys] += grad_k[rows_of(j)]
            acc[block_rows(places[j]), values] += grad_v[rows_of(j)]

    def two_blocks(pair, carry):
        for even in range(2):
            products(2 * pair + even + 1, 1 - even)
            softmax(even)
            gradients(2 * pair + even, even)
        return carry

    products(0, 0)
    lax.fori_loop(0, QB_DOM // 2, two_blocks, 0)
    softmax(0)
    gradients(QB_DOM - 1, 0)

    own_ref[...] = acc[:QB_DOM * BT, :]
    for i, count in enumerate(plan.shapes):
        for c in range(count):
            if c == 0 or c >= CAP:
                turn = turned(i, c, True)
            slot = acc[rows_of(plan.starts[i] + c), :].astype(jnp.bfloat16)
            leaving[i][rows_of(c), :] = dot(turn, slot, (1, 0)).astype(jnp.bfloat16)


def smem_specs(count):
    return [pl.BlockSpec(memory_space=pltpu.SMEM)] * count


def vmem_specs(count):
    return [pl.BlockSpec(memory_space=pltpu.VMEM)] * count


def params():
    return pltpu.CompilerParams(vmem_limit_bytes=VMEM_LIMIT)


def bf16(*shape):
    return jax.ShapeDtypeStruct(shape, jnp.bfloat16)


def any_specs(count):
    return [pl.BlockSpec(memory_space=pl.ANY)] * count


def call(kernel, name, scalars, arrays, outs, after=(), in_place=False, **more):
    after = [x[tuple(slice(0, n) for n in (1,) * (x.ndim - 2) + (16, 128))] for x in after]
    taken = len(scalars) + len(arrays)

    def body(*refs):
        kernel(*refs[:taken], *refs[taken + len(after):])

    return pl.pallas_call(
        body,
        out_shape=outs,
        in_specs=smem_specs(len(scalars)) + (any_specs if in_place else vmem_specs)(len(arrays)) + any_specs(len(after)),
        out_specs=vmem_specs(len(outs)),
        compiler_params=params(),
        name=name,
        **more,
    )(*scalars, *arrays, *after)


def per_device(plan, queries, keys_in, values_in, grad_out, pos_bias, neighbours, send_block, orient):
    chunks = 2 if pos_bias.shape[0] % 2 == 0 else 1
    heads = pos_bias.shape[0] // chunks
    width = heads * HD
    tokens = queries.shape[0]
    holders = lax.axis_size("head")
    tokens_dom = tokens * holders
    sides = plan.sides
    table = lax.dynamic_index_in_dim(jnp.asarray(plan.table), lax.axis_index("dom"), 0, False)
    near, sends, turns = neighbours.reshape(-1), send_block.reshape(-1), orient.reshape(-1)

    def swap(matrix):
        return lax.all_to_all(matrix, "head", split_axis=0, concat_axis=0, tiled=True)

    def pack(left, right, picked, after):
        more = {}
        if width % 128 == 0:
            more = dict(in_place=True, scratch_shapes=[pltpu.SemaphoreType.DMA((2 * holders * len(picked),))])
        return call(functools.partial(pack_kernel, chunks, picked), "pack", [], [left, right],
                    [bf16(holders, tokens, 2 * len(picked) * width)], after, **more)[0]

    def permute(value, pairs):
        return lax.ppermute(value, "dom", pairs)

    def permute_back(value, pairs):
        return lax.ppermute(value, "dom", [(d, p) for p, d in pairs])

    def lend(kv, after):
        columns = kv.shape[1]
        corners = call(functools.partial(lend_corners_kernel, plan), "lend_corners", [table, sends], [kv],
                       [bf16(2 * BT, columns)] * sides, after)
        corners = [permute(x, pairs) for x, pairs in zip(corners, plan.side_pairs)]
        lent = call(functools.partial(lend_edges_kernel, plan), "lend_edges", [table, sends], [kv, *corners],
                    [bf16(count * BT, columns) for count in plan.shapes])
        return lent, [permute(x, pairs) for x, pairs in zip(lent, plan.side_pairs + plan.rise_pairs)]

    def attend(kv, qg, arrived, bias, after):
        return call(
            functools.partial(attend_kernel, plan, heads), "attend", [table, near, turns],
            [qg, kv, bias, *arrived],
            [bf16(tokens_dom, width), jax.ShapeDtypeStruct((tokens_dom, 2 * width), jnp.float32)]
            + [bf16(count * BT, 2 * width) for count in plan.shapes], after,
            scratch_shapes=[
                pltpu.VMEM((plan.slots * BT, 2 * width), jnp.bfloat16),
                pltpu.VMEM((plan.slots * BT, 2 * width), jnp.float32),
                pltpu.VMEM((2, WINK, 2 * width), jnp.bfloat16),
                pltpu.VMEM((2, 2, width, width), jnp.bfloat16),
                pltpu.VMEM((2, 2, WINK, width), jnp.float32),
                pltpu.VMEM((2, WINK, width), jnp.bfloat16),
                pltpu.VMEM((2, WINK, width), jnp.bfloat16),
            ],
            cost_estimate=pl.CostEstimate(flops=5 * 2 * tokens_dom * WINK * width,
                                          bytes_accessed=8 * tokens_dom * width,
                                          transcendentals=tokens_dom * WINK * heads),
        )

    def settle(grad_q, own, *rest):
        leaving, after = rest[:-1], rest[-1]
        rises = [permute_back(x, pairs) for x, pairs in zip(leaving[sides:], plan.rise_pairs)]
        edges = [permute_back(x, pairs) for x, pairs in zip(leaving[:sides], plan.side_pairs)]
        corners = call(functools.partial(forward_kernel, plan), "forward", [], rises, [bf16(2 * BT, 2 * width)] * sides)
        corners = [permute_back(x, pairs) for x, pairs in zip(corners, plan.side_pairs)]
        return call(functools.partial(settle_kernel, plan), "settle", [table, sends],
                    [grad_q, own, *edges, *rises, *corners], [bf16(tokens_dom, 3 * width)],
                    after, scratch_shapes=[pltpu.VMEM((tokens_dom, 2 * width), jnp.float32)])[0]

    bias = [jnp.transpose(x, (2, 0, 1)).reshape(WINK, heads * BT)
            for x in jnp.split(pos_bias, chunks, axis=0)]
    kv, qg, arrived, settled, grads = [], [], [], [], []
    chain = []
    for chunk in range(chunks):
        packed_kv = pack(keys_in, values_in, [chunk], chain)
        kv.append(swap(packed_kv).reshape(tokens_dom, 2 * width))
        chain = [kv[-1]] + (bias if chunk == 0 else [])
        if chunk > 0:
            attended = attend(kv[-2], qg[-1], arrived[-1], bias[chunk - 1], [packed_kv] + settled[-1:])
            chain = [*chain, attended[0]]
        packed_qg = pack(queries, grad_out, [chunk], chain)
        qg.append(swap(packed_qg).reshape(tokens_dom, 2 * width))
        lent, borrowed = lend(kv[-1], [packed_qg])
        arrived.append(borrowed)
        chain = [qg[-1], lent[-1]]
        if chunk > 0:
            settled.append(settle(*attended, chain))
            grads.append(swap(settled[-1].reshape(holders, tokens, 3 * width)))
    attended = attend(kv[-1], qg[-1], arrived[-1], bias[-1], settled[-1:])
    settled.append(settle(*attended, ()))
    grads.append(swap(settled[-1].reshape(holders, tokens, 3 * width)))
    return call(functools.partial(unpack_kernel, chunks), "unpack", [], grads,
                [bf16(tokens, holders * chunks * width)] * 3)


def solution(mesh):
    plan = Plan(mesh.shape["dom"])
    tokens = P(("dom", "head"), None)
    return jax.shard_map(
        functools.partial(per_device, plan),
        mesh=mesh,
        in_specs=(
            tokens,
            tokens,
            tokens,
            tokens,
            P("head", None, None),
            P("dom", None),
            P("dom", None, None),
            P("dom", None),
        ),
        out_specs=(tokens, tokens, tokens),
        check_vma=False,
    )
```

```python
import functools

import jax
import jax.numpy as jnp
import numpy as np
from jax import lax
from jax.experimental import pallas as pl
from jax.experimental.pallas import tpu as pltpu
from jax.sharding import PartitionSpec as P

HD = 64
PATCH = 8
BT = 64
GRID_ROWS = 4
DIRS = 8
WIN = 9
WINK = 576
QB_DOM = 9
CAP = 3
SLAB = 32
VMEM_LIMIT = 48 * 1024 * 1024

OFFSET_LIST = [(-1, -1), (-1, 0), (-1, 1), (0, -1), (0, 1), (1, -1), (1, 0), (1, 1)]


class Plan:
    def __init__(self, domains):
        cols = domains // GRID_ROWS
        cells = [divmod(d, cols) for d in range(domains)]
        steps = [(-1, 1)] if cols == 2 else [(-1,), (1,)] if cols > 2 else []
        self.side_pairs = [[(d + step, d) for step in side for d, (_, col) in enumerate(cells)
                            if 0 <= col + step < cols] for side in steps]
        self.rise_pairs = [[(d + step * cols, d) for d, (row, _) in enumerate(cells)
                            if 0 <= row + step < GRID_ROWS] for step in (-1, 1)]
        sides = len(steps)
        self.sides = sides
        self.rise_blocks = CAP + sides
        self.borrowed = sides * CAP + 2 * self.rise_blocks
        self.slots = QB_DOM + self.borrowed
        self.shapes = [CAP] * sides + [self.rise_blocks] * 2
        self.starts = [QB_DOM + sum(self.shapes[:i]) for i in range(len(self.shapes))]
        slot_total = QB_DOM + DIRS * CAP
        self.dir_at = slot_total
        self.lend_at = slot_total + self.borrowed
        table = np.zeros((domains, self.lend_at + 3 * sides), np.int32)
        for d, (_, col) in enumerate(cells):
            table[d, :QB_DOM] = np.arange(QB_DOM)

            def borrow(k, place, count):
                for c in range(CAP):
                    table[d, QB_DOM + k * CAP + c] = place + c % count
                table[d, self.dir_at + place - QB_DOM:self.dir_at + place - QB_DOM + count] = k

            for v, row_step in enumerate((-1, 1)):
                borrow(OFFSET_LIST.index((row_step, 0)), self.starts[sides + v], CAP)
            for i, side in enumerate(steps):
                for step in side:
                    if 0 <= col + step < cols:
                        borrow(OFFSET_LIST.index((0, step)), self.starts[i], CAP)
                        for v, row_step in enumerate((-1, 1)):
                            borrow(OFFSET_LIST.index((row_step, step)), self.starts[sides + v] + CAP + i, 1)
                    if 0 <= col - step < cols:
                        for n, row_step in enumerate((0, -1, 1)):
                            table[d, self.lend_at + 3 * i + n] = OFFSET_LIST.index((row_step, step))
        self.table = table

    def side_edge(self, i, c, table_ref, send_ref):
        return send_ref[table_ref[self.lend_at + 3 * i] * CAP + c]

    def side_corner(self, i, v, table_ref, send_ref):
        k = table_ref[self.lend_at + 3 * i + 1 + v]
        found = send_ref[k * CAP]
        for other in range(1, CAP):
            found = jnp.maximum(found, send_ref[k * CAP + other])
        return found

    def rise_edge(self, v, c, send_ref):
        return send_ref[OFFSET_LIST.index((2 * v - 1, 0)) * CAP + c]


def rows_of(c):
    return slice(c * BT, (c + 1) * BT)


def block_rows(index):
    return pl.ds(pl.multiple_of(index * BT, BT), BT)


def turn_matrix(orient, back):
    token = lax.broadcasted_iota(jnp.int32, (BT, BT), 1 if back else 0)
    place = lax.broadcasted_iota(jnp.int32, (BT, BT), 0 if back else 1)
    row, col = token >> 3, token & (PATCH - 1)
    row = jnp.where((orient & 1) == 1, PATCH - 1 - row, row)
    col = jnp.where(((orient >> 1) & 1) == 1, PATCH - 1 - col, col)
    mapped = jnp.where(orient >= 4, PATCH * col + row, PATCH * row + col)
    return (mapped == place).astype(jnp.float32).astype(jnp.bfloat16)


def pack_kernel(chunks, picked, left_ref, right_ref, out_ref, *sems):
    holders = out_ref.shape[0]
    width = left_ref.shape[1] // (holders * chunks)
    copies = []
    for s in range(holders):
        for n, chunk in enumerate(picked):
            at, to = (s * chunks + chunk) * width, 2 * n * width
            for ref, to in ((left_ref, 2 * n * width), (right_ref, (2 * n + 1) * width)):
                if sems:
                    copies.append(pltpu.make_async_copy(ref.at[:, at:at + width], out_ref.at[s, :, to:to + width],
                                                        sems[0].at[len(copies)]))
                    copies[-1].start()
                else:
                    out_ref[s, :, to:to + width] = ref[:, at:at + width]
    for copy in copies:
        copy.wait()


def unpack_kernel(chunks, width, sources, *refs):
    outs = refs[-3:]
    for which, out_ref in enumerate(outs):
        for chunk in range(chunks):
            index, lane = sources[which, chunk]
            for s in range(refs[index].shape[0]):
                at = (s * chunks + chunk) * width
                out_ref[:, at:at + width] = refs[index][s, :, lane:lane + width]


def lend_corners_kernel(plan, table_ref, send_ref, kv_ref, *out_refs):
    for i in range(plan.sides):
        for v in range(2):
            block = plan.side_corner(i, v, table_ref, send_ref)
            out_refs[i][rows_of(v), :] = kv_ref[block_rows(block), :]


def lend_edges_kernel(plan, table_ref, send_ref, kv_ref, *refs):
    corners, out_refs = refs[:plan.sides], refs[plan.sides:]
    for v in range(2):
        out_ref = out_refs[plan.sides + v]
        for c in range(CAP):
            out_ref[rows_of(c), :] = kv_ref[block_rows(plan.rise_edge(v, c, send_ref)), :]
        for i in range(plan.sides):
            out_ref[rows_of(CAP + i), :] = corners[i][rows_of(v), :]
    for i in range(plan.sides):
        for c in range(CAP):
            out_refs[i][rows_of(c), :] = kv_ref[block_rows(plan.side_edge(i, c, table_ref, send_ref)), :]


def forward_kernel(plan, *refs):
    for i in range(plan.sides):
        for v in range(2):
            refs[2 + i][rows_of(v), :] = refs[v][rows_of(CAP + i), :]


def settle_kernel(plan, table_ref, send_ref, own_ref, *refs):
    out_ref, total = refs[-2:]
    sides, rises = refs[:plan.sides], refs[plan.sides:plan.sides + 2]
    corners, beside = refs[plan.sides + 2:2 * plan.sides + 2], refs[2 * plan.sides + 2:-2]
    pair_width = own_ref.shape[1]
    for grad_q_ref in beside:
        out_ref[:, pair_width:] = grad_q_ref[...]
    total[...] = own_ref[...]

    def add(block, ref, c):
        total[block_rows(block), :] += ref[rows_of(c), :].astype(jnp.float32)

    for i in range(plan.sides):
        for c in range(CAP):
            add(plan.side_edge(i, c, table_ref, send_ref), sides[i], c)
        for v in range(2):
            add(plan.side_corner(i, v, table_ref, send_ref), corners[i], v)
    for v in range(2):
        for c in range(CAP):
            add(plan.rise_edge(v, c, send_ref), rises[v], c)
    out_ref[:, :pair_width] = total[...].astype(jnp.bfloat16)


def dot(a, b, contract):
    return lax.dot_general(a, b, ((contract[:1], contract[1:]), ((), ())),
                           preferred_element_type=jnp.float32)


def attend_kernel(plan, heads, chunk, table_ref, near_ref, orient_ref, qg_ref, kv_ref, bias_ref, *refs):
    groups = len(plan.shapes)
    arrived = refs[:groups]
    dq_ref, own_ref, *leaving = refs[-9 - groups:-7]
    ext, acc, win, wide, work, probs_ref, dscores_ref = refs[-7:]
    width = heads * HD
    scale = HD ** -0.5
    keys, values = slice(0, width), slice(width, 2 * width)
    mine = slice(2 * chunk * width, 2 * (chunk + 1) * width)
    slabs = [slice(at, at + SLAB) for at in range(0, WINK, SLAB)]

    def turned(i, c, back):
        return turn_matrix(orient_ref[table_ref[plan.dir_at + plan.starts[i] - QB_DOM + c]], back)

    ext[:QB_DOM * BT, :] = kv_ref[:, mine]
    for i, count in enumerate(plan.shapes):
        for c in range(count):
            if c == 0 or c >= CAP:
                turn = turned(i, c, False)
            ext[rows_of(plan.starts[i] + c), :] = dot(turn, arrived[i][rows_of(c), mine], (1, 0)).astype(jnp.bfloat16)
    acc[...] = jnp.zeros_like(acc)

    same_head = (lax.broadcasted_iota(jnp.int32, (width, width), 0) // HD
                 == lax.broadcasted_iota(jnp.int32, (width, width), 1) // HD)

    def spread(block):
        copies = jnp.concatenate([block] * heads, axis=0)
        return jnp.where(same_head, copies, jnp.zeros_like(copies))

    def products(b, even):
        places = [table_ref[near_ref[b * WIN + j]] for j in range(WIN)]
        for j in range(WIN):
            win[even, rows_of(j), :] = ext[block_rows(places[j]), :]
        block = qg_ref[block_rows(b), :]
        wide[even, 0] = spread(block[:, keys] * jnp.bfloat16(scale))
        wide[even, 1] = spread(block[:, values])
        work[even, 0] = dot(win[even, :, keys], wide[even, 0], (1, 1)) + bias_ref[...]
        work[even, 1] = dot(win[even, :, values], wide[even, 1], (1, 1))

    def softmax(even):
        top = work[even, 0, slabs[0], :]
        for slab in slabs[1:]:
            top = jnp.maximum(top, work[even, 0, slab, :])
        top = jnp.max(top, axis=0, keepdims=True)
        total = jnp.zeros((SLAB, width), jnp.float32)
        delta = jnp.zeros((SLAB, width), jnp.float32)
        for slab in slabs:
            weight = jnp.exp(work[even, 0, slab, :] - top)
            work[even, 0, slab, :] = weight
            total = total + weight
            delta = delta + weight * work[even, 1, slab, :]
        inverse = 1.0 / jnp.sum(total, axis=0, keepdims=True)
        delta = jnp.sum(delta, axis=0, keepdims=True) * inverse
        for slab in slabs:
            probs = work[even, 0, slab, :] * inverse
            probs_ref[even, slab, :] = probs.astype(jnp.bfloat16)
            dscores_ref[even, slab, :] = (probs * (work[even, 1, slab, :] - delta)).astype(jnp.bfloat16)

    def gradients(b, even):
        places = [table_ref[near_ref[b * WIN + j]] for j in range(WIN)]
        dscores = dscores_ref[even]
        grad_q = dot(dscores, win[even, :, keys], (0, 0))
        grad_q = jnp.where(same_head, grad_q, 0.0)
        total_q = grad_q[:BT]
        for h in range(1, heads):
            total_q = total_q + grad_q[rows_of(h)]
        dq_ref[block_rows(b), :] = (total_q * scale).astype(jnp.bfloat16)
        grad_k = dot(dscores, wide[even, 0], (1, 0))
        grad_v = dot(probs_ref[even], wide[even, 1], (1, 0))
        for j in range(WIN):
            acc[block_rows(places[j]), keys] += grad_k[rows_of(j)]
            acc[block_rows(places[j]), values] += grad_v[rows_of(j)]

    def two_blocks(pair, carry):
        for even in range(2):
            products(2 * pair + even + 1, 1 - even)
            softmax(even)
            gradients(2 * pair + even, even)
        return carry

    products(0, 0)
    lax.fori_loop(0, QB_DOM // 2, two_blocks, 0)
    softmax(0)
    gradients(QB_DOM - 1, 0)

    own_ref[...] = acc[:QB_DOM * BT, :]
    for i, count in enumerate(plan.shapes):
        for c in range(count):
            if c == 0 or c >= CAP:
                turn = turned(i, c, True)
            slot = acc[rows_of(plan.starts[i] + c), :].astype(jnp.bfloat16)
            leaving[i][rows_of(c), :] = dot(turn, slot, (1, 0)).astype(jnp.bfloat16)


def smem_specs(count):
    return [pl.BlockSpec(memory_space=pltpu.SMEM)] * count


def vmem_specs(count):
    return [pl.BlockSpec(memory_space=pltpu.VMEM)] * count


def params():
    return pltpu.CompilerParams(vmem_limit_bytes=VMEM_LIMIT)


def bf16(*shape):
    return jax.ShapeDtypeStruct(shape, jnp.bfloat16)


def any_specs(count):
    return [pl.BlockSpec(memory_space=pl.ANY)] * count


def busy(microseconds):
    return pl.CostEstimate(flops=int(microseconds * 1.15e9), bytes_accessed=0, transcendentals=0)


def call(kernel, name, scalars, arrays, outs, after=(), in_place=False, takes=1.0, **more):
    after = [x[tuple(slice(0, n) for n in (1,) * (x.ndim - 2) + (16, 128))] for x in after]
    taken = len(scalars) + len(arrays)

    def body(*refs):
        kernel(*refs[:taken], *refs[taken + len(after):])

    return pl.pallas_call(
        body,
        out_shape=outs,
        in_specs=smem_specs(len(scalars)) + (any_specs if in_place else vmem_specs)(len(arrays)) + any_specs(len(after)),
        out_specs=vmem_specs(len(outs)),
        compiler_params=params(),
        cost_estimate=busy(takes),
        name=name,
        **more,
    )(*scalars, *arrays, *after)


def per_device(plan, queries, keys_in, values_in, grad_out, pos_bias, neighbours, send_block, orient):
    chunks = 2 if pos_bias.shape[0] % 2 == 0 else 1
    heads = pos_bias.shape[0] // chunks
    width = heads * HD
    tokens = queries.shape[0]
    holders = lax.axis_size("head")
    tokens_dom = tokens * holders
    sides = plan.sides
    table = lax.dynamic_index_in_dim(jnp.asarray(plan.table), lax.axis_index("dom"), 0, False)
    near, sends, turns = neighbours.reshape(-1), send_block.reshape(-1), orient.reshape(-1)

    def swap(matrix):
        return lax.all_to_all(matrix, "head", split_axis=0, concat_axis=0, tiled=True)

    def pack(left, right, picked, after):
        more = {}
        if width % 128 == 0:
            more = dict(in_place=True, scratch_shapes=[pltpu.SemaphoreType.DMA((2 * holders * len(picked),))])
        return call(functools.partial(pack_kernel, chunks, picked), "pack", [], [left, right],
                    [bf16(holders, tokens, 2 * len(picked) * width)], after, **more)[0]

    def permute(value, pairs):
        return lax.ppermute(value, "dom", pairs)

    def permute_back(value, pairs):
        return lax.ppermute(value, "dom", [(d, p) for p, d in pairs])

    def lend(kv, after):
        columns = kv.shape[1]
        corners = call(functools.partial(lend_corners_kernel, plan), "lend_corners", [table, sends], [kv],
                       [bf16(2 * BT, columns)] * sides, after)
        corners = [permute(x, pairs) for x, pairs in zip(corners, plan.side_pairs)]
        lent = call(functools.partial(lend_edges_kernel, plan), "lend_edges", [table, sends], [kv, *corners],
                    [bf16(count * BT, columns) for count in plan.shapes])
        return lent, [permute(x, pairs) for x, pairs in zip(lent, plan.side_pairs + plan.rise_pairs)]

    def attend(chunk, after):
        grad_q, own, *leaving = call(
            functools.partial(attend_kernel, plan, heads, chunk), "attend", [table, near, turns],
            [qg[chunk], kv, bias[chunk], *arrived],
            [bf16(tokens_dom, width), jax.ShapeDtypeStruct((tokens_dom, 2 * width), jnp.float32)]
            + [bf16(count * BT, 2 * width) for count in plan.shapes], after, takes=10.0,
            scratch_shapes=[
                pltpu.VMEM((plan.slots * BT, 2 * width), jnp.bfloat16),
                pltpu.VMEM((plan.slots * BT, 2 * width), jnp.float32),
                pltpu.VMEM((2, WINK, 2 * width), jnp.bfloat16),
                pltpu.VMEM((2, 2, width, width), jnp.bfloat16),
                pltpu.VMEM((2, 2, WINK, width), jnp.float32),
                pltpu.VMEM((2, WINK, width), jnp.bfloat16),
                pltpu.VMEM((2, WINK, width), jnp.bfloat16),
            ],
        )
        rises = [permute_back(x, pairs) for x, pairs in zip(leaving[sides:], plan.rise_pairs)]
        edges = [permute_back(x, pairs) for x, pairs in zip(leaving[:sides], plan.side_pairs)]
        corners = call(functools.partial(forward_kernel, plan), "forward", [], rises, [bf16(2 * BT, 2 * width)] * sides)
        corners = [permute_back(x, pairs) for x, pairs in zip(corners, plan.side_pairs)]
        return grad_q, [own, *edges, *rises, *corners]

    def settle(parts, beside, after):
        columns = (2 + len(beside)) * width
        return call(functools.partial(settle_kernel, plan), "settle", [table, sends], [*parts, *beside],
                    [bf16(tokens_dom, columns)], after, scratch_shapes=[pltpu.VMEM((tokens_dom, 2 * width), jnp.float32)])[0]

    def swap_back(matrix):
        return swap(matrix.reshape(holders, tokens, -1))

    bias = [jnp.transpose(x, (2, 0, 1)).reshape(WINK, heads * BT)
            for x in jnp.split(pos_bias, chunks, axis=0)]
    kv = swap(pack(keys_in, values_in, range(chunks), ())).reshape(tokens_dom, 2 * chunks * width)
    packed, qg = [], []
    for chunk in range(chunks):
        packed.append(pack(queries, grad_out, [chunk], [qg[-1], lent[-1]] if chunk else [kv, *bias]))
        qg.append(swap(packed[-1]).reshape(tokens_dom, 2 * width))
        if chunk == 0:
            lent, arrived = lend(kv, packed)
    attended = [attend(chunk, packed[chunk + 1:chunk + 2]) for chunk in range(chunks)]
    grads, sources, settled = [swap_back(attended[0][0])], {(0, 0): (0, 0)}, []
    for chunk in range(chunks):
        beside = [grad_q for grad_q, _ in attended[chunk + 1:chunk + 2]]
        settled.append(settle(attended[chunk][1], beside, settled[-1:]))
        grads.append(swap_back(settled[-1]))
        for which in range(2):
            sources[1 + which, chunk] = (1 + chunk, which * width)
        sources[0, chunk + 1] = (1 + chunk, 2 * width)
    return call(functools.partial(unpack_kernel, chunks, width, sources), "unpack", [], grads,
                [bf16(tokens, holders * chunks * width)] * 3)


def solution(mesh):
    plan = Plan(mesh.shape["dom"])
    tokens = P(("dom", "head"), None)
    return jax.shard_map(
        functools.partial(per_device, plan),
        mesh=mesh,
        in_specs=(
            tokens,
            tokens,
            tokens,
            tokens,
            P("head", None, None),
            P("dom", None),
            P("dom", None, None),
            P("dom", None),
        ),
        out_specs=(tokens, tokens, tokens),
        check_vma=False,
    )
```

```python
import functools

import jax
import jax.numpy as jnp
import numpy as np
from jax import lax
from jax.experimental import pallas as pl
from jax.experimental.pallas import tpu as pltpu
from jax.sharding import PartitionSpec as P

HD = 64
PATCH = 8
BT = 64
GRID_ROWS = 4
DIRS = 8
WIN = 9
WINK = 576
QB_DOM = 9
CAP = 3
GROUP_HEADS = 4
SLAB = 32
VMEM_LIMIT = 48 * 1024 * 1024

OFFSET_LIST = [(-1, -1), (-1, 0), (-1, 1), (0, -1), (0, 1), (1, -1), (1, 0), (1, 1)]


class Plan:
    def __init__(self, domains):
        cols = domains // GRID_ROWS
        cells = [divmod(d, cols) for d in range(domains)]
        steps = [(-1, 1)] if cols == 2 else [(-1,), (1,)] if cols > 2 else []
        self.side_pairs = [[(d + step, d) for step in side for d, (_, col) in enumerate(cells)
                            if 0 <= col + step < cols] for side in steps]
        self.rise_pairs = [[(d + step * cols, d) for d, (row, _) in enumerate(cells)
                            if 0 <= row + step < GRID_ROWS] for step in (-1, 1)]
        sides = len(steps)
        self.sides = sides
        self.rise_blocks = CAP + sides
        self.borrowed = sides * CAP + 2 * self.rise_blocks
        self.slots = QB_DOM + self.borrowed
        self.shapes = [CAP] * sides + [self.rise_blocks] * 2
        self.starts = [QB_DOM + sum(self.shapes[:i]) for i in range(len(self.shapes))]
        slot_total = QB_DOM + DIRS * CAP
        self.dir_at = slot_total
        self.lend_at = slot_total + self.borrowed
        table = np.zeros((domains, self.lend_at + 3 * sides), np.int32)
        for d, (_, col) in enumerate(cells):
            table[d, :QB_DOM] = np.arange(QB_DOM)

            def borrow(k, place, count):
                for c in range(CAP):
                    table[d, QB_DOM + k * CAP + c] = place + c % count
                table[d, self.dir_at + place - QB_DOM:self.dir_at + place - QB_DOM + count] = k

            for v, row_step in enumerate((-1, 1)):
                borrow(OFFSET_LIST.index((row_step, 0)), self.starts[sides + v], CAP)
            for i, side in enumerate(steps):
                for step in side:
                    if 0 <= col + step < cols:
                        borrow(OFFSET_LIST.index((0, step)), self.starts[i], CAP)
                        for v, row_step in enumerate((-1, 1)):
                            borrow(OFFSET_LIST.index((row_step, step)), self.starts[sides + v] + CAP + i, 1)
                    if 0 <= col - step < cols:
                        for n, row_step in enumerate((0, -1, 1)):
                            table[d, self.lend_at + 3 * i + n] = OFFSET_LIST.index((row_step, step))
        self.table = table

    def side_edge(self, i, c, table_ref, send_ref):
        return send_ref[table_ref[self.lend_at + 3 * i] * CAP + c]

    def side_corner(self, i, v, table_ref, send_ref):
        k = table_ref[self.lend_at + 3 * i + 1 + v]
        found = send_ref[k * CAP]
        for other in range(1, CAP):
            found = jnp.maximum(found, send_ref[k * CAP + other])
        return found

    def rise_edge(self, v, c, send_ref):
        return send_ref[OFFSET_LIST.index((2 * v - 1, 0)) * CAP + c]


def rows_of(c):
    return slice(c * BT, (c + 1) * BT)


def block_rows(index):
    return pl.ds(pl.multiple_of(index * BT, BT), BT)


def turn_matrix(orient, back):
    token = lax.broadcasted_iota(jnp.int32, (BT, BT), 1 if back else 0)
    place = lax.broadcasted_iota(jnp.int32, (BT, BT), 0 if back else 1)
    row, col = token >> 3, token & (PATCH - 1)
    row = jnp.where((orient & 1) == 1, PATCH - 1 - row, row)
    col = jnp.where(((orient >> 1) & 1) == 1, PATCH - 1 - col, col)
    mapped = jnp.where(orient >= 4, PATCH * col + row, PATCH * row + col)
    return (mapped == place).astype(jnp.float32).astype(jnp.bfloat16)


def pack_kernel(parts, left_ref, right_ref, out_ref, *sems):
    holders = out_ref.shape[0]
    width = left_ref.shape[1] // (holders * parts)
    copies = []
    for s in range(holders):
        for part in range(parts):
            at = (s * parts + part) * width
            for ref, to in ((left_ref, 2 * part * width), (right_ref, (2 * part + 1) * width)):
                if sems:
                    copies.append(pltpu.make_async_copy(ref.at[:, at:at + width], out_ref.at[s, :, to:to + width],
                                                        sems[0].at[len(copies)]))
                    copies[-1].start()
                else:
                    out_ref[s, :, to:to + width] = ref[:, at:at + width]
    for copy in copies:
        copy.wait()


def unpack_kernel(parts, dq_ref, dkv_ref, *outs):
    holders = dq_ref.shape[0]
    width = dq_ref.shape[2] // parts
    for s in range(holders):
        for part in range(parts):
            to = slice((s * parts + part) * width, (s * parts + part + 1) * width)
            outs[0][:, to] = dq_ref[s, :, part * width:(part + 1) * width]
            for half in range(2):
                at = (2 * part + half) * width
                outs[1 + half][:, to] = dkv_ref[s, :, at:at + width]


def lend_corners_kernel(plan, table_ref, send_ref, kv_ref, *out_refs):
    for i in range(plan.sides):
        for v in range(2):
            block = plan.side_corner(i, v, table_ref, send_ref)
            out_refs[i][rows_of(v), :] = kv_ref[block_rows(block), :]


def lend_edges_kernel(plan, table_ref, send_ref, kv_ref, *refs):
    corners, out_refs = refs[:plan.sides], refs[plan.sides:]
    for v in range(2):
        out_ref = out_refs[plan.sides + v]
        for c in range(CAP):
            out_ref[rows_of(c), :] = kv_ref[block_rows(plan.rise_edge(v, c, send_ref)), :]
        for i in range(plan.sides):
            out_ref[rows_of(CAP + i), :] = corners[i][rows_of(v), :]
    for i in range(plan.sides):
        for c in range(CAP):
            out_refs[i][rows_of(c), :] = kv_ref[block_rows(plan.side_edge(i, c, table_ref, send_ref)), :]


def forward_kernel(plan, *refs):
    for i in range(plan.sides):
        for v in range(2):
            refs[2 + i][rows_of(v), :] = refs[v][rows_of(CAP + i), :]


def settle_kernel(plan, table_ref, send_ref, own_ref, *refs):
    out_ref, total = refs[-2:]
    sides, rises = refs[:plan.sides], refs[plan.sides:plan.sides + 2]
    corners = refs[plan.sides + 2:-2]
    total[...] = own_ref[...]

    def add(block, ref, c):
        total[block_rows(block), :] += ref[rows_of(c), :].astype(jnp.float32)

    for i in range(plan.sides):
        for c in range(CAP):
            add(plan.side_edge(i, c, table_ref, send_ref), sides[i], c)
        for v in range(2):
            add(plan.side_corner(i, v, table_ref, send_ref), corners[i], v)
    for v in range(2):
        for c in range(CAP):
            add(plan.rise_edge(v, c, send_ref), rises[v], c)
    out_ref[...] = total[...].astype(jnp.bfloat16)


def dot(a, b, contract):
    return lax.dot_general(a, b, ((contract[:1], contract[1:]), ((), ())),
                           preferred_element_type=jnp.float32)


def attend_kernel(plan, parts, table_ref, near_ref, orient_ref, qg_ref, kv_ref, bias_ref, *refs):
    groups = len(plan.shapes)
    arrived = refs[:groups]
    dq_ref, own_ref, *leaving = refs[groups:2 * groups + 2]
    ext, acc, win, wide, work, probs_ref, dscores_ref = refs[2 * groups + 2:]
    width = win.shape[2] // 2
    heads = width // HD
    scale = HD ** -0.5
    keys, values = slice(0, width), slice(width, 2 * width)
    slabs = [slice(at, at + SLAB) for at in range(0, WINK, SLAB)]

    def turned(i, c, back):
        return turn_matrix(orient_ref[table_ref[plan.dir_at + plan.starts[i] - QB_DOM + c]], back)

    ext[:QB_DOM * BT, :] = kv_ref[...]
    for i, count in enumerate(plan.shapes):
        for c in range(count):
            if c == 0 or c >= CAP:
                turn = turned(i, c, False)
            ext[rows_of(plan.starts[i] + c), :] = dot(turn, arrived[i][rows_of(c), :], (1, 0)).astype(jnp.bfloat16)
    acc[...] = jnp.zeros_like(acc)

    same_head = (lax.broadcasted_iota(jnp.int32, (width, width), 0) // HD
                 == lax.broadcasted_iota(jnp.int32, (width, width), 1) // HD)

    def spread(block):
        copies = jnp.concatenate([block] * heads, axis=0)
        return jnp.where(same_head, copies, jnp.zeros_like(copies))

    def columns(part, half):
        return slice((2 * part + half) * width, (2 * part + half + 1) * width)

    def products(b, part, slot):
        pair = slice(2 * part * width, 2 * (part + 1) * width)
        for j in range(WIN):
            win[slot, rows_of(j), :] = ext[block_rows(table_ref[near_ref[b * WIN + j]]), pair]
        block = qg_ref[block_rows(b), pair]
        wide[slot, 0] = spread(block[:, keys] * jnp.bfloat16(scale))
        wide[slot, 1] = spread(block[:, values])
        work[slot, 0] = dot(win[slot, :, keys], wide[slot, 0], (1, 1)) + bias_ref[:, part * width:(part + 1) * width]
        work[slot, 1] = dot(win[slot, :, values], wide[slot, 1], (1, 1))

    def softmax(slot):
        top = work[slot, 0, slabs[0], :]
        for slab in slabs[1:]:
            top = jnp.maximum(top, work[slot, 0, slab, :])
        top = jnp.max(top, axis=0, keepdims=True)
        total = jnp.zeros((SLAB, width), jnp.float32)
        delta = jnp.zeros((SLAB, width), jnp.float32)
        for slab in slabs:
            weight = jnp.exp(work[slot, 0, slab, :] - top)
            work[slot, 0, slab, :] = weight
            total = total + weight
            delta = delta + weight * work[slot, 1, slab, :]
        inverse = 1.0 / jnp.sum(total, axis=0, keepdims=True)
        delta = jnp.sum(delta, axis=0, keepdims=True) * inverse
        for slab in slabs:
            probs = work[slot, 0, slab, :] * inverse
            probs_ref[slot, slab, :] = probs.astype(jnp.bfloat16)
            dscores_ref[slot, slab, :] = (probs * (work[slot, 1, slab, :] - delta)).astype(jnp.bfloat16)

    def gradients(b, part, slot):
        dscores = dscores_ref[slot]
        grad_q = dot(dscores, win[slot, :, keys], (0, 0))
        grad_q = jnp.where(same_head, grad_q, 0.0)
        total_q = grad_q[:BT]
        for h in range(1, heads):
            total_q = total_q + grad_q[rows_of(h)]
        dq_ref[block_rows(b), part * width:(part + 1) * width] = (total_q * scale).astype(jnp.bfloat16)
        grad_k = dot(dscores, wide[slot, 0], (1, 0))
        grad_v = dot(probs_ref[slot], wide[slot, 1], (1, 0))
        for j in range(WIN):
            place = block_rows(table_ref[near_ref[b * WIN + j]])
            acc[place, columns(part, 0)] += grad_k[rows_of(j)]
            acc[place, columns(part, 1)] += grad_v[rows_of(j)]

    def three_blocks(turn, carry):
        for u in range(3 * parts):
            after, before = u + 1, u - 1
            products(jnp.minimum(3 * turn + after // parts, QB_DOM - 1), after % parts, after % 3)
            softmax(u % 3)
            gradients(jnp.maximum(3 * turn + before // parts, 0), before % parts, before % 3)
        return carry

    for ref in (win, wide, probs_ref, dscores_ref):
        ref[2] = jnp.zeros_like(ref[2])
    products(0, 0, 0)
    lax.fori_loop(0, QB_DOM // 3, three_blocks, 0)
    gradients(QB_DOM - 1, parts - 1, 2)

    own_ref[...] = acc[:QB_DOM * BT, :]
    for i, count in enumerate(plan.shapes):
        for c in range(count):
            if c == 0 or c >= CAP:
                turn = turned(i, c, True)
            slot = acc[rows_of(plan.starts[i] + c), :].astype(jnp.bfloat16)
            leaving[i][rows_of(c), :] = dot(turn, slot, (1, 0)).astype(jnp.bfloat16)


def smem_specs(count):
    return [pl.BlockSpec(memory_space=pltpu.SMEM)] * count


def vmem_specs(count):
    return [pl.BlockSpec(memory_space=pltpu.VMEM)] * count


def params():
    return pltpu.CompilerParams(vmem_limit_bytes=VMEM_LIMIT)


def bf16(*shape):
    return jax.ShapeDtypeStruct(shape, jnp.bfloat16)


def any_specs(count):
    return [pl.BlockSpec(memory_space=pl.ANY)] * count


def busy(microseconds):
    return pl.CostEstimate(flops=int(microseconds * 1.15e9), bytes_accessed=0, transcendentals=0)


def call(kernel, name, scalars, arrays, outs, after=(), in_place=False, takes=1.0, **more):
    after = [x[tuple(slice(0, n) for n in (1,) * (x.ndim - 2) + (16, 128))] for x in after]
    taken = len(scalars) + len(arrays)

    def body(*refs):
        kernel(*refs[:taken], *refs[taken + len(after):])

    return pl.pallas_call(
        body,
        out_shape=outs,
        in_specs=smem_specs(len(scalars)) + (any_specs if in_place else vmem_specs)(len(arrays)) + any_specs(len(after)),
        out_specs=vmem_specs(len(outs)),
        compiler_params=params(),
        cost_estimate=busy(takes),
        name=name,
        **more,
    )(*scalars, *arrays, *after)


def per_device(plan, queries, keys_in, values_in, grad_out, pos_bias, neighbours, send_block, orient):
    heads = pos_bias.shape[0]
    parts = heads // GROUP_HEADS if heads % GROUP_HEADS == 0 else 1
    width = heads * HD
    part_width = width // parts
    tokens = queries.shape[0]
    holders = lax.axis_size("head")
    tokens_dom = tokens * holders
    sides = plan.sides
    table = lax.dynamic_index_in_dim(jnp.asarray(plan.table), lax.axis_index("dom"), 0, False)
    near, sends, turns = neighbours.reshape(-1), send_block.reshape(-1), orient.reshape(-1)

    def swap(matrix):
        return lax.all_to_all(matrix, "head", split_axis=0, concat_axis=0, tiled=True)

    def swap_back(matrix):
        return swap(matrix.reshape(holders, tokens, -1))

    def pack(left, right, after):
        more = {}
        if part_width % 128 == 0:
            more = dict(in_place=True, scratch_shapes=[pltpu.SemaphoreType.DMA((2 * holders * parts,))])
        return call(functools.partial(pack_kernel, parts), "pack", [], [left, right],
                    [bf16(holders, tokens, 2 * width)], after, **more)[0]

    def permute(value, pairs):
        return lax.ppermute(value, "dom", pairs)

    def permute_back(value, pairs):
        return lax.ppermute(value, "dom", [(d, p) for p, d in pairs])

    block_shapes = [bf16(count * BT, 2 * width) for count in plan.shapes]
    corner_shapes = [bf16(2 * BT, 2 * width)] * sides

    packed = pack(keys_in, values_in, [])
    kv = swap(packed).reshape(tokens_dom, 2 * width)
    bias = jnp.transpose(pos_bias, (2, 0, 1)).reshape(WINK, heads * BT)
    packed = pack(queries, grad_out, [kv, bias])
    qg = swap(packed).reshape(tokens_dom, 2 * width)

    corners = call(functools.partial(lend_corners_kernel, plan), "lend_corners", [table, sends], [kv],
                   corner_shapes, [packed])
    corners = [permute(x, pairs) for x, pairs in zip(corners, plan.side_pairs)]
    lent = call(functools.partial(lend_edges_kernel, plan), "lend_edges", [table, sends], [kv, *corners], block_shapes)
    arrived = [permute(x, pairs) for x, pairs in zip(lent, plan.side_pairs + plan.rise_pairs)]

    grad_q, own, *leaving = call(
        functools.partial(attend_kernel, plan, parts), "attend", [table, near, turns], [qg, kv, bias, *arrived],
        [bf16(tokens_dom, width), jax.ShapeDtypeStruct((tokens_dom, 2 * width), jnp.float32)] + block_shapes,
        takes=15.0,
        scratch_shapes=[
            pltpu.VMEM((plan.slots * BT, 2 * width), jnp.bfloat16),
            pltpu.VMEM((plan.slots * BT, 2 * width), jnp.float32),
            pltpu.VMEM((3, WINK, 2 * part_width), jnp.bfloat16),
            pltpu.VMEM((3, 2, part_width, part_width), jnp.bfloat16),
            pltpu.VMEM((3, 2, WINK, part_width), jnp.float32),
            pltpu.VMEM((3, WINK, part_width), jnp.bfloat16),
            pltpu.VMEM((3, WINK, part_width), jnp.bfloat16),
        ],
    )
    rises = [permute_back(x, pairs) for x, pairs in zip(leaving[sides:], plan.rise_pairs)]
    edges = [permute_back(x, pairs) for x, pairs in zip(leaving[:sides], plan.side_pairs)]
    corners = call(functools.partial(forward_kernel, plan), "forward", [], rises, corner_shapes)
    corners = [permute_back(x, pairs) for x, pairs in zip(corners, plan.side_pairs)]
    settled = call(functools.partial(settle_kernel, plan), "settle", [table, sends], [own, *edges, *rises, *corners],
                   [bf16(tokens_dom, 2 * width)],
                   scratch_shapes=[pltpu.VMEM((tokens_dom, 2 * width), jnp.float32)])[0]
    return call(functools.partial(unpack_kernel, parts), "unpack", [], [swap_back(grad_q), swap_back(settled)],
                [bf16(tokens, holders * width)] * 3)


def solution(mesh):
    plan = Plan(mesh.shape["dom"])
    tokens = P(("dom", "head"), None)
    return jax.shard_map(
        functools.partial(per_device, plan),
        mesh=mesh,
        in_specs=(
            tokens,
            tokens,
            tokens,
            tokens,
            P("head", None, None),
            P("dom", None),
            P("dom", None, None),
            P("dom", None),
        ),
        out_specs=(tokens, tokens, tokens),
        check_vma=False,
    )
```

```python
import functools

import jax
import jax.numpy as jnp
import numpy as np
from jax import lax
from jax.experimental import pallas as pl
from jax.experimental.pallas import tpu as pltpu
from jax.sharding import PartitionSpec as P

HD = 64
PATCH = 8
BT = 64
GRID_ROWS = 4
DIRS = 8
WIN = 9
WINK = 576
QB_DOM = 9
CAP = 3
GROUP_HEADS = 4
SLAB = 32
VMEM_LIMIT = 48 * 1024 * 1024

OFFSET_LIST = [(-1, -1), (-1, 0), (-1, 1), (0, -1), (0, 1), (1, -1), (1, 0), (1, 1)]


class Plan:
    def __init__(self, domains):
        cols = domains // GRID_ROWS
        cells = [divmod(d, cols) for d in range(domains)]
        steps = [(-1, 1)] if cols == 2 else [(-1,), (1,)] if cols > 2 else []
        self.side_pairs = [[(d + step, d) for step in side for d, (_, col) in enumerate(cells)
                            if 0 <= col + step < cols] for side in steps]
        self.rise_pairs = [[(d + step * cols, d) for d, (row, _) in enumerate(cells)
                            if 0 <= row + step < GRID_ROWS] for step in (-1, 1)]
        sides = len(steps)
        self.sides = sides
        self.rise_blocks = CAP + sides
        self.borrowed = sides * CAP + 2 * self.rise_blocks
        self.slots = QB_DOM + self.borrowed
        self.shapes = [CAP] * sides + [self.rise_blocks] * 2
        self.starts = [QB_DOM + sum(self.shapes[:i]) for i in range(len(self.shapes))]
        slot_total = QB_DOM + DIRS * CAP
        self.dir_at = slot_total
        self.lend_at = slot_total + self.borrowed
        table = np.zeros((domains, self.lend_at + 3 * sides), np.int32)
        for d, (_, col) in enumerate(cells):
            table[d, :QB_DOM] = np.arange(QB_DOM)

            def borrow(k, place, count):
                for c in range(CAP):
                    table[d, QB_DOM + k * CAP + c] = place + c % count
                table[d, self.dir_at + place - QB_DOM:self.dir_at + place - QB_DOM + count] = k

            for v, row_step in enumerate((-1, 1)):
                borrow(OFFSET_LIST.index((row_step, 0)), self.starts[sides + v], CAP)
            for i, side in enumerate(steps):
                for step in side:
                    if 0 <= col + step < cols:
                        borrow(OFFSET_LIST.index((0, step)), self.starts[i], CAP)
                        for v, row_step in enumerate((-1, 1)):
                            borrow(OFFSET_LIST.index((row_step, step)), self.starts[sides + v] + CAP + i, 1)
                    if 0 <= col - step < cols:
                        for n, row_step in enumerate((0, -1, 1)):
                            table[d, self.lend_at + 3 * i + n] = OFFSET_LIST.index((row_step, step))
        self.table = table

    def entry(self, table_ref, at):
        return table_ref[lax.axis_index("dom"), at]

    def side_edge(self, i, c, table_ref, send_ref):
        return send_ref[self.entry(table_ref, self.lend_at + 3 * i) * CAP + c]

    def side_corner(self, i, v, table_ref, send_ref):
        k = self.entry(table_ref, self.lend_at + 3 * i + 1 + v)
        found = send_ref[k * CAP]
        for other in range(1, CAP):
            found = jnp.maximum(found, send_ref[k * CAP + other])
        return found

    def rise_edge(self, v, c, send_ref):
        return send_ref[OFFSET_LIST.index((2 * v - 1, 0)) * CAP + c]


def rows_of(c):
    return slice(c * BT, (c + 1) * BT)


def block_rows(index):
    return pl.ds(pl.multiple_of(index * BT, BT), BT)


def turn_matrix(orient, back):
    token = lax.broadcasted_iota(jnp.int32, (BT, BT), 1 if back else 0)
    place = lax.broadcasted_iota(jnp.int32, (BT, BT), 0 if back else 1)
    row, col = token >> 3, token & (PATCH - 1)
    row = jnp.where((orient & 1) == 1, PATCH - 1 - row, row)
    col = jnp.where(((orient >> 1) & 1) == 1, PATCH - 1 - col, col)
    mapped = jnp.where(orient >= 4, PATCH * col + row, PATCH * row + col)
    return (mapped == place).astype(jnp.float32).astype(jnp.bfloat16)


def pack_kernel(parts, left_ref, right_ref, out_ref, *sems):
    holders = out_ref.shape[0]
    width = left_ref.shape[1] // (holders * parts)
    copies = []
    for s in range(holders):
        for part in range(parts):
            at = (s * parts + part) * width
            for ref, to in ((left_ref, 2 * part * width), (right_ref, (2 * part + 1) * width)):
                if sems:
                    copies.append(pltpu.make_async_copy(ref.at[:, at:at + width], out_ref.at[s, :, to:to + width],
                                                        sems[0].at[len(copies)]))
                    copies[-1].start()
                else:
                    out_ref[s, :, to:to + width] = ref[:, at:at + width]
    for copy in copies:
        copy.wait()


def unpack_kernel(parts, dq_ref, dkv_ref, *outs):
    holders = dq_ref.shape[0]
    width = dq_ref.shape[2] // parts
    for s in range(holders):
        for part in range(parts):
            to = slice((s * parts + part) * width, (s * parts + part + 1) * width)
            outs[0][:, to] = dq_ref[s, :, part * width:(part + 1) * width]
            for half in range(2):
                at = (2 * part + half) * width
                outs[1 + half][:, to] = dkv_ref[s, :, at:at + width]


def copy_all(pairs, sems):
    copies = [pltpu.make_async_copy(source, target, sems.at[n]) for n, (source, target) in enumerate(pairs)]
    for copy in copies:
        copy.start()
    for copy in copies:
        copy.wait()


def lend_corners_kernel(plan, table_ref, send_ref, kv_ref, *refs):
    pairs = []
    for i in range(plan.sides):
        for v in range(2):
            block = plan.side_corner(i, v, table_ref, send_ref)
            pairs.append((kv_ref.at[block_rows(block), :], refs[i].at[rows_of(v), :]))
    copy_all(pairs, refs[-1])


def lend_edges_kernel(plan, table_ref, send_ref, kv_ref, *refs):
    corners, out_refs = refs[:plan.sides], refs[plan.sides:]
    pairs = []
    for v in range(2):
        out_ref = out_refs[plan.sides + v]
        for c in range(CAP):
            pairs.append((kv_ref.at[block_rows(plan.rise_edge(v, c, send_ref)), :], out_ref.at[rows_of(c), :]))
        for i in range(plan.sides):
            pairs.append((corners[i].at[rows_of(v), :], out_ref.at[rows_of(CAP + i), :]))
    for i in range(plan.sides):
        for c in range(CAP):
            block = plan.side_edge(i, c, table_ref, send_ref)
            pairs.append((kv_ref.at[block_rows(block), :], out_refs[i].at[rows_of(c), :]))
    copy_all(pairs, refs[-1])


def place_kernel(plan, table_ref, near_ref, orient_ref, places_ref, turns_ref):
    for n in range(QB_DOM * WIN):
        places_ref[n] = plan.entry(table_ref, near_ref[n])
    for n in range(plan.borrowed):
        turns_ref[n] = orient_ref[plan.entry(table_ref, plan.dir_at + n)]


def forward_kernel(plan, *refs):
    for i in range(plan.sides):
        for v in range(2):
            refs[2 + i][rows_of(v), :] = refs[v][rows_of(CAP + i), :]


def settle_kernel(plan, table_ref, send_ref, own_ref, *refs):
    out_ref, total = refs[-2:]
    sides, rises = refs[:plan.sides], refs[plan.sides:plan.sides + 2]
    corners = refs[plan.sides + 2:-2]
    total[...] = own_ref[...]

    def add(block, ref, c):
        total[block_rows(block), :] += ref[rows_of(c), :].astype(jnp.float32)

    for i in range(plan.sides):
        for c in range(CAP):
            add(plan.side_edge(i, c, table_ref, send_ref), sides[i], c)
        for v in range(2):
            add(plan.side_corner(i, v, table_ref, send_ref), corners[i], v)
    for v in range(2):
        for c in range(CAP):
            add(plan.rise_edge(v, c, send_ref), rises[v], c)
    out_ref[...] = total[...].astype(jnp.bfloat16)


def dot(a, b, contract):
    return lax.dot_general(a, b, ((contract[:1], contract[1:]), ((), ())),
                           preferred_element_type=jnp.float32)


def attend_kernel(plan, parts, places_ref, turns_ref, qg_ref, kv_ref, bias_ref, *refs):
    groups = len(plan.shapes)
    arrived = refs[:groups]
    dq_ref, own_ref, *leaving = refs[groups:2 * groups + 2]
    ext, acc, win, wide, scores_ref, dprobs_ref, weights_ref, dscores_ref = refs[2 * groups + 2:]
    width = win.shape[2] // 2
    heads = width // HD
    scale = HD ** -0.5
    keys, values = slice(0, width), slice(width, 2 * width)
    slabs = [slice(at, at + SLAB) for at in range(0, WINK, SLAB)]

    def turned(i, c, back):
        return turn_matrix(turns_ref[plan.starts[i] - QB_DOM + c], back)

    ext[:QB_DOM * BT, :] = kv_ref[...]
    for i, count in enumerate(plan.shapes):
        for c in range(count):
            if c == 0 or c >= CAP:
                turn = turned(i, c, False)
            ext[rows_of(plan.starts[i] + c), :] = dot(turn, arrived[i][rows_of(c), :], (1, 0)).astype(jnp.bfloat16)
    acc[...] = jnp.zeros_like(acc)

    same_head = (lax.broadcasted_iota(jnp.int32, (width, width), 0) // HD
                 == lax.broadcasted_iota(jnp.int32, (width, width), 1) // HD)

    def spread(block):
        copies = jnp.concatenate([block] * heads, axis=0)
        return jnp.where(same_head, copies, jnp.zeros_like(copies))

    def columns(part, half):
        return slice((2 * part + half) * width, (2 * part + half + 1) * width)

    def products(b, part, slot):
        pair = slice(2 * part * width, 2 * (part + 1) * width)
        for j in range(WIN):
            win[slot, rows_of(j), :] = ext[block_rows(places_ref[b * WIN + j]), pair]
        block = qg_ref[block_rows(b), pair]
        wide[slot, 0] = spread(block[:, keys] * jnp.bfloat16(scale))
        wide[slot, 1] = spread(block[:, values])
        bias = bias_ref[:, part * width:(part + 1) * width]
        scores_ref[slot] = dot(win[slot, :, keys], wide[slot, 0], (1, 1)) + bias
        dprobs_ref[slot] = dot(win[slot, :, values], wide[slot, 1], (1, 1)).astype(jnp.bfloat16)

    def softmax(slot):
        top = scores_ref[slot, slabs[0], :]
        for slab in slabs[1:]:
            top = jnp.maximum(top, scores_ref[slot, slab, :])
        top = jnp.max(top, axis=0, keepdims=True)
        total = jnp.zeros((SLAB, width), jnp.float32)
        delta = jnp.zeros((SLAB, width), jnp.float32)
        for slab in slabs:
            weight = jnp.exp(scores_ref[slot, slab, :] - top)
            weights_ref[slot, slab, :] = weight.astype(jnp.bfloat16)
            total = total + weight
            delta = delta + weight * dprobs_ref[slot, slab, :].astype(jnp.float32)
        inverse = 1.0 / jnp.sum(total, axis=0, keepdims=True)
        delta = jnp.sum(delta, axis=0, keepdims=True) * inverse
        for slab in slabs:
            spare = (dprobs_ref[slot, slab, :].astype(jnp.float32) - delta) * inverse
            dscores_ref[slot, slab, :] = (weights_ref[slot, slab, :].astype(jnp.float32) * spare).astype(jnp.bfloat16)
        by_row = jnp.transpose(jnp.broadcast_to(inverse, (8, width)))[:, :1]
        wide[slot, 1] = (wide[slot, 1].astype(jnp.float32) * by_row).astype(jnp.bfloat16)

    def gradients(b, part, slot):
        dscores = dscores_ref[slot]
        grad_q = dot(dscores, win[slot, :, keys], (0, 0))
        grad_q = jnp.where(same_head, grad_q, 0.0)
        total_q = grad_q[:BT]
        for h in range(1, heads):
            total_q = total_q + grad_q[rows_of(h)]
        dq_ref[block_rows(b), part * width:(part + 1) * width] = (total_q * scale).astype(jnp.bfloat16)
        grad_k = dot(dscores, wide[slot, 0], (1, 0))
        grad_v = dot(weights_ref[slot], wide[slot, 1], (1, 0))
        for j in range(WIN):
            place = block_rows(places_ref[b * WIN + j])
            acc[place, columns(part, 0)] += grad_k[rows_of(j)]
            acc[place, columns(part, 1)] += grad_v[rows_of(j)]

    def three_blocks(turn, carry):
        for u in range(3 * parts):
            after, before = u + 1, u - 1
            products(jnp.minimum(3 * turn + after // parts, QB_DOM - 1), after % parts, after % 3)
            softmax(u % 3)
            gradients(jnp.maximum(3 * turn + before // parts, 0), before % parts, before % 3)
        return carry

    for ref in (win, wide, weights_ref, dscores_ref):
        ref[2] = jnp.zeros_like(ref[2])
    products(0, 0, 0)
    lax.fori_loop(0, QB_DOM // 3, three_blocks, 0)
    gradients(QB_DOM - 1, parts - 1, 2)

    own_ref[...] = acc[:QB_DOM * BT, :]
    for i, count in enumerate(plan.shapes):
        for c in range(count):
            if c == 0 or c >= CAP:
                turn = turned(i, c, True)
            slot = acc[rows_of(plan.starts[i] + c), :].astype(jnp.bfloat16)
            leaving[i][rows_of(c), :] = dot(turn, slot, (1, 0)).astype(jnp.bfloat16)


def smem_specs(count):
    return [pl.BlockSpec(memory_space=pltpu.SMEM)] * count


def vmem_specs(count):
    return [pl.BlockSpec(memory_space=pltpu.VMEM)] * count


def params():
    return pltpu.CompilerParams(vmem_limit_bytes=VMEM_LIMIT)


def bf16(*shape):
    return jax.ShapeDtypeStruct(shape, jnp.bfloat16)


def any_specs(count):
    return [pl.BlockSpec(memory_space=pl.ANY)] * count


def busy(microseconds):
    return pl.CostEstimate(flops=int(microseconds * 1.15e9), bytes_accessed=0, transcendentals=0)


def call(kernel, name, scalars, arrays, outs, after=(), in_place=False, out_specs=None, takes=1.0, **more):
    after = [x[tuple(slice(0, n) for n in (1,) * (x.ndim - 2) + (16, 128))] for x in after]
    taken = len(scalars) + len(arrays)

    def body(*refs):
        kernel(*refs[:taken], *refs[taken + len(after):])

    return pl.pallas_call(
        body,
        out_shape=outs,
        in_specs=smem_specs(len(scalars)) + (any_specs if in_place else vmem_specs)(len(arrays)) + any_specs(len(after)),
        out_specs=out_specs or vmem_specs(len(outs)),
        compiler_params=params(),
        cost_estimate=busy(takes),
        name=name,
        **more,
    )(*scalars, *arrays, *after)


def per_device(plan, queries, keys_in, values_in, grad_out, pos_bias, neighbours, send_block, orient):
    heads = pos_bias.shape[0]
    parts = heads // GROUP_HEADS if heads % GROUP_HEADS == 0 else 1
    width = heads * HD
    part_width = width // parts
    tokens = queries.shape[0]
    holders = lax.axis_size("head")
    tokens_dom = tokens * holders
    sides = plan.sides
    table = jnp.asarray(plan.table)
    near, sends, turns = neighbours.reshape(-1), send_block.reshape(-1), orient.reshape(-1)

    def swap(matrix):
        return lax.all_to_all(matrix, "head", split_axis=0, concat_axis=0, tiled=True)

    def swap_back(matrix):
        return swap(matrix.reshape(holders, tokens, -1))

    def pack(left, right, after):
        more = {}
        if part_width % 128 == 0:
            more = dict(in_place=True, scratch_shapes=[pltpu.SemaphoreType.DMA((2 * holders * parts,))])
        return call(functools.partial(pack_kernel, parts), "pack", [], [left, right],
                    [bf16(holders, tokens, 2 * width)], after, **more)[0]

    def permute(value, pairs):
        return lax.ppermute(value, "dom", pairs)

    def permute_back(value, pairs):
        return lax.ppermute(value, "dom", [(d, p) for p, d in pairs])

    block_shapes = [bf16(count * BT, 2 * width) for count in plan.shapes]
    corner_shapes = [bf16(2 * BT, 2 * width)] * sides

    def in_place(copies, outs):
        return dict(in_place=True, out_specs=any_specs(len(outs)), scratch_shapes=[pltpu.SemaphoreType.DMA((copies,))])

    packed_kv = pack(keys_in, values_in, [])
    kv = swap(packed_kv).reshape(tokens_dom, 2 * width)
    bias = jnp.transpose(pos_bias, (2, 0, 1)).reshape(WINK, heads * BT)
    qg = swap(pack(queries, grad_out, [packed_kv, bias])).reshape(tokens_dom, 2 * width)

    corners = call(functools.partial(lend_corners_kernel, plan), "lend_corners", [table, sends], [kv],
                   corner_shapes, **in_place(2 * sides, corner_shapes))
    corners = [permute(x, pairs) for x, pairs in zip(corners, plan.side_pairs)]
    lent = call(functools.partial(lend_edges_kernel, plan), "lend_edges", [table, sends], [kv, *corners], block_shapes,
                **in_place(plan.borrowed, block_shapes))
    arrived = [permute(x, pairs) for x, pairs in zip(lent, plan.side_pairs + plan.rise_pairs)]
    places, turned = call(functools.partial(place_kernel, plan), "place", [table, near, turns], [],
                          [jax.ShapeDtypeStruct((n,), jnp.int32) for n in (QB_DOM * WIN, plan.borrowed)],
                          out_specs=smem_specs(2))

    grad_q, own, *leaving = call(
        functools.partial(attend_kernel, plan, parts), "attend", [places, turned], [qg, kv, bias, *arrived],
        [bf16(tokens_dom, width), jax.ShapeDtypeStruct((tokens_dom, 2 * width), jnp.float32)] + block_shapes,
        takes=15.0,
        scratch_shapes=[
            pltpu.VMEM((plan.slots * BT, 2 * width), jnp.bfloat16),
            pltpu.VMEM((plan.slots * BT, 2 * width), jnp.float32),
            pltpu.VMEM((3, WINK, 2 * part_width), jnp.bfloat16),
            pltpu.VMEM((3, 2, part_width, part_width), jnp.bfloat16),
            pltpu.VMEM((3, WINK, part_width), jnp.float32),
            pltpu.VMEM((3, WINK, part_width), jnp.bfloat16),
            pltpu.VMEM((3, WINK, part_width), jnp.bfloat16),
            pltpu.VMEM((3, WINK, part_width), jnp.bfloat16),
        ],
    )
    rises = [permute_back(x, pairs) for x, pairs in zip(leaving[sides:], plan.rise_pairs)]
    edges = [permute_back(x, pairs) for x, pairs in zip(leaving[:sides], plan.side_pairs)]
    corners = call(functools.partial(forward_kernel, plan), "forward", [], rises, corner_shapes)
    corners = [permute_back(x, pairs) for x, pairs in zip(corners, plan.side_pairs)]
    settled = call(functools.partial(settle_kernel, plan), "settle", [table, sends], [own, *edges, *rises, *corners],
                   [bf16(tokens_dom, 2 * width)],
                   scratch_shapes=[pltpu.VMEM((tokens_dom, 2 * width), jnp.float32)])[0]
    return call(functools.partial(unpack_kernel, parts), "unpack", [], [swap_back(grad_q), swap_back(settled)],
                [bf16(tokens, holders * width)] * 3)


def solution(mesh):
    plan = Plan(mesh.shape["dom"])
    tokens = P(("dom", "head"), None)
    return jax.shard_map(
        functools.partial(per_device, plan),
        mesh=mesh,
        in_specs=(
            tokens,
            tokens,
            tokens,
            tokens,
            P("head", None, None),
            P("dom", None),
            P("dom", None, None),
            P("dom", None),
        ),
        out_specs=(tokens, tokens, tokens),
        check_vma=False,
    )
```

```python
import functools

import jax
import jax.numpy as jnp
import numpy as np
from jax import lax
from jax.experimental import pallas as pl
from jax.experimental.pallas import tpu as pltpu
from jax.sharding import PartitionSpec as P

HD = 64
PATCH = 8
BT = 64
GRID_ROWS = 4
DIRS = 8
WIN = 9
WINK = 576
QB_DOM = 9
CAP = 3
SLAB = 32
VMEM_LIMIT = 48 * 1024 * 1024

OFFSET_LIST = [(-1, -1), (-1, 0), (-1, 1), (0, -1), (0, 1), (1, -1), (1, 0), (1, 1)]


class Plan:
    def __init__(self, domains):
        cols = domains // GRID_ROWS
        cells = [divmod(d, cols) for d in range(domains)]
        steps = [(-1, 1)] if cols == 2 else [(-1,), (1,)] if cols > 2 else []
        self.side_pairs = [[(d + step, d) for step in side for d, (_, col) in enumerate(cells)
                            if 0 <= col + step < cols] for side in steps]
        self.rise_pairs = [[(d + step * cols, d) for d, (row, _) in enumerate(cells)
                            if 0 <= row + step < GRID_ROWS] for step in (-1, 1)]
        sides = len(steps)
        self.sides = sides
        self.rise_blocks = CAP + sides
        self.borrowed = sides * CAP + 2 * self.rise_blocks
        self.slots = QB_DOM + self.borrowed
        self.shapes = [CAP] * sides + [self.rise_blocks] * 2
        self.starts = [QB_DOM + sum(self.shapes[:i]) for i in range(len(self.shapes))]
        slot_total = QB_DOM + DIRS * CAP
        self.dir_at = slot_total
        self.lend_at = slot_total + self.borrowed
        table = np.zeros((domains, self.lend_at + 3 * sides), np.int32)
        for d, (_, col) in enumerate(cells):
            table[d, :QB_DOM] = np.arange(QB_DOM)

            def borrow(k, place, count):
                for c in range(CAP):
                    table[d, QB_DOM + k * CAP + c] = place + c % count
                table[d, self.dir_at + place - QB_DOM:self.dir_at + place - QB_DOM + count] = k

            for v, row_step in enumerate((-1, 1)):
                borrow(OFFSET_LIST.index((row_step, 0)), self.starts[sides + v], CAP)
            for i, side in enumerate(steps):
                for step in side:
                    if 0 <= col + step < cols:
                        borrow(OFFSET_LIST.index((0, step)), self.starts[i], CAP)
                        for v, row_step in enumerate((-1, 1)):
                            borrow(OFFSET_LIST.index((row_step, step)), self.starts[sides + v] + CAP + i, 1)
                    if 0 <= col - step < cols:
                        for n, row_step in enumerate((0, -1, 1)):
                            table[d, self.lend_at + 3 * i + n] = OFFSET_LIST.index((row_step, step))
        self.table = table

    def entry(self, table_ref, at):
        return table_ref[lax.axis_index("dom"), at]

    def side_edge(self, i, c, table_ref, send_ref):
        return send_ref[self.entry(table_ref, self.lend_at + 3 * i) * CAP + c]

    def side_corner(self, i, v, table_ref, send_ref):
        k = self.entry(table_ref, self.lend_at + 3 * i + 1 + v)
        found = send_ref[k * CAP]
        for other in range(1, CAP):
            found = jnp.maximum(found, send_ref[k * CAP + other])
        return found

    def rise_edge(self, v, c, send_ref):
        return send_ref[OFFSET_LIST.index((2 * v - 1, 0)) * CAP + c]


def rows_of(c):
    return slice(c * BT, (c + 1) * BT)


def block_rows(index):
    return pl.ds(pl.multiple_of(index * BT, BT), BT)


def turn_matrix(orient, back):
    token = lax.broadcasted_iota(jnp.int32, (BT, BT), 1 if back else 0)
    place = lax.broadcasted_iota(jnp.int32, (BT, BT), 0 if back else 1)
    row, col = token >> 3, token & (PATCH - 1)
    row = jnp.where((orient & 1) == 1, PATCH - 1 - row, row)
    col = jnp.where(((orient >> 1) & 1) == 1, PATCH - 1 - col, col)
    mapped = jnp.where(orient >= 4, PATCH * col + row, PATCH * row + col)
    return (mapped == place).astype(jnp.float32).astype(jnp.bfloat16)


def pack_kernel(chunks, chunk, left_ref, right_ref, out_ref, *sems):
    holders, _, pair_width = out_ref.shape
    width = pair_width // 2
    pairs = []
    for s in range(holders):
        at = (s * chunks + chunk) * width
        pairs.append((left_ref.at[:, at:at + width], out_ref.at[s, :, :width]))
        pairs.append((right_ref.at[:, at:at + width], out_ref.at[s, :, width:]))
    if sems:
        copy_all(pairs, sems[0])
    else:
        for source, target in pairs:
            target[...] = source[...]


def unpack_kernel(*refs):
    grads, outs = refs[:-3], refs[-3:]
    holders, _, all_width = grads[0].shape
    width = all_width // 3
    for chunk, grad_ref in enumerate(grads):
        for s in range(holders):
            to = slice((s * len(grads) + chunk) * width, (s * len(grads) + chunk + 1) * width)
            for which, at in enumerate((2 * width, 0, width)):
                outs[which][:, to] = grad_ref[s, :, at:at + width]


def copy_all(pairs, sems):
    copies = [pltpu.make_async_copy(source, target, sems.at[n]) for n, (source, target) in enumerate(pairs)]
    for copy in copies:
        copy.start()
    for copy in copies:
        copy.wait()


def lend_corners_kernel(plan, table_ref, send_ref, kv_ref, *refs):
    pairs = []
    for i in range(plan.sides):
        for v in range(2):
            block = plan.side_corner(i, v, table_ref, send_ref)
            pairs.append((kv_ref.at[block_rows(block), :], refs[i].at[rows_of(v), :]))
    copy_all(pairs, refs[-1])


def lend_edges_kernel(plan, table_ref, send_ref, kv_ref, *refs):
    corners, out_refs = refs[:plan.sides], refs[plan.sides:]
    pairs = []
    for v in range(2):
        out_ref = out_refs[plan.sides + v]
        for c in range(CAP):
            pairs.append((kv_ref.at[block_rows(plan.rise_edge(v, c, send_ref)), :], out_ref.at[rows_of(c), :]))
        for i in range(plan.sides):
            pairs.append((corners[i].at[rows_of(v), :], out_ref.at[rows_of(CAP + i), :]))
    for i in range(plan.sides):
        for c in range(CAP):
            block = plan.side_edge(i, c, table_ref, send_ref)
            pairs.append((kv_ref.at[block_rows(block), :], out_refs[i].at[rows_of(c), :]))
    copy_all(pairs, refs[-1])


def place_kernel(plan, table_ref, near_ref, orient_ref, places_ref, turns_ref):
    for n in range(QB_DOM * WIN):
        places_ref[n] = plan.entry(table_ref, near_ref[n])
    for n in range(plan.borrowed):
        turns_ref[n] = orient_ref[plan.entry(table_ref, plan.dir_at + n)]


def forward_kernel(plan, *refs):
    for i in range(plan.sides):
        for v in range(2):
            refs[2 + i][rows_of(v), :] = refs[v][rows_of(CAP + i), :]


def settle_kernel(plan, table_ref, send_ref, own_ref, *refs):
    out_ref, total = refs[-2:]
    sides, rises = refs[:plan.sides], refs[plan.sides:plan.sides + 2]
    corners, grad_q_ref = refs[plan.sides + 2:-3], refs[-3]
    pair_width = own_ref.shape[1]
    out_ref[:, pair_width:] = grad_q_ref[...]
    total[...] = own_ref[...]

    def add(block, ref, c):
        total[block_rows(block), :] += ref[rows_of(c), :].astype(jnp.float32)

    for i in range(plan.sides):
        for c in range(CAP):
            add(plan.side_edge(i, c, table_ref, send_ref), sides[i], c)
        for v in range(2):
            add(plan.side_corner(i, v, table_ref, send_ref), corners[i], v)
    for v in range(2):
        for c in range(CAP):
            add(plan.rise_edge(v, c, send_ref), rises[v], c)
    out_ref[:, :pair_width] = total[...].astype(jnp.bfloat16)


def dot(a, b, contract):
    return lax.dot_general(a, b, ((contract[:1], contract[1:]), ((), ())),
                           preferred_element_type=jnp.float32)


def attend_kernel(plan, places_ref, turns_ref, qg_ref, kv_ref, bias_ref, *refs):
    groups = len(plan.shapes)
    arrived = refs[:groups]
    dq_ref, own_ref, *leaving = refs[groups:2 * groups + 2]
    ext, acc, win, wide, scores_ref, dprobs_ref, weights_ref, dscores_ref = refs[2 * groups + 2:]
    width = win.shape[2] // 2
    heads = width // HD
    scale = HD ** -0.5
    keys, values = slice(0, width), slice(width, 2 * width)
    slabs = [slice(at, at + SLAB) for at in range(0, WINK, SLAB)]

    def turned(i, c, back):
        return turn_matrix(turns_ref[plan.starts[i] - QB_DOM + c], back)

    ext[:QB_DOM * BT, :] = kv_ref[...]
    for i, count in enumerate(plan.shapes):
        for c in range(count):
            if c == 0 or c >= CAP:
                turn = turned(i, c, False)
            ext[rows_of(plan.starts[i] + c), :] = dot(turn, arrived[i][rows_of(c), :], (1, 0)).astype(jnp.bfloat16)
    acc[...] = jnp.zeros_like(acc)

    same_head = (lax.broadcasted_iota(jnp.int32, (width, width), 0) // HD
                 == lax.broadcasted_iota(jnp.int32, (width, width), 1) // HD)

    def spread(block):
        copies = jnp.concatenate([block] * heads, axis=0)
        return jnp.where(same_head, copies, jnp.zeros_like(copies))

    places = [block_rows(places_ref[n]) for n in range(QB_DOM * WIN)]

    def products(b, slot):
        for j in range(WIN):
            win[slot, rows_of(j), :] = ext[places[b * WIN + j], :]
        block = qg_ref[rows_of(b), :]
        wide[slot, 0] = spread(block[:, keys] * jnp.bfloat16(scale))
        wide[slot, 1] = spread(block[:, values])
        scores_ref[slot] = dot(win[slot, :, keys], wide[slot, 0], (1, 1)) + bias_ref[...]
        dprobs_ref[slot] = dot(win[slot, :, values], wide[slot, 1], (1, 1)).astype(jnp.bfloat16)

    def softmax(slot):
        top = scores_ref[slot, slabs[0], :]
        for slab in slabs[1:]:
            top = jnp.maximum(top, scores_ref[slot, slab, :])
        top = jnp.max(top, axis=0, keepdims=True)
        total = jnp.zeros((SLAB, width), jnp.float32)
        delta = jnp.zeros((SLAB, width), jnp.float32)
        for slab in slabs:
            weight = jnp.exp(scores_ref[slot, slab, :] - top)
            weights_ref[slot, slab, :] = weight.astype(jnp.bfloat16)
            total = total + weight
            delta = delta + weight * dprobs_ref[slot, slab, :].astype(jnp.float32)
        inverse = 1.0 / jnp.sum(total, axis=0, keepdims=True)
        delta = jnp.sum(delta, axis=0, keepdims=True) * inverse
        for slab in slabs:
            spare = (dprobs_ref[slot, slab, :].astype(jnp.float32) - delta) * inverse
            dscores_ref[slot, slab, :] = (weights_ref[slot, slab, :].astype(jnp.float32) * spare).astype(jnp.bfloat16)
        by_row = jnp.transpose(jnp.broadcast_to(inverse, (8, width)))[:, :1]
        wide[slot, 1] = (wide[slot, 1].astype(jnp.float32) * by_row).astype(jnp.bfloat16)

    def gradients(b, slot):
        dscores = dscores_ref[slot]
        grad_q = dot(dscores, win[slot, :, keys], (0, 0))
        grad_q = jnp.where(same_head, grad_q, 0.0)
        total_q = grad_q[:BT]
        for h in range(1, heads):
            total_q = total_q + grad_q[rows_of(h)]
        dq_ref[rows_of(b), :] = (total_q * scale).astype(jnp.bfloat16)
        grad_k = dot(dscores, wide[slot, 0], (1, 0))
        grad_v = dot(weights_ref[slot], wide[slot, 1], (1, 0))
        for j in range(WIN):
            acc[places[b * WIN + j], keys] += grad_k[rows_of(j)]
            acc[places[b * WIN + j], values] += grad_v[rows_of(j)]

    products(0, 0)
    for b in range(QB_DOM):
        if b + 1 < QB_DOM:
            products(b + 1, (b + 1) % 3)
        softmax(b % 3)
        if b > 0:
            gradients(b - 1, (b - 1) % 3)
    gradients(QB_DOM - 1, (QB_DOM - 1) % 3)

    own_ref[...] = acc[:QB_DOM * BT, :]
    for i, count in enumerate(plan.shapes):
        for c in range(count):
            if c == 0 or c >= CAP:
                turn = turned(i, c, True)
            slot = acc[rows_of(plan.starts[i] + c), :].astype(jnp.bfloat16)
            leaving[i][rows_of(c), :] = dot(turn, slot, (1, 0)).astype(jnp.bfloat16)


def smem_specs(count):
    return [pl.BlockSpec(memory_space=pltpu.SMEM)] * count


def vmem_specs(count):
    return [pl.BlockSpec(memory_space=pltpu.VMEM)] * count


def params():
    return pltpu.CompilerParams(vmem_limit_bytes=VMEM_LIMIT)


def bf16(*shape):
    return jax.ShapeDtypeStruct(shape, jnp.bfloat16)


def any_specs(count):
    return [pl.BlockSpec(memory_space=pl.ANY)] * count


def busy(microseconds):
    return pl.CostEstimate(flops=int(microseconds * 1.15e9), bytes_accessed=0, transcendentals=0)


def call(kernel, name, scalars, arrays, outs, after=(), in_place=False, out_specs=None, takes=1.0, **more):
    after = [x[tuple(slice(0, n) for n in (1,) * (x.ndim - 2) + (16, 128))] for x in after]
    taken = len(scalars) + len(arrays)

    def body(*refs):
        kernel(*refs[:taken], *refs[taken + len(after):])

    return pl.pallas_call(
        body,
        out_shape=outs,
        in_specs=smem_specs(len(scalars)) + (any_specs if in_place else vmem_specs)(len(arrays)) + any_specs(len(after)),
        out_specs=out_specs or vmem_specs(len(outs)),
        compiler_params=params(),
        cost_estimate=busy(takes),
        name=name,
        **more,
    )(*scalars, *arrays, *after)


def per_device(plan, queries, keys_in, values_in, grad_out, pos_bias, neighbours, send_block, orient):
    chunks = 2 if pos_bias.shape[0] % 2 == 0 else 1
    heads = pos_bias.shape[0] // chunks
    width = heads * HD
    tokens = queries.shape[0]
    holders = lax.axis_size("head")
    tokens_dom = tokens * holders
    sides = plan.sides
    table = jnp.asarray(plan.table)
    near, sends, turns = neighbours.reshape(-1), send_block.reshape(-1), orient.reshape(-1)
    block_shapes = [bf16(count * BT, 2 * width) for count in plan.shapes]
    corner_shapes = [bf16(2 * BT, 2 * width)] * sides

    def swap(matrix):
        return lax.all_to_all(matrix.reshape(holders, tokens, -1), "head", split_axis=0, concat_axis=0, tiled=True)

    def pack(left, right, chunk, after):
        more = {}
        if width % 128 == 0:
            more = dict(in_place=True, scratch_shapes=[pltpu.SemaphoreType.DMA((2 * holders,))])
        return call(functools.partial(pack_kernel, chunks, chunk), "pack", [], [left, right],
                    [bf16(holders, tokens, 2 * width)], after, **more)[0]

    def permute(value, pairs):
        return lax.ppermute(value, "dom", pairs)

    def permute_back(value, pairs):
        return lax.ppermute(value, "dom", [(d, p) for p, d in pairs])

    def in_place(copies, outs):
        return dict(in_place=True, out_specs=any_specs(len(outs)), scratch_shapes=[pltpu.SemaphoreType.DMA((copies,))])

    def lend(kv):
        corners = call(functools.partial(lend_corners_kernel, plan), "lend_corners", [table, sends], [kv],
                       corner_shapes, **in_place(2 * sides, corner_shapes))
        corners = [permute(x, pairs) for x, pairs in zip(corners, plan.side_pairs)]
        lent = call(functools.partial(lend_edges_kernel, plan), "lend_edges", [table, sends], [kv, *corners],
                    block_shapes, **in_place(plan.borrowed, block_shapes))
        return lent, [permute(x, pairs) for x, pairs in zip(lent, plan.side_pairs + plan.rise_pairs)]

    def attend(chunk, after):
        grad_q, own, *leaving = call(
            functools.partial(attend_kernel, plan), "attend", [places, turned],
            [qg[chunk], kv[chunk], bias[chunk], *arrived[chunk]],
            [bf16(tokens_dom, width), jax.ShapeDtypeStruct((tokens_dom, 2 * width), jnp.float32)] + block_shapes,
            after, takes=8.0,
            scratch_shapes=[
                pltpu.VMEM((plan.slots * BT, 2 * width), jnp.bfloat16),
                pltpu.VMEM((plan.slots * BT, 2 * width), jnp.float32),
                pltpu.VMEM((3, WINK, 2 * width), jnp.bfloat16),
                pltpu.VMEM((3, 2, width, width), jnp.bfloat16),
                pltpu.VMEM((3, WINK, width), jnp.float32),
                pltpu.VMEM((3, WINK, width), jnp.bfloat16),
                pltpu.VMEM((3, WINK, width), jnp.bfloat16),
                pltpu.VMEM((3, WINK, width), jnp.bfloat16),
            ],
        )
        rises = [permute_back(x, pairs) for x, pairs in zip(leaving[sides:], plan.rise_pairs)]
        edges = [permute_back(x, pairs) for x, pairs in zip(leaving[:sides], plan.side_pairs)]
        corners = call(functools.partial(forward_kernel, plan), "forward", [], rises, corner_shapes)
        corners = [permute_back(x, pairs) for x, pairs in zip(corners, plan.side_pairs)]
        return call(functools.partial(settle_kernel, plan), "settle", [table, sends],
                    [own, *edges, *rises, *corners, grad_q], [bf16(tokens_dom, 3 * width)],
                    scratch_shapes=[pltpu.VMEM((tokens_dom, 2 * width), jnp.float32)])[0]

    places, turned = call(functools.partial(place_kernel, plan), "place", [table, near, turns], [],
                          [jax.ShapeDtypeStruct((n,), jnp.int32) for n in (QB_DOM * WIN, plan.borrowed)],
                          out_specs=smem_specs(2))
    bias = [jnp.transpose(x, (2, 0, 1)).reshape(WINK, heads * BT) for x in jnp.split(pos_bias, chunks, axis=0)]
    kv, lent, arrived, qg, packed = [], [], [], [], []
    for chunk in range(chunks):
        kv.append(swap(pack(keys_in, values_in, chunk, [])).reshape(tokens_dom, 2 * width))
        sent, got = lend(kv[chunk])
        lent.append(sent)
        arrived.append(got)
    for chunk in range(chunks):
        packed.append(pack(queries, grad_out, chunk, [lent[chunk][-1], *(bias if chunk == 0 else [])]))
        qg.append(swap(packed[chunk]).reshape(tokens_dom, 2 * width))
    grads = [swap(attend(chunk, packed[chunk + 1:chunk + 2])) for chunk in range(chunks)]
    return call(unpack_kernel, "unpack", [], grads, [bf16(tokens, holders * chunks * width)] * 3)


def solution(mesh):
    plan = Plan(mesh.shape["dom"])
    tokens = P(("dom", "head"), None)
    return jax.shard_map(
        functools.partial(per_device, plan),
        mesh=mesh,
        in_specs=(
            tokens,
            tokens,
            tokens,
            tokens,
            P("head", None, None),
            P("dom", None),
            P("dom", None, None),
            P("dom", None),
        ),
        out_specs=(tokens, tokens, tokens),
        check_vma=False,
    )
```

```python
import functools

import jax
import jax.numpy as jnp
import numpy as np
from jax import lax
from jax.experimental import pallas as pl
from jax.experimental.pallas import tpu as pltpu
from jax.sharding import PartitionSpec as P

HD = 64
PATCH = 8
BT = 64
GRID_ROWS = 4
DIRS = 8
WIN = 9
WINK = 576
QB_DOM = 9
CAP = 3
GROUP_HEADS = 4
SLAB = 32
VMEM_LIMIT = 48 * 1024 * 1024
VMEM_MOST = 60 * 1024 * 1024

OFFSET_LIST = [(-1, -1), (-1, 0), (-1, 1), (0, -1), (0, 1), (1, -1), (1, 0), (1, 1)]


class Plan:
    def __init__(self, domains):
        cols = domains // GRID_ROWS
        cells = [divmod(d, cols) for d in range(domains)]
        steps = [(-1, 1)] if cols == 2 else [(-1,), (1,)] if cols > 2 else []
        self.side_pairs = [[(d + step, d) for step in side for d, (_, col) in enumerate(cells)
                            if 0 <= col + step < cols] for side in steps]
        rows_apart = [[1 if (row + v) % 2 == 0 else -1 for row, _ in cells] for v in range(2)]
        self.rise_pairs = [[(d + apart[d] * cols, d) for d, (row, _) in enumerate(cells)
                            if 0 <= row + apart[d] < GRID_ROWS] for apart in rows_apart]
        sides = len(steps)
        self.sides = sides
        self.rise_blocks = CAP + sides
        self.borrowed = sides * CAP + 2 * self.rise_blocks
        self.slots = QB_DOM + self.borrowed
        self.shapes = [CAP] * sides + [self.rise_blocks] * 2
        self.starts = [QB_DOM + sum(self.shapes[:i]) for i in range(len(self.shapes))]
        slot_total = QB_DOM + DIRS * CAP
        self.dir_at = slot_total
        self.lend_at = slot_total + self.borrowed
        self.rise_at = self.lend_at + 3 * sides
        table = np.zeros((domains, self.rise_at + 2), np.int32)
        for d, (_, col) in enumerate(cells):
            table[d, :QB_DOM] = np.arange(QB_DOM)

            def borrow(k, place, count):
                for c in range(CAP):
                    table[d, QB_DOM + k * CAP + c] = place + c % count
                table[d, self.dir_at + place - QB_DOM:self.dir_at + place - QB_DOM + count] = k

            above = [apart[d] for apart in rows_apart]
            for v, row_step in enumerate(above):
                borrow(OFFSET_LIST.index((row_step, 0)), self.starts[sides + v], CAP)
                table[d, self.rise_at + v] = OFFSET_LIST.index((-row_step, 0))
            for i, side in enumerate(steps):
                for step in side:
                    if 0 <= col + step < cols:
                        borrow(OFFSET_LIST.index((0, step)), self.starts[i], CAP)
                        for v, row_step in enumerate(above):
                            borrow(OFFSET_LIST.index((row_step, step)), self.starts[sides + v] + CAP + i, 1)
                    if 0 <= col - step < cols:
                        for n, row_step in enumerate((0, -above[0], -above[1])):
                            table[d, self.lend_at + 3 * i + n] = OFFSET_LIST.index((row_step, step))
        self.table = table

    def entry(self, table_ref, at):
        return table_ref[lax.axis_index("dom"), at]

    def side_edge(self, i, c, table_ref, send_ref):
        return send_ref[self.entry(table_ref, self.lend_at + 3 * i) * CAP + c]

    def side_corner(self, i, v, table_ref, send_ref):
        k = self.entry(table_ref, self.lend_at + 3 * i + 1 + v)
        found = send_ref[k * CAP]
        for other in range(1, CAP):
            found = jnp.maximum(found, send_ref[k * CAP + other])
        return found

    def rise_edge(self, v, c, table_ref, send_ref):
        return send_ref[self.entry(table_ref, self.rise_at + v) * CAP + c]


def rows_of(c):
    return slice(c * BT, (c + 1) * BT)


def block_rows(index):
    return pl.ds(pl.multiple_of(index * BT, BT), BT)


def turn_matrix(orient, back):
    token = lax.broadcasted_iota(jnp.int32, (BT, BT), 1 if back else 0)
    place = lax.broadcasted_iota(jnp.int32, (BT, BT), 0 if back else 1)
    row, col = token >> 3, token & (PATCH - 1)
    row = jnp.where((orient & 1) == 1, PATCH - 1 - row, row)
    col = jnp.where(((orient >> 1) & 1) == 1, PATCH - 1 - col, col)
    mapped = jnp.where(orient >= 4, PATCH * col + row, PATCH * row + col)
    return (mapped == place).astype(jnp.float32).astype(jnp.bfloat16)


def pack_kernel(parts, left_ref, right_ref, out_ref, *sems):
    holders = out_ref.shape[0]
    width = left_ref.shape[1] // (holders * parts)
    copies = []
    for s in range(holders):
        for part in range(parts):
            at = (s * parts + part) * width
            for ref, to in ((left_ref, 2 * part * width), (right_ref, (2 * part + 1) * width)):
                if sems:
                    copies.append(pltpu.make_async_copy(ref.at[:, at:at + width], out_ref.at[s, :, to:to + width],
                                                        sems[0].at[len(copies)]))
                    copies[-1].start()
                else:
                    out_ref[s, :, to:to + width] = ref[:, at:at + width]
    for copy in copies:
        copy.wait()


def unpack_kernel(parts, dq_ref, dkv_ref, *outs):
    holders = dq_ref.shape[0]
    width = dq_ref.shape[2] // parts
    for s in range(holders):
        for part in range(parts):
            to = slice((s * parts + part) * width, (s * parts + part + 1) * width)
            outs[0][:, to] = dq_ref[s, :, part * width:(part + 1) * width]
            for half in range(2):
                at = (2 * part + half) * width
                outs[1 + half][:, to] = dkv_ref[s, :, at:at + width]


def copy_all(pairs, sems):
    copies = [pltpu.make_async_copy(source, target, sems.at[n]) for n, (source, target) in enumerate(pairs)]
    for copy in copies:
        copy.start()
    for copy in copies:
        copy.wait()


def lend_corners_kernel(plan, table_ref, send_ref, kv_ref, *refs):
    pairs = []
    for i in range(plan.sides):
        for v in range(2):
            block = plan.side_corner(i, v, table_ref, send_ref)
            pairs.append((kv_ref.at[block_rows(block), :], refs[i].at[rows_of(v), :]))
    copy_all(pairs, refs[-1])


def lend_edges_kernel(plan, table_ref, send_ref, kv_ref, *refs):
    corners, out_refs = refs[:plan.sides], refs[plan.sides:]
    pairs = []
    for v in range(2):
        out_ref = out_refs[plan.sides + v]
        for c in range(CAP):
            pairs.append((kv_ref.at[block_rows(plan.rise_edge(v, c, table_ref, send_ref)), :], out_ref.at[rows_of(c), :]))
        for i in range(plan.sides):
            pairs.append((corners[i].at[rows_of(v), :], out_ref.at[rows_of(CAP + i), :]))
    for i in range(plan.sides):
        for c in range(CAP):
            block = plan.side_edge(i, c, table_ref, send_ref)
            pairs.append((kv_ref.at[block_rows(block), :], out_refs[i].at[rows_of(c), :]))
    copy_all(pairs, refs[-1])


def place_kernel(plan, table_ref, near_ref, orient_ref, places_ref, turns_ref):
    for n in range(QB_DOM * WIN):
        places_ref[n] = plan.entry(table_ref, near_ref[n])
    for n in range(plan.borrowed):
        turns_ref[n] = orient_ref[plan.entry(table_ref, plan.dir_at + n)]


def forward_kernel(plan, *refs):
    for i in range(plan.sides):
        for v in range(2):
            refs[2 + i][rows_of(v), :] = refs[v][rows_of(CAP + i), :]


def settle_kernel(plan, table_ref, send_ref, own_ref, *refs):
    out_ref, total = refs[-2:]
    sides, rises = refs[:plan.sides], refs[plan.sides:plan.sides + 2]
    corners = refs[plan.sides + 2:-2]
    total[...] = own_ref[...]

    def add(block, ref, c):
        total[block_rows(block), :] += ref[rows_of(c), :].astype(jnp.float32)

    for i in range(plan.sides):
        for c in range(CAP):
            add(plan.side_edge(i, c, table_ref, send_ref), sides[i], c)
        for v in range(2):
            add(plan.side_corner(i, v, table_ref, send_ref), corners[i], v)
    for v in range(2):
        for c in range(CAP):
            add(plan.rise_edge(v, c, table_ref, send_ref), rises[v], c)
    out_ref[...] = total[...].astype(jnp.bfloat16)


def dot(a, b, contract):
    return lax.dot_general(a, b, ((contract[:1], contract[1:]), ((), ())),
                           preferred_element_type=jnp.float32)


def attend_kernel(plan, parts, places_ref, turns_ref, qg_ref, kv_ref, bias_ref, *refs):
    groups = len(plan.shapes)
    arrived = refs[:groups]
    dq_ref, own_ref, *leaving = refs[groups:2 * groups + 2]
    ext, acc, qg, dq, win, work, probs_ref, dscores_ref = refs[2 * groups + 2:]
    width = dq.shape[2]
    heads = width // HD
    scale = HD ** -0.5
    keys, values = slice(0, width), slice(width, 2 * width)
    pairs = [slice(2 * part * width, 2 * (part + 1) * width) for part in range(parts)]
    slabs = [slice(at, at + SLAB) for at in range(0, WINK, SLAB)]
    places = [block_rows(places_ref[n]) for n in range(QB_DOM * WIN)]

    def turned(i, c, back):
        return turn_matrix(turns_ref[plan.starts[i] - QB_DOM + c], back)

    for part, pair in enumerate(pairs):
        qg[part] = qg_ref[:, pair]
        ext[part, :QB_DOM * BT, :] = kv_ref[:, pair]
    for i, count in enumerate(plan.shapes):
        for c in range(count):
            if c == 0 or c >= CAP:
                turn = turned(i, c, False)
            block = dot(turn, arrived[i][rows_of(c), :], (1, 0)).astype(jnp.bfloat16)
            for part, pair in enumerate(pairs):
                ext[part, rows_of(plan.starts[i] + c), :] = block[:, pair]
    acc[...] = jnp.zeros_like(acc)

    same_head = (lax.broadcasted_iota(jnp.int32, (width, width), 0) // HD
                 == lax.broadcasted_iota(jnp.int32, (width, width), 1) // HD)

    def spread(block):
        copies = jnp.concatenate([block] * heads, axis=0)
        return jnp.where(same_head, copies, jnp.zeros_like(copies))

    def products(part, b):
        even = b % 2
        for j in range(WIN):
            win[even, rows_of(j), :] = ext[part, places[b * WIN + j], :]
        query = spread(qg[part, rows_of(b), keys] * jnp.bfloat16(scale))
        grad = spread(qg[part, rows_of(b), values])
        work[even, 0] = dot(win[even, :, keys], query, (1, 1)) + bias_ref[part]
        work[even, 1] = dot(win[even, :, values], grad, (1, 1))
        return query, grad

    def softmax(b):
        even = b % 2
        top = work[even, 0, slabs[0], :]
        for slab in slabs[1:]:
            top = jnp.maximum(top, work[even, 0, slab, :])
        top = jnp.max(top, axis=0, keepdims=True)
        total = jnp.zeros((SLAB, width), jnp.float32)
        delta = jnp.zeros((SLAB, width), jnp.float32)
        for slab in slabs:
            weight = jnp.exp(work[even, 0, slab, :] - top)
            work[even, 0, slab, :] = weight
            total = total + weight
            delta = delta + weight * work[even, 1, slab, :]
        inverse = 1.0 / jnp.sum(total, axis=0, keepdims=True)
        delta = jnp.sum(delta, axis=0, keepdims=True) * inverse
        for slab in slabs:
            probs = work[even, 0, slab, :] * inverse
            probs_ref[even, slab, :] = probs.astype(jnp.bfloat16)
            dscores_ref[even, slab, :] = (probs * (work[even, 1, slab, :] - delta)).astype(jnp.bfloat16)

    def gradients(part, b, query, grad):
        even = b % 2
        dscores = dscores_ref[even]
        grad_q = dot(dscores, win[even, :, keys], (0, 0))
        grad_q = jnp.where(same_head, grad_q, 0.0)
        total_q = grad_q[:BT]
        for h in range(1, heads):
            total_q = total_q + grad_q[rows_of(h)]
        dq[part, rows_of(b), :] = (total_q * scale).astype(jnp.bfloat16)
        grad_k = dot(dscores, query, (1, 0))
        grad_v = dot(probs_ref[even], grad, (1, 0))
        for j in range(WIN):
            acc[part, places[b * WIN + j], keys] += grad_k[rows_of(j)]
            acc[part, places[b * WIN + j], values] += grad_v[rows_of(j)]

    def one_part(part, carry):
        here = products(part, 0)
        for b in range(QB_DOM):
            following = products(part, b + 1) if b + 1 < QB_DOM else None
            softmax(b)
            gradients(part, b, *here)
            here = following
        return carry

    lax.fori_loop(0, parts, one_part, 0)
    for part, pair in enumerate(pairs):
        own_ref[:, pair] = acc[part, :QB_DOM * BT, :]
        dq_ref[:, part * width:(part + 1) * width] = dq[part]
    for i, count in enumerate(plan.shapes):
        for c in range(count):
            if c == 0 or c >= CAP:
                turn = turned(i, c, True)
            for part, pair in enumerate(pairs):
                slot = acc[part, rows_of(plan.starts[i] + c), :].astype(jnp.bfloat16)
                leaving[i][rows_of(c), pair] = dot(turn, slot, (1, 0)).astype(jnp.bfloat16)


def smem_specs(count):
    return [pl.BlockSpec(memory_space=pltpu.SMEM)] * count


def vmem_specs(count):
    return [pl.BlockSpec(memory_space=pltpu.VMEM)] * count


def params(limit):
    return pltpu.CompilerParams(vmem_limit_bytes=limit)


def bf16(*shape):
    return jax.ShapeDtypeStruct(shape, jnp.bfloat16)


def any_specs(count):
    return [pl.BlockSpec(memory_space=pl.ANY)] * count


def busy(microseconds):
    return pl.CostEstimate(flops=int(microseconds * 1.15e9), bytes_accessed=0, transcendentals=0)


def call(kernel, name, scalars, arrays, outs, after=(), in_place=False, out_specs=None, takes=1.0, limit=VMEM_LIMIT, **more):
    after = [x[tuple(slice(0, n) for n in (1,) * (x.ndim - 2) + (16, 128))] for x in after]
    taken = len(scalars) + len(arrays)

    def body(*refs):
        kernel(*refs[:taken], *refs[taken + len(after):])

    return pl.pallas_call(
        body,
        out_shape=outs,
        in_specs=smem_specs(len(scalars)) + (any_specs if in_place else vmem_specs)(len(arrays)) + any_specs(len(after)),
        out_specs=out_specs or vmem_specs(len(outs)),
        compiler_params=params(limit),
        cost_estimate=busy(takes),
        name=name,
        **more,
    )(*scalars, *arrays, *after)


def per_device(plan, queries, keys_in, values_in, grad_out, pos_bias, neighbours, send_block, orient):
    heads = pos_bias.shape[0]
    parts = heads // GROUP_HEADS if heads % GROUP_HEADS == 0 else 1
    width = heads * HD
    part_width = width // parts
    tokens = queries.shape[0]
    holders = lax.axis_size("head")
    tokens_dom = tokens * holders
    sides = plan.sides
    table = jnp.asarray(plan.table)
    near, sends, turns = neighbours.reshape(-1), send_block.reshape(-1), orient.reshape(-1)

    def swap(matrix):
        return lax.all_to_all(matrix, "head", split_axis=0, concat_axis=0, tiled=True)

    def swap_back(matrix):
        return swap(matrix.reshape(holders, tokens, -1))

    def pack(left, right, after):
        more = {}
        if part_width % 128 == 0:
            more = dict(in_place=True, limit=VMEM_MOST, scratch_shapes=[pltpu.SemaphoreType.DMA((2 * holders * parts,))])
        return call(functools.partial(pack_kernel, parts), "pack", [], [left, right],
                    [bf16(holders, tokens, 2 * width)], after, **more)[0]

    def permute(value, pairs):
        return lax.ppermute(value, "dom", pairs)

    def permute_back(value, pairs):
        return lax.ppermute(value, "dom", [(d, p) for p, d in pairs])

    block_shapes = [bf16(count * BT, 2 * width) for count in plan.shapes]
    corner_shapes = [bf16(2 * BT, 2 * width)] * sides

    def in_place(copies, outs):
        return dict(in_place=True, out_specs=any_specs(len(outs)), scratch_shapes=[pltpu.SemaphoreType.DMA((copies,))])

    packed_kv = pack(keys_in, values_in, [])
    kv = swap(packed_kv).reshape(tokens_dom, 2 * width)
    bias = jnp.transpose(pos_bias.reshape(parts, heads // parts, BT, WINK), (0, 3, 1, 2)).reshape(parts, WINK, -1)
    qg = swap(pack(queries, grad_out, [packed_kv, bias])).reshape(tokens_dom, 2 * width)

    corners = call(functools.partial(lend_corners_kernel, plan), "lend_corners", [table, sends], [kv],
                   corner_shapes, **in_place(2 * sides, corner_shapes))
    corners = [permute(x, pairs) for x, pairs in zip(corners, plan.side_pairs)]
    lent = call(functools.partial(lend_edges_kernel, plan), "lend_edges", [table, sends], [kv, *corners], block_shapes,
                **in_place(plan.borrowed, block_shapes))
    arrived = [permute(x, pairs) for x, pairs in zip(lent, plan.side_pairs + plan.rise_pairs)]
    places, turned = call(functools.partial(place_kernel, plan), "place", [table, near, turns], [],
                          [jax.ShapeDtypeStruct((n,), jnp.int32) for n in (QB_DOM * WIN, plan.borrowed)],
                          out_specs=smem_specs(2))

    grad_q, own, *leaving = call(
        functools.partial(attend_kernel, plan, parts), "attend", [places, turned], [qg, kv, bias, *arrived],
        [bf16(tokens_dom, width), jax.ShapeDtypeStruct((tokens_dom, 2 * width), jnp.float32)] + block_shapes,
        takes=15.0,
        scratch_shapes=[
            pltpu.VMEM((parts, plan.slots * BT, 2 * part_width), jnp.bfloat16),
            pltpu.VMEM((parts, plan.slots * BT, 2 * part_width), jnp.float32),
            pltpu.VMEM((parts, tokens_dom, 2 * part_width), jnp.bfloat16),
            pltpu.VMEM((parts, tokens_dom, part_width), jnp.bfloat16),
            pltpu.VMEM((2, WINK, 2 * part_width), jnp.bfloat16),
            pltpu.VMEM((2, 2, WINK, part_width), jnp.float32),
            pltpu.VMEM((2, WINK, part_width), jnp.bfloat16),
            pltpu.VMEM((2, WINK, part_width), jnp.bfloat16),
        ],
    )
    rises = [permute_back(x, pairs) for x, pairs in zip(leaving[sides:], plan.rise_pairs)]
    edges = [permute_back(x, pairs) for x, pairs in zip(leaving[:sides], plan.side_pairs)]
    corners = call(functools.partial(forward_kernel, plan), "forward", [], rises, corner_shapes)
    corners = [permute_back(x, pairs) for x, pairs in zip(corners, plan.side_pairs)]
    settled = call(functools.partial(settle_kernel, plan), "settle", [table, sends], [own, *edges, *rises, *corners],
                   [bf16(tokens_dom, 2 * width)],
                   scratch_shapes=[pltpu.VMEM((tokens_dom, 2 * width), jnp.float32)])[0]
    return call(functools.partial(unpack_kernel, parts), "unpack", [], [swap_back(grad_q), swap_back(settled)],
                [bf16(tokens, holders * width)] * 3)


def solution(mesh):
    plan = Plan(mesh.shape["dom"])
    tokens = P(("dom", "head"), None)
    return jax.shard_map(
        functools.partial(per_device, plan),
        mesh=mesh,
        in_specs=(
            tokens,
            tokens,
            tokens,
            tokens,
            P("head", None, None),
            P("dom", None),
            P("dom", None, None),
            P("dom", None),
        ),
        out_specs=(tokens, tokens, tokens),
        check_vma=False,
    )
```

```python
import functools

import jax
import jax.numpy as jnp
import numpy as np
from jax import lax
from jax.experimental import pallas as pl
from jax.experimental.pallas import tpu as pltpu
from jax.sharding import PartitionSpec as P

HD = 64
PATCH = 8
BT = 64
GRID_ROWS = 4
DIRS = 8
WIN = 9
WINK = 576
QB_DOM = 9
CAP = 3
GROUP_HEADS = 4
SLAB = 32
VMEM_LIMIT = 48 * 1024 * 1024
VMEM_MOST = 60 * 1024 * 1024

OFFSET_LIST = [(-1, -1), (-1, 0), (-1, 1), (0, -1), (0, 1), (1, -1), (1, 0), (1, 1)]


class Plan:
    def __init__(self, domains):
        cols = domains // GRID_ROWS
        cells = [divmod(d, cols) for d in range(domains)]
        steps = [(-1, 1)] if cols == 2 else [(-1,), (1,)] if cols > 2 else []
        self.side_pairs = [[(d + step, d) for step in side for d, (_, col) in enumerate(cells)
                            if 0 <= col + step < cols] for side in steps]
        rows_apart = [[1 if (row + v) % 2 == 0 else -1 for row, _ in cells] for v in range(2)]
        self.rise_pairs = [[(d + apart[d] * cols, d) for d, (row, _) in enumerate(cells)
                            if 0 <= row + apart[d] < GRID_ROWS] for apart in rows_apart]
        sides = len(steps)
        self.sides = sides
        self.rise_blocks = CAP + sides
        self.borrowed = sides * CAP + 2 * self.rise_blocks
        self.slots = QB_DOM + self.borrowed
        self.shapes = [CAP] * sides + [self.rise_blocks] * 2
        self.starts = [QB_DOM + sum(self.shapes[:i]) for i in range(len(self.shapes))]
        slot_total = QB_DOM + DIRS * CAP
        self.dir_at = slot_total
        self.lend_at = slot_total + self.borrowed
        self.rise_at = self.lend_at + 3 * sides
        table = np.zeros((domains, self.rise_at + 2), np.int32)
        for d, (_, col) in enumerate(cells):
            table[d, :QB_DOM] = np.arange(QB_DOM)

            def borrow(k, place, count):
                for c in range(CAP):
                    table[d, QB_DOM + k * CAP + c] = place + c % count
                table[d, self.dir_at + place - QB_DOM:self.dir_at + place - QB_DOM + count] = k

            above = [apart[d] for apart in rows_apart]
            for v, row_step in enumerate(above):
                borrow(OFFSET_LIST.index((row_step, 0)), self.starts[sides + v], CAP)
                table[d, self.rise_at + v] = OFFSET_LIST.index((-row_step, 0))
            for i, side in enumerate(steps):
                for step in side:
                    if 0 <= col + step < cols:
                        borrow(OFFSET_LIST.index((0, step)), self.starts[i], CAP)
                        for v, row_step in enumerate(above):
                            borrow(OFFSET_LIST.index((row_step, step)), self.starts[sides + v] + CAP + i, 1)
                    if 0 <= col - step < cols:
                        for n, row_step in enumerate((0, -above[0], -above[1])):
                            table[d, self.lend_at + 3 * i + n] = OFFSET_LIST.index((row_step, step))
        self.table = table

    def entry(self, table_ref, at):
        return table_ref[lax.axis_index("dom"), at]

    def side_edge(self, i, c, table_ref, send_ref):
        return send_ref[self.entry(table_ref, self.lend_at + 3 * i) * CAP + c]

    def side_corner(self, i, v, table_ref, send_ref):
        k = self.entry(table_ref, self.lend_at + 3 * i + 1 + v)
        found = send_ref[k * CAP]
        for other in range(1, CAP):
            found = jnp.maximum(found, send_ref[k * CAP + other])
        return found

    def rise_edge(self, v, c, table_ref, send_ref):
        return send_ref[self.entry(table_ref, self.rise_at + v) * CAP + c]


def rows_of(c):
    return slice(c * BT, (c + 1) * BT)


def block_rows(index):
    return pl.ds(pl.multiple_of(index * BT, BT), BT)


def turn_matrix(orient, back):
    token = lax.broadcasted_iota(jnp.int32, (BT, BT), 1 if back else 0)
    place = lax.broadcasted_iota(jnp.int32, (BT, BT), 0 if back else 1)
    row, col = token >> 3, token & (PATCH - 1)
    row = jnp.where((orient & 1) == 1, PATCH - 1 - row, row)
    col = jnp.where(((orient >> 1) & 1) == 1, PATCH - 1 - col, col)
    mapped = jnp.where(orient >= 4, PATCH * col + row, PATCH * row + col)
    return (mapped == place).astype(jnp.float32).astype(jnp.bfloat16)


def pack_kernel(parts, left_ref, right_ref, out_ref, *sems):
    holders = out_ref.shape[0]
    width = left_ref.shape[1] // (holders * parts)
    copies = []
    for s in range(holders):
        for part in range(parts):
            at = (s * parts + part) * width
            for ref, to in ((left_ref, 2 * part * width), (right_ref, (2 * part + 1) * width)):
                if sems:
                    copies.append(pltpu.make_async_copy(ref.at[:, at:at + width], out_ref.at[s, :, to:to + width],
                                                        sems[0].at[len(copies)]))
                    copies[-1].start()
                else:
                    out_ref[s, :, to:to + width] = ref[:, at:at + width]
    for copy in copies:
        copy.wait()


def unpack_kernel(parts, halves, grad_ref, *outs):
    holders = grad_ref.shape[0]
    width = grad_ref.shape[2] // (parts * halves)
    for s in range(holders):
        for part in range(parts):
            to = slice((s * parts + part) * width, (s * parts + part + 1) * width)
            for half, out_ref in enumerate(outs):
                at = (halves * part + half) * width
                out_ref[:, to] = grad_ref[s, :, at:at + width]


def copy_all(pairs, sems):
    copies = [pltpu.make_async_copy(source, target, sems.at[n]) for n, (source, target) in enumerate(pairs)]
    for copy in copies:
        copy.start()
    for copy in copies:
        copy.wait()


def lend_corners_kernel(plan, table_ref, send_ref, kv_ref, *refs):
    pairs = []
    for i in range(plan.sides):
        for v in range(2):
            block = plan.side_corner(i, v, table_ref, send_ref)
            pairs.append((kv_ref.at[block_rows(block), :], refs[i].at[rows_of(v), :]))
    copy_all(pairs, refs[-1])


def lend_edges_kernel(plan, table_ref, send_ref, kv_ref, *refs):
    corners, out_refs = refs[:plan.sides], refs[plan.sides:]
    pairs = []
    for v in range(2):
        out_ref = out_refs[plan.sides + v]
        for c in range(CAP):
            pairs.append((kv_ref.at[block_rows(plan.rise_edge(v, c, table_ref, send_ref)), :], out_ref.at[rows_of(c), :]))
        for i in range(plan.sides):
            pairs.append((corners[i].at[rows_of(v), :], out_ref.at[rows_of(CAP + i), :]))
    for i in range(plan.sides):
        for c in range(CAP):
            block = plan.side_edge(i, c, table_ref, send_ref)
            pairs.append((kv_ref.at[block_rows(block), :], out_refs[i].at[rows_of(c), :]))
    copy_all(pairs, refs[-1])


def place_kernel(plan, table_ref, near_ref, orient_ref, places_ref, turns_ref):
    for n in range(QB_DOM * WIN):
        places_ref[n] = plan.entry(table_ref, near_ref[n])
    for n in range(plan.borrowed):
        turns_ref[n] = orient_ref[plan.entry(table_ref, plan.dir_at + n)]


def forward_kernel(plan, *refs):
    for i in range(plan.sides):
        for v in range(2):
            refs[2 + i][rows_of(v), :] = refs[v][rows_of(CAP + i), :]


def settle_kernel(plan, parts, table_ref, send_ref, *refs):
    out_ref, total = refs[-2:]
    sides, rises = refs[parts:parts + plan.sides], refs[parts + plan.sides:parts + plan.sides + 2]
    corners = refs[parts + plan.sides + 2:-2]
    for part in range(parts):
        columns = refs[part].shape[1]
        total[:, part * columns:(part + 1) * columns] = refs[part][...]

    def add(block, ref, c):
        total[block_rows(block), :] += ref[rows_of(c), :].astype(jnp.float32)

    for i in range(plan.sides):
        for c in range(CAP):
            add(plan.side_edge(i, c, table_ref, send_ref), sides[i], c)
        for v in range(2):
            add(plan.side_corner(i, v, table_ref, send_ref), corners[i], v)
    for v in range(2):
        for c in range(CAP):
            add(plan.rise_edge(v, c, table_ref, send_ref), rises[v], c)
    out_ref[...] = total[...].astype(jnp.bfloat16)


def dot(a, b, contract):
    return lax.dot_general(a, b, ((contract[:1], contract[1:]), ((), ())),
                           preferred_element_type=jnp.float32)


def attend_kernel(plan, part, places_ref, turns_ref, qg_ref, kv_ref, bias_ref, *refs):
    groups = len(plan.shapes)
    arrived, refs = refs[:groups], refs[groups:]
    given, refs = (refs[:groups + 1], refs[groups + 1:]) if part > 0 else ([], refs)
    own_ref, dq_ref, *leaving = refs[:groups + 2]
    ext, acc, mask, win, work, probs_ref, dscores_ref = refs[groups + 2:]
    width = probs_ref.shape[2]
    heads = width // HD
    scale = HD ** -0.5
    keys, values = slice(0, width), slice(width, 2 * width)
    mine = slice(2 * part * width, 2 * (part + 1) * width)
    query_lanes = slice(2 * part * width, (2 * part + 1) * width)
    grad_lanes = slice((2 * part + 1) * width, 2 * (part + 1) * width)
    slabs = [slice(at, at + SLAB) for at in range(0, WINK, SLAB)]
    places = [block_rows(places_ref[n]) for n in range(QB_DOM * WIN)]

    def turned(i, c, back):
        return turn_matrix(turns_ref[plan.starts[i] - QB_DOM + c], back)

    for source, target in zip(given, [dq_ref, *leaving]):
        target[:, :source.shape[1]] = source[...]
    ext[:QB_DOM * BT, :] = kv_ref[:, mine]
    for i, count in enumerate(plan.shapes):
        for c in range(count):
            if c == 0 or c >= CAP:
                turn = turned(i, c, False)
            ext[rows_of(plan.starts[i] + c), :] = dot(turn, arrived[i][rows_of(c), mine], (1, 0)).astype(jnp.bfloat16)
    acc[...] = jnp.zeros_like(acc)

    same_head = (lax.broadcasted_iota(jnp.int32, (width, width), 0) // HD
                 == lax.broadcasted_iota(jnp.int32, (width, width), 1) // HD)
    mask[...] = same_head.astype(jnp.float32).astype(jnp.bfloat16)

    def spread(block):
        return jnp.concatenate([block] * heads, axis=0) * mask[...]

    def products(b):
        even = b % 2
        for j in range(WIN):
            win[even, rows_of(j), :] = ext[places[b * WIN + j], :]
        query = spread(qg_ref[rows_of(b), query_lanes] * jnp.bfloat16(scale))
        grad = spread(qg_ref[rows_of(b), grad_lanes])
        work[even, 0] = dot(win[even, :, keys], query, (1, 1)) + bias_ref[part]
        work[even, 1] = dot(win[even, :, values], grad, (1, 1))
        return query, grad

    def softmax(b):
        even = b % 2
        top = work[even, 0, slabs[0], :]
        for slab in slabs[1:]:
            top = jnp.maximum(top, work[even, 0, slab, :])
        top = jnp.max(top, axis=0, keepdims=True)
        total = jnp.zeros((SLAB, width), jnp.float32)
        delta = jnp.zeros((SLAB, width), jnp.float32)
        for slab in slabs:
            weight = jnp.exp(work[even, 0, slab, :] - top)
            work[even, 0, slab, :] = weight
            total = total + weight
            delta = delta + weight * work[even, 1, slab, :]
        inverse = 1.0 / jnp.sum(total, axis=0, keepdims=True)
        delta = jnp.sum(delta, axis=0, keepdims=True) * inverse
        for slab in slabs:
            probs = work[even, 0, slab, :] * inverse
            probs_ref[even, slab, :] = probs.astype(jnp.bfloat16)
            dscores_ref[even, slab, :] = (probs * (work[even, 1, slab, :] - delta)).astype(jnp.bfloat16)

    def gradients(b, query, grad):
        even = b % 2
        dscores = dscores_ref[even]
        grad_q = dot(dscores, win[even, :, keys], (0, 0))
        grad_q = jnp.where(same_head, grad_q, 0.0)
        total_q = grad_q[:BT]
        for h in range(1, heads):
            total_q = total_q + grad_q[rows_of(h)]
        dq_ref[rows_of(b), part * width:(part + 1) * width] = (total_q * scale).astype(jnp.bfloat16)
        grad_k = dot(dscores, query, (1, 0))
        grad_v = dot(probs_ref[even], grad, (1, 0))
        for j in range(WIN):
            acc[places[b * WIN + j], keys] += grad_k[rows_of(j)]
            acc[places[b * WIN + j], values] += grad_v[rows_of(j)]

    here = products(0)
    for b in range(QB_DOM):
        following = products(b + 1) if b + 1 < QB_DOM else None
        softmax(b)
        gradients(b, *here)
        here = following

    own_ref[...] = acc[:QB_DOM * BT, :]
    for i, count in enumerate(plan.shapes):
        for c in range(count):
            if c == 0 or c >= CAP:
                turn = turned(i, c, True)
            slot = acc[rows_of(plan.starts[i] + c), :].astype(jnp.bfloat16)
            leaving[i][rows_of(c), mine] = dot(turn, slot, (1, 0)).astype(jnp.bfloat16)


def smem_specs(count):
    return [pl.BlockSpec(memory_space=pltpu.SMEM)] * count


def vmem_specs(count):
    return [pl.BlockSpec(memory_space=pltpu.VMEM)] * count


def params(limit):
    return pltpu.CompilerParams(vmem_limit_bytes=limit)


def bf16(*shape):
    return jax.ShapeDtypeStruct(shape, jnp.bfloat16)


def any_specs(count):
    return [pl.BlockSpec(memory_space=pl.ANY)] * count


def busy(microseconds):
    return pl.CostEstimate(flops=int(microseconds * 1.15e9), bytes_accessed=0, transcendentals=0)


def call(kernel, name, scalars, arrays, outs, after=(), in_place=False, out_specs=None, takes=1.0, limit=VMEM_LIMIT, **more):
    after = [x[tuple(slice(0, n) for n in (1,) * (x.ndim - 2) + (16, 128))] for x in after]
    taken = len(scalars) + len(arrays)

    def body(*refs):
        kernel(*refs[:taken], *refs[taken + len(after):])

    return pl.pallas_call(
        body,
        out_shape=outs,
        in_specs=smem_specs(len(scalars)) + (any_specs if in_place else vmem_specs)(len(arrays)) + any_specs(len(after)),
        out_specs=out_specs or vmem_specs(len(outs)),
        compiler_params=params(limit),
        cost_estimate=busy(takes),
        name=name,
        **more,
    )(*scalars, *arrays, *after)


def per_device(plan, queries, keys_in, values_in, grad_out, pos_bias, neighbours, send_block, orient):
    heads = pos_bias.shape[0]
    parts = heads // GROUP_HEADS if heads % GROUP_HEADS == 0 else 1
    width = heads * HD
    part_width = width // parts
    tokens = queries.shape[0]
    holders = lax.axis_size("head")
    tokens_dom = tokens * holders
    sides = plan.sides
    table = jnp.asarray(plan.table)
    near, sends, turns = neighbours.reshape(-1), send_block.reshape(-1), orient.reshape(-1)

    def swap(matrix):
        return lax.all_to_all(matrix, "head", split_axis=0, concat_axis=0, tiled=True)

    def swap_back(matrix):
        return swap(matrix.reshape(holders, tokens, -1))

    def pack(left, right, after):
        more = {}
        if part_width % 128 == 0:
            more = dict(in_place=True, limit=VMEM_MOST, scratch_shapes=[pltpu.SemaphoreType.DMA((2 * holders * parts,))])
        return call(functools.partial(pack_kernel, parts), "pack", [], [left, right],
                    [bf16(holders, tokens, 2 * width)], after, **more)[0]

    def permute(value, pairs):
        return lax.ppermute(value, "dom", pairs)

    def permute_back(value, pairs):
        return lax.ppermute(value, "dom", [(d, p) for p, d in pairs])

    block_shapes = [bf16(count * BT, 2 * width) for count in plan.shapes]
    corner_shapes = [bf16(2 * BT, 2 * width)] * sides

    def in_place(copies, outs):
        return dict(in_place=True, out_specs=any_specs(len(outs)), scratch_shapes=[pltpu.SemaphoreType.DMA((copies,))])

    packed_kv = pack(keys_in, values_in, [])
    kv = swap(packed_kv).reshape(tokens_dom, 2 * width)
    bias = jnp.transpose(pos_bias.reshape(parts, heads // parts, BT, WINK), (0, 3, 1, 2)).reshape(parts, WINK, -1)
    qg = swap(pack(queries, grad_out, [packed_kv, bias])).reshape(tokens_dom, 2 * width)

    corners = call(functools.partial(lend_corners_kernel, plan), "lend_corners", [table, sends], [kv],
                   corner_shapes, **in_place(2 * sides, corner_shapes))
    corners = [permute(x, pairs) for x, pairs in zip(corners, plan.side_pairs)]
    lent = call(functools.partial(lend_edges_kernel, plan), "lend_edges", [table, sends], [kv, *corners], block_shapes,
                **in_place(plan.borrowed, block_shapes))
    arrived = [permute(x, pairs) for x, pairs in zip(lent, plan.side_pairs + plan.rise_pairs)]
    places, turned = call(functools.partial(place_kernel, plan), "place", [table, near, turns], [],
                          [jax.ShapeDtypeStruct((n,), jnp.int32) for n in (QB_DOM * WIN, plan.borrowed)],
                          out_specs=smem_specs(2))

    owns, given = [], []
    for part in range(parts):
        done = (part + 1) * part_width
        own, *given = call(
            functools.partial(attend_kernel, plan, part), "attend", [places, turned],
            [qg, kv, bias, *arrived, *given],
            [jax.ShapeDtypeStruct((tokens_dom, 2 * part_width), jnp.float32), bf16(tokens_dom, done)]
            + [bf16(count * BT, 2 * done) for count in plan.shapes],
            takes=8.0,
            scratch_shapes=[
                pltpu.VMEM((plan.slots * BT, 2 * part_width), jnp.bfloat16),
                pltpu.VMEM((plan.slots * BT, 2 * part_width), jnp.float32),
                pltpu.VMEM((part_width, part_width), jnp.bfloat16),
                pltpu.VMEM((2, WINK, 2 * part_width), jnp.bfloat16),
                pltpu.VMEM((2, 2, WINK, part_width), jnp.float32),
                pltpu.VMEM((2, WINK, part_width), jnp.bfloat16),
                pltpu.VMEM((2, WINK, part_width), jnp.bfloat16),
            ],
        )
        owns.append(own)
    grad_q, *leaving = given
    rises = [permute_back(x, pairs) for x, pairs in zip(leaving[sides:], plan.rise_pairs)]
    edges = [permute_back(x, pairs) for x, pairs in zip(leaving[:sides], plan.side_pairs)]
    corners = call(functools.partial(forward_kernel, plan), "forward", [], rises, corner_shapes)
    corners = [permute_back(x, pairs) for x, pairs in zip(corners, plan.side_pairs)]
    settled = call(functools.partial(settle_kernel, plan, parts), "settle", [table, sends], [*owns, *edges, *rises, *corners],
                   [bf16(tokens_dom, 2 * width)],
                   scratch_shapes=[pltpu.VMEM((tokens_dom, 2 * width), jnp.float32)])[0]
    grads = []
    for halves, grad in ((1, grad_q), (2, settled)):
        grads += call(functools.partial(unpack_kernel, parts, halves), "unpack", [], [swap_back(grad)],
                      [bf16(tokens, holders * width)] * halves)
    return tuple(grads)


def solution(mesh):
    plan = Plan(mesh.shape["dom"])
    tokens = P(("dom", "head"), None)
    return jax.shard_map(
        functools.partial(per_device, plan),
        mesh=mesh,
        in_specs=(
            tokens,
            tokens,
            tokens,
            tokens,
            P("head", None, None),
            P("dom", None),
            P("dom", None, None),
            P("dom", None),
        ),
        out_specs=(tokens, tokens, tokens),
        check_vma=False,
    )
```

```python
import functools

import jax
import jax.numpy as jnp
import numpy as np
from jax import lax
from jax.experimental import pallas as pl
from jax.experimental.pallas import tpu as pltpu
from jax.sharding import PartitionSpec as P

HD = 64
PATCH = 8
BT = 64
GRID_ROWS = 4
DIRS = 8
WIN = 9
WINK = 576
QB_DOM = 9
CAP = 3
GROUP_HEADS = 4
SLAB = 32
VMEM_LIMIT = 48 * 1024 * 1024
VMEM_MOST = 60 * 1024 * 1024

OFFSET_LIST = [(-1, -1), (-1, 0), (-1, 1), (0, -1), (0, 1), (1, -1), (1, 0), (1, 1)]


class Plan:
    def __init__(self, domains):
        cols = domains // GRID_ROWS
        cells = [divmod(d, cols) for d in range(domains)]
        steps = [(-1, 1)] if cols == 2 else [(-1,), (1,)] if cols > 2 else []
        self.side_pairs = [[(d + step, d) for step in side for d, (_, col) in enumerate(cells)
                            if 0 <= col + step < cols] for side in steps]
        rows_apart = [[1 if (row + v) % 2 == 0 else -1 for row, _ in cells] for v in range(2)]
        self.rise_pairs = [[(d + apart[d] * cols, d) for d, (row, _) in enumerate(cells)
                            if 0 <= row + apart[d] < GRID_ROWS] for apart in rows_apart]
        sides = len(steps)
        self.sides = sides
        self.rise_blocks = CAP + sides
        self.borrowed = sides * CAP + 2 * self.rise_blocks
        self.slots = QB_DOM + self.borrowed
        self.shapes = [CAP] * sides + [self.rise_blocks] * 2
        self.starts = [QB_DOM + sum(self.shapes[:i]) for i in range(len(self.shapes))]
        slot_total = QB_DOM + DIRS * CAP
        self.dir_at = slot_total
        self.lend_at = slot_total + self.borrowed
        self.rise_at = self.lend_at + 3 * sides
        table = np.zeros((domains, self.rise_at + 2), np.int32)
        for d, (_, col) in enumerate(cells):
            table[d, :QB_DOM] = np.arange(QB_DOM)

            def borrow(k, place, count):
                for c in range(CAP):
                    table[d, QB_DOM + k * CAP + c] = place + c % count
                table[d, self.dir_at + place - QB_DOM:self.dir_at + place - QB_DOM + count] = k

            above = [apart[d] for apart in rows_apart]
            for v, row_step in enumerate(above):
                borrow(OFFSET_LIST.index((row_step, 0)), self.starts[sides + v], CAP)
                table[d, self.rise_at + v] = OFFSET_LIST.index((-row_step, 0))
            for i, side in enumerate(steps):
                for step in side:
                    if 0 <= col + step < cols:
                        borrow(OFFSET_LIST.index((0, step)), self.starts[i], CAP)
                        for v, row_step in enumerate(above):
                            borrow(OFFSET_LIST.index((row_step, step)), self.starts[sides + v] + CAP + i, 1)
                    if 0 <= col - step < cols:
                        for n, row_step in enumerate((0, -above[0], -above[1])):
                            table[d, self.lend_at + 3 * i + n] = OFFSET_LIST.index((row_step, step))
        self.table = table

    def entry(self, table_ref, at):
        return table_ref[lax.axis_index("dom"), at]

    def side_edge(self, i, c, table_ref, send_ref):
        return send_ref[self.entry(table_ref, self.lend_at + 3 * i) * CAP + c]

    def side_corner(self, i, v, table_ref, send_ref):
        k = self.entry(table_ref, self.lend_at + 3 * i + 1 + v)
        found = send_ref[k * CAP]
        for other in range(1, CAP):
            found = jnp.maximum(found, send_ref[k * CAP + other])
        return found

    def rise_edge(self, v, c, table_ref, send_ref):
        return send_ref[self.entry(table_ref, self.rise_at + v) * CAP + c]


def rows_of(c):
    return slice(c * BT, (c + 1) * BT)


def block_rows(index):
    return pl.ds(pl.multiple_of(index * BT, BT), BT)


def turn_matrix(orient, back):
    token = lax.broadcasted_iota(jnp.int32, (BT, BT), 1 if back else 0)
    place = lax.broadcasted_iota(jnp.int32, (BT, BT), 0 if back else 1)
    row, col = token >> 3, token & (PATCH - 1)
    row = jnp.where((orient & 1) == 1, PATCH - 1 - row, row)
    col = jnp.where(((orient >> 1) & 1) == 1, PATCH - 1 - col, col)
    mapped = jnp.where(orient >= 4, PATCH * col + row, PATCH * row + col)
    return (mapped == place).astype(jnp.float32).astype(jnp.bfloat16)


def pack_kernel(parts, left_ref, right_ref, out_ref, *sems):
    holders = out_ref.shape[0]
    width = left_ref.shape[1] // (holders * parts)
    copies = []
    for s in range(holders):
        for part in range(parts):
            at = (s * parts + part) * width
            for ref, to in ((left_ref, 2 * part * width), (right_ref, (2 * part + 1) * width)):
                if sems:
                    copies.append(pltpu.make_async_copy(ref.at[:, at:at + width], out_ref.at[s, :, to:to + width],
                                                        sems[0].at[len(copies)]))
                    copies[-1].start()
                else:
                    out_ref[s, :, to:to + width] = ref[:, at:at + width]
    for copy in copies:
        copy.wait()


def unpack_kernel(parts, dq_ref, dkv_ref, *outs):
    holders = dq_ref.shape[0]
    width = dq_ref.shape[2] // parts
    for s in range(holders):
        for part in range(parts):
            to = slice((s * parts + part) * width, (s * parts + part + 1) * width)
            outs[0][:, to] = dq_ref[s, :, part * width:(part + 1) * width]
            for half in range(2):
                at = (2 * part + half) * width
                outs[1 + half][:, to] = dkv_ref[s, :, at:at + width]


def copy_all(pairs, sems):
    copies = [pltpu.make_async_copy(source, target, sems.at[n]) for n, (source, target) in enumerate(pairs)]
    for copy in copies:
        copy.start()
    for copy in copies:
        copy.wait()


def lend_corners_kernel(plan, table_ref, send_ref, kv_ref, *refs):
    pairs = []
    for i in range(plan.sides):
        for v in range(2):
            block = plan.side_corner(i, v, table_ref, send_ref)
            pairs.append((kv_ref.at[block_rows(block), :], refs[i].at[rows_of(v), :]))
    copy_all(pairs, refs[-1])


def lend_edges_kernel(plan, table_ref, send_ref, kv_ref, *refs):
    corners, out_refs = refs[:plan.sides], refs[plan.sides:]
    pairs = []
    for v in range(2):
        out_ref = out_refs[plan.sides + v]
        for c in range(CAP):
            pairs.append((kv_ref.at[block_rows(plan.rise_edge(v, c, table_ref, send_ref)), :], out_ref.at[rows_of(c), :]))
        for i in range(plan.sides):
            pairs.append((corners[i].at[rows_of(v), :], out_ref.at[rows_of(CAP + i), :]))
    for i in range(plan.sides):
        for c in range(CAP):
            block = plan.side_edge(i, c, table_ref, send_ref)
            pairs.append((kv_ref.at[block_rows(block), :], out_refs[i].at[rows_of(c), :]))
    copy_all(pairs, refs[-1])


def place_kernel(plan, table_ref, near_ref, orient_ref, places_ref, turns_ref):
    for n in range(QB_DOM * WIN):
        places_ref[n] = plan.entry(table_ref, near_ref[n])
    for n in range(plan.borrowed):
        turns_ref[n] = orient_ref[plan.entry(table_ref, plan.dir_at + n)]


def forward_kernel(plan, *refs):
    for i in range(plan.sides):
        for v in range(2):
            refs[2 + i][rows_of(v), :] = refs[v][rows_of(CAP + i), :]


def settle_kernel(plan, table_ref, send_ref, own_ref, *refs):
    out_ref, total = refs[-2:]
    sides, rises = refs[:plan.sides], refs[plan.sides:plan.sides + 2]
    corners = refs[plan.sides + 2:-2]
    columns = own_ref.shape[2]
    for part in range(own_ref.shape[0]):
        total[:, part * columns:(part + 1) * columns] = own_ref[part]

    def add(block, ref, c):
        total[block_rows(block), :] += ref[rows_of(c), :].astype(jnp.float32)

    for i in range(plan.sides):
        for c in range(CAP):
            add(plan.side_edge(i, c, table_ref, send_ref), sides[i], c)
        for v in range(2):
            add(plan.side_corner(i, v, table_ref, send_ref), corners[i], v)
    for v in range(2):
        for c in range(CAP):
            add(plan.rise_edge(v, c, table_ref, send_ref), rises[v], c)
    out_ref[...] = total[...].astype(jnp.bfloat16)


def dot(a, b, contract):
    return lax.dot_general(a, b, ((contract[:1], contract[1:]), ((), ())),
                           preferred_element_type=jnp.float32)


def attend_kernel(plan, parts, places_ref, turns_ref, qg_ref, kv_ref, bias_ref, *refs):
    groups = len(plan.shapes)
    arrived = refs[:groups]
    dq_ref, own_ref, *leaving = refs[groups:2 * groups + 2]
    ext, acc, qg, dq, bias, win, work, probs_ref, dscores_ref = refs[2 * groups + 2:2 * groups + 11]
    turned_back, (in_sems, out_sems, leave_sems) = refs[2 * groups + 11:-3], refs[-3:]
    width = dq.shape[2]
    heads = width // HD
    scale = HD ** -0.5
    keys, values = slice(0, width), slice(width, 2 * width)
    pairs = [slice(2 * part * width, 2 * (part + 1) * width) for part in range(parts)]
    slabs = [slice(at, at + SLAB) for at in range(0, WINK, SLAB)]
    places = [block_rows(places_ref[n]) for n in range(QB_DOM * WIN)]

    def turned(i, c, back):
        return turn_matrix(turns_ref[plan.starts[i] - QB_DOM + c], back)

    def copies(part, moves, sems):
        return [pltpu.make_async_copy(source, target, sems.at[part, n]) for n, (source, target) in enumerate(moves)]

    loads = [copies(part, [(kv_ref.at[:, pair], ext.at[part, :QB_DOM * BT, :]), (qg_ref.at[:, pair], qg.at[part]),
                           (bias_ref.at[part], bias.at[part])], in_sems) for part, pair in enumerate(pairs)]
    stores = [copies(part, [(acc.at[part, :QB_DOM * BT, :], own_ref.at[part]),
                            (dq.at[part], dq_ref.at[:, part * width:(part + 1) * width])], out_sems)
              for part in range(parts)]
    for copy in sum(loads, []):
        copy.start()
    for i, count in enumerate(plan.shapes):
        for c in range(count):
            if c == 0 or c >= CAP:
                turn = turned(i, c, False)
            block = dot(turn, arrived[i][rows_of(c), :], (1, 0)).astype(jnp.bfloat16)
            for part, pair in enumerate(pairs):
                ext[part, rows_of(plan.starts[i] + c), :] = block[:, pair]
    acc[...] = jnp.zeros_like(acc)

    same_head = (lax.broadcasted_iota(jnp.int32, (width, width), 0) // HD
                 == lax.broadcasted_iota(jnp.int32, (width, width), 1) // HD)

    def spread(block):
        copies = jnp.concatenate([block] * heads, axis=0)
        return jnp.where(same_head, copies, jnp.zeros_like(copies))

    def products(part, b):
        even = b % 2
        for j in range(WIN):
            win[even, rows_of(j), :] = ext[part, places[b * WIN + j], :]
        query = spread(qg[part, rows_of(b), keys] * jnp.bfloat16(scale))
        grad = spread(qg[part, rows_of(b), values])
        work[even, 0] = dot(win[even, :, keys], query, (1, 1)) + bias[part]
        work[even, 1] = dot(win[even, :, values], grad, (1, 1))
        return query, grad

    def softmax(b):
        even = b % 2
        top = work[even, 0, slabs[0], :]
        for slab in slabs[1:]:
            top = jnp.maximum(top, work[even, 0, slab, :])
        top = jnp.max(top, axis=0, keepdims=True)
        total = jnp.zeros((SLAB, width), jnp.float32)
        delta = jnp.zeros((SLAB, width), jnp.float32)
        for slab in slabs:
            weight = jnp.exp(work[even, 0, slab, :] - top)
            work[even, 0, slab, :] = weight
            total = total + weight
            delta = delta + weight * work[even, 1, slab, :]
        inverse = 1.0 / jnp.sum(total, axis=0, keepdims=True)
        delta = jnp.sum(delta, axis=0, keepdims=True) * inverse
        for slab in slabs:
            probs = work[even, 0, slab, :] * inverse
            probs_ref[even, slab, :] = probs.astype(jnp.bfloat16)
            dscores_ref[even, slab, :] = (probs * (work[even, 1, slab, :] - delta)).astype(jnp.bfloat16)

    def gradients(part, b, query, grad):
        even = b % 2
        dscores = dscores_ref[even]
        grad_q = dot(dscores, win[even, :, keys], (0, 0))
        grad_q = jnp.where(same_head, grad_q, 0.0)
        total_q = grad_q[:BT]
        for h in range(1, heads):
            total_q = total_q + grad_q[rows_of(h)]
        dq[part, rows_of(b), :] = (total_q * scale).astype(jnp.bfloat16)
        grad_k = dot(dscores, query, (1, 0))
        grad_v = dot(probs_ref[even], grad, (1, 0))
        for j in range(WIN):
            acc[part, places[b * WIN + j], keys] += grad_k[rows_of(j)]
            acc[part, places[b * WIN + j], values] += grad_v[rows_of(j)]

    def only(part, these, act):
        for n in range(parts):
            @pl.when(part == n)
            def _():
                for copy in these[n]:
                    act(copy)

    def one_part(part, carry):
        only(part, loads, lambda copy: copy.wait())
        here = products(part, 0)
        for b in range(QB_DOM):
            following = products(part, b + 1) if b + 1 < QB_DOM else None
            softmax(b)
            gradients(part, b, *here)
            here = following
        only(part, stores, lambda copy: copy.start())
        return carry

    lax.fori_loop(0, parts, one_part, 0)
    leaves = []
    for i, count in enumerate(plan.shapes):
        for c in range(count):
            if c == 0 or c >= CAP:
                turn = turned(i, c, True)
            for part, pair in enumerate(pairs):
                slot = acc[part, rows_of(plan.starts[i] + c), :].astype(jnp.bfloat16)
                turned_back[i][rows_of(c), pair] = dot(turn, slot, (1, 0)).astype(jnp.bfloat16)
        leaves.append(pltpu.make_async_copy(turned_back[i], leaving[i], leave_sems.at[i]))
        leaves[-1].start()
    for copy in sum(stores, []) + leaves:
        copy.wait()


def smem_specs(count):
    return [pl.BlockSpec(memory_space=pltpu.SMEM)] * count


def vmem_specs(count):
    return [pl.BlockSpec(memory_space=pltpu.VMEM)] * count


def params(limit):
    return pltpu.CompilerParams(vmem_limit_bytes=limit)


def bf16(*shape):
    return jax.ShapeDtypeStruct(shape, jnp.bfloat16)


def any_specs(count):
    return [pl.BlockSpec(memory_space=pl.ANY)] * count


def busy(microseconds):
    return pl.CostEstimate(flops=int(microseconds * 1.15e9), bytes_accessed=0, transcendentals=0)


def call(kernel, name, scalars, arrays, outs, after=(), in_place=False, in_specs=None, out_specs=None, takes=1.0, limit=VMEM_LIMIT, **more):
    after = [x[tuple(slice(0, n) for n in (1,) * (x.ndim - 2) + (16, 128))] for x in after]
    taken = len(scalars) + len(arrays)

    def body(*refs):
        kernel(*refs[:taken], *refs[taken + len(after):])

    return pl.pallas_call(
        body,
        out_shape=outs,
        in_specs=smem_specs(len(scalars)) + (in_specs or (any_specs if in_place else vmem_specs)(len(arrays)))
        + any_specs(len(after)),
        out_specs=out_specs or vmem_specs(len(outs)),
        compiler_params=params(limit),
        cost_estimate=busy(takes),
        name=name,
        **more,
    )(*scalars, *arrays, *after)


def per_device(plan, queries, keys_in, values_in, grad_out, pos_bias, neighbours, send_block, orient):
    heads = pos_bias.shape[0]
    parts = heads // GROUP_HEADS if heads % GROUP_HEADS == 0 else 1
    width = heads * HD
    part_width = width // parts
    tokens = queries.shape[0]
    holders = lax.axis_size("head")
    tokens_dom = tokens * holders
    sides = plan.sides
    table = jnp.asarray(plan.table)
    near, sends, turns = neighbours.reshape(-1), send_block.reshape(-1), orient.reshape(-1)

    def swap(matrix):
        return lax.all_to_all(matrix, "head", split_axis=0, concat_axis=0, tiled=True)

    def swap_back(matrix):
        return swap(matrix.reshape(holders, tokens, -1))

    def pack(left, right, after):
        more = {}
        if part_width % 128 == 0:
            more = dict(in_place=True, limit=VMEM_MOST, scratch_shapes=[pltpu.SemaphoreType.DMA((2 * holders * parts,))])
        return call(functools.partial(pack_kernel, parts), "pack", [], [left, right],
                    [bf16(holders, tokens, 2 * width)], after, **more)[0]

    def permute(value, pairs):
        return lax.ppermute(value, "dom", pairs)

    def permute_back(value, pairs):
        return lax.ppermute(value, "dom", [(d, p) for p, d in pairs])

    block_shapes = [bf16(count * BT, 2 * width) for count in plan.shapes]
    corner_shapes = [bf16(2 * BT, 2 * width)] * sides

    def in_place(copies, outs):
        return dict(in_place=True, out_specs=any_specs(len(outs)), scratch_shapes=[pltpu.SemaphoreType.DMA((copies,))])

    packed_kv = pack(keys_in, values_in, [])
    kv = swap(packed_kv).reshape(tokens_dom, 2 * width)
    bias = jnp.transpose(pos_bias.reshape(parts, heads // parts, BT, WINK), (0, 3, 1, 2)).reshape(parts, WINK, -1)
    qg = swap(pack(queries, grad_out, [packed_kv, bias])).reshape(tokens_dom, 2 * width)

    corners = call(functools.partial(lend_corners_kernel, plan), "lend_corners", [table, sends], [kv],
                   corner_shapes, **in_place(2 * sides, corner_shapes))
    corners = [permute(x, pairs) for x, pairs in zip(corners, plan.side_pairs)]
    lent = call(functools.partial(lend_edges_kernel, plan), "lend_edges", [table, sends], [kv, *corners], block_shapes,
                **in_place(plan.borrowed, block_shapes))
    arrived = [permute(x, pairs) for x, pairs in zip(lent, plan.side_pairs + plan.rise_pairs)]
    places, turned = call(functools.partial(place_kernel, plan), "place", [table, near, turns], [],
                          [jax.ShapeDtypeStruct((n,), jnp.int32) for n in (QB_DOM * WIN, plan.borrowed)],
                          out_specs=smem_specs(2))

    grad_q, own, *leaving = call(
        functools.partial(attend_kernel, plan, parts), "attend", [places, turned], [qg, kv, bias, *arrived],
        [bf16(tokens_dom, width), jax.ShapeDtypeStruct((parts, tokens_dom, 2 * part_width), jnp.float32)] + block_shapes,
        in_specs=any_specs(3) + vmem_specs(len(arrived)), out_specs=any_specs(2 + len(block_shapes)),
        takes=15.0,
        scratch_shapes=[
            pltpu.VMEM((parts, plan.slots * BT, 2 * part_width), jnp.bfloat16),
            pltpu.VMEM((parts, plan.slots * BT, 2 * part_width), jnp.float32),
            pltpu.VMEM((parts, tokens_dom, 2 * part_width), jnp.bfloat16),
            pltpu.VMEM((parts, tokens_dom, part_width), jnp.bfloat16),
            pltpu.VMEM((parts, WINK, part_width), jnp.float32),
            pltpu.VMEM((2, WINK, 2 * part_width), jnp.bfloat16),
            pltpu.VMEM((2, 2, WINK, part_width), jnp.float32),
            pltpu.VMEM((2, WINK, part_width), jnp.bfloat16),
            pltpu.VMEM((2, WINK, part_width), jnp.bfloat16),
            *[pltpu.VMEM(shape.shape, jnp.bfloat16) for shape in block_shapes],
            pltpu.SemaphoreType.DMA((parts, 3)),
            pltpu.SemaphoreType.DMA((parts, 2)),
            pltpu.SemaphoreType.DMA((len(block_shapes),)),
        ],
    )
    rises = [permute_back(x, pairs) for x, pairs in zip(leaving[sides:], plan.rise_pairs)]
    edges = [permute_back(x, pairs) for x, pairs in zip(leaving[:sides], plan.side_pairs)]
    corners = call(functools.partial(forward_kernel, plan), "forward", [], rises, corner_shapes)
    corners = [permute_back(x, pairs) for x, pairs in zip(corners, plan.side_pairs)]
    settled = call(functools.partial(settle_kernel, plan), "settle", [table, sends], [own, *edges, *rises, *corners],
                   [bf16(tokens_dom, 2 * width)],
                   scratch_shapes=[pltpu.VMEM((tokens_dom, 2 * width), jnp.float32)])[0]
    return call(functools.partial(unpack_kernel, parts), "unpack", [], [swap_back(grad_q), swap_back(settled)],
                [bf16(tokens, holders * width)] * 3)


def solution(mesh):
    plan = Plan(mesh.shape["dom"])
    tokens = P(("dom", "head"), None)
    return jax.shard_map(
        functools.partial(per_device, plan),
        mesh=mesh,
        in_specs=(
            tokens,
            tokens,
            tokens,
            tokens,
            P("head", None, None),
            P("dom", None),
            P("dom", None, None),
            P("dom", None),
        ),
        out_specs=(tokens, tokens, tokens),
        check_vma=False,
    )
```
